32 devices in a mesh: gx: 8 (over z, x), gy: 4 (over y, core).
Axes of the slice: x: 2, y: 2, z: 4, core: 2. Of those that a mesh axis runs over, the one named last changes fastest.
Arguments:
- vel0: bfloat16 [2, 2048, 1024], P(None, 'gx', 'gy'), may hold values from -6 to 6
- visc: float32 [2048, 1024], P('gx', 'gy'), may hold values from 0.1 to 1
- fric: float32 [2048, 1024], P('gx', 'gy'), may hold values from 0.5 to 5
- drive: bfloat16 [2, 2048, 1024], P(None, 'gx', 'gy'), may hold values from -6 to 6
- scene_obs: bfloat16 [4, 128, 2, 128, 128], P('gy', 'gx'), may hold values from -6 to 6
- scene_weight: bfloat16 [4, 128], P('gy', 'gx'), may hold values from 0.5 to 4
- scene_owner: int32 [4, 128, 1], P('gy', 'gx'), may hold values from 0 to 7; in each aligned block of 16 rows (0 to 15, 16 to 31, ..., all dimensions but the last counted through in order) at most 2 rows name the same one
- scene_slot: int32 [4, 128], P('gy', 'gx'), may hold values from 0 to 3
- ice_mask: int32 [16, 8], P('gx', 'gy'), may hold values 0 or 1
Outputs:
- grad_fric: float32 [2048, 1024], P('gx', 'gy')
The draws below stay inside these ranges and needn't reach their ends.
Inputs may be any that keep to these rules, and one draw needn't show every extreme that they name: `scene_owner`: among one device's 16 scenes at most 2 name the same owner, and in some device one owner is named exactly 2 times.
All inputs are finite; a program needn't handle non-finite values. No bound on the sum of `ice_mask` on one device may be relied on, other than what follows from the above.
Results may differ from the reference program's by a relative error of at most 0.0003.
Values may be sent and summed in bfloat16 or wider, within the bound.
No kernel may reach another device: no remote copies, remote signals or barrier semaphores. Data moves between devices by JAX's collectives and lax.ppermute only.
A program may use at most 64 MiB of HBM per device.

```python
import math
import jax
import jax.numpy as jnp
import numpy as np
from jax import lax

TILE = 128
NS = 16
CAP = 2
SX = 2
SY = 2
SLOTS = 4
NX = 2048
NY = 1024
SCENES_X = 128
N_GX = 8
N_GY = 4


def plant(array, own_key, low, top_value):
    longest = array.shape.index(max(array.shape))
    spots = []
    for shift in (0, 1):
        where = [jax.random.randint(jax.random.fold_in(own_key, axis), (), 0, length) for axis, length in enumerate(array.shape)]
        where[longest] = (where[longest] + shift) % array.shape[longest]
        spots.append(tuple(where))
    return array.at[spots[0]].set(low).at[spots[1]].set(top_value)


def steps_of(key, shape, split, least, high):
    factor_of, own = 1.0, jax.random.fold_in(key, 6)
    for dim, parts in split:
        draws = jnp.exp(jax.random.uniform(jax.random.fold_in(own, dim), (parts,), jnp.float32, least / len(split), high / len(split)))
        factor_of = factor_of * jnp.repeat(draws, shape[dim] // parts).reshape([-1 if axis == dim else 1 for axis in range(len(shape))])
    return factor_of


def assign_block(stream_key, own, number, rows, amount, top, reach, lean):
    ranking = jax.random.permutation(stream_key, amount)
    crowded, common = load_shares(amount, rows * top, reach, lean, True), load_shares(amount, rows * top, reach, lean, False)
    places = jnp.arange(amount)

    def named(sizes, turn):
        used = int((sizes > 0).sum())
        fixed = max(1, used // 4)
        moved = fixed + (places - fixed + turn * (used - fixed)) % max(1, amount - fixed)
        return jnp.zeros((amount,), jnp.int32).at[ranking[jnp.where(places < fixed, places, moved)]].set(jnp.asarray(sizes, jnp.int32))

    sizes = jnp.where(number % 4 == 0, named(crowded, number // 4), named(common, number - number // 4 - 1))
    mixed = jax.random.permutation(jax.random.fold_in(own, 3), amount)
    giver, sink = mixed[0:amount // 2 * 2:2], mixed[1:amount // 2 * 2:2]
    room = jnp.minimum(sizes[giver] - 1, reach - sizes[sink]) // 2
    room = jnp.where((giver == ranking[0]) | (sink == ranking[0]) | (sizes[sink] == 0), 0, jnp.maximum(room, 0))
    moved = jax.random.randint(jax.random.fold_in(own, 4), (amount // 2,), 0, 1 << 20) % (room + 1)
    sizes = sizes.at[giver].add(-moved).at[sink].add(moved)
    members = jnp.searchsorted(jnp.cumsum(sizes), jnp.arange(rows * top), side="right").astype(jnp.int32)
    listing = members.reshape(top, rows).T
    listing = listing[jax.random.permutation(jax.random.fold_in(own, 1), rows)]
    turn = jax.random.randint(jax.random.fold_in(own, 2), (rows, 1), 0, top)
    return jnp.take_along_axis(listing, (jnp.arange(top)[None, :] + turn) % top, axis=1)


def load_shares(count, total, bound, lean, full):
    loads = [(1 << 20) // math.isqrt(rank ** lean) + 1 for rank in range(1, count + 1)]
    largest = bound if full else min(bound, max(-(-total // count), total * loads[0] // sum(loads)))
    least = 1 if total - largest >= count - 1 else 0
    given, spare = [largest] + [least] * (count - 1), total - largest - least * (count - 1)
    while spare > 0:
        candidates = [i for i in range(1, count) if given[i] < largest] or [i for i in range(1, count) if given[i] < bound]
        whole, budget = sum([loads[i] for i in candidates]), spare
        for i in candidates:
            extra = min(bound - given[i], max(1, budget * loads[i] // whole), spare)
            given[i] = given[i] + extra
            spare = spare - extra
    return np.array(given)


def scatter_about(stream_key, extent, width, most, pieces=(), kind=jnp.bfloat16):
    values = jax.random.normal(stream_key, extent, jnp.float32) * width
    if len(pieces) > 0:
        values = steps_of(stream_key, extent, pieces, -0.22, 0.18) * values
    return jnp.clip(values, min=-most, max=most).astype(kind)


def setup_inputs(seed: int = 0) -> dict:
    seeds = jax.random.split(jax.random.key(seed), 10)
    vel0 = scatter_about(seeds[0], (2, NX, NY), 1.0, 6.0, ((1, 8), (2, 4)))
    visc = jnp.clip(jnp.exp(math.log(1.0) - 2.3025851 * jax.random.uniform(seeds[1], (NX, NY), jnp.float32) ** steps_of(seeds[1], (NX, NY), ((0, 8), (1, 4)), -0.2, 0.2)), 0.1, 1.0)
    fric = jnp.clip(jnp.exp(math.log(5.0) - 2.3025851 * jax.random.uniform(seeds[2], (NX, NY), jnp.float32) ** steps_of(seeds[2], (NX, NY), ((0, 8), (1, 4)), -0.2, 0.2)), 0.5, 5.0)
    drive = scatter_about(seeds[3], (2, NX, NY), 1.0, 6.0, ((1, 8), (2, 4)))
    scene_obs = scatter_about(seeds[4], (N_GY, SCENES_X, 2, TILE, TILE), 1.0, 6.0, ((0, 4), (1, 8)))
    scene_weight = jnp.clip(jnp.exp(math.log(4.0) - 2.0794415 * jax.random.uniform(seeds[5], (N_GY, SCENES_X), jnp.float32) ** steps_of(seeds[5], (N_GY, SCENES_X), ((0, 4), (1, 8)), -0.2, 0.2)), 0.5, 4.0).astype(jnp.bfloat16)
    scene_owner_keys = jax.random.split(jax.random.fold_in(seeds[6], 1), N_GY * SCENES_X // NS)
    scene_owner_turns = jax.random.permutation(jax.random.fold_in(seeds[6], 3), N_GY * SCENES_X // NS)
    scene_owner = jax.vmap(lambda own, number: assign_block(jax.random.fold_in(seeds[6], 2), own, number, NS, N_GX, 1, CAP, 2))(scene_owner_keys, scene_owner_turns).reshape((N_GY, SCENES_X, 1))
    scene_slot = plant(jax.random.randint(seeds[7], (N_GY, SCENES_X), 0, SLOTS), jax.random.fold_in(seeds[7], 1), 0, SLOTS - 1).astype(jnp.int32)
    ice_mask = plant((jax.random.randint(seeds[8], (NX // TILE, NY // TILE), 0, 4) < 3).astype(jnp.int32), jax.random.fold_in(seeds[8], 1), 0, 1)
    return {"vel0": vel0, "visc": visc, "fric": fric, "drive": drive, "scene_obs": scene_obs, "scene_weight": scene_weight, "scene_owner": scene_owner, "scene_slot": scene_slot, "ice_mask": ice_mask}


def upper(a, axis):
    if axis == 0:
        return jnp.concatenate([a[1:], jnp.zeros_like(a[:1])], axis=0)
    return jnp.concatenate([a[:, 1:], jnp.zeros_like(a[:, :1])], axis=1)


def lower(a, axis):
    if axis == 0:
        return jnp.concatenate([jnp.zeros_like(a[:1]), a[:-1]], axis=0)
    return jnp.concatenate([jnp.zeros_like(a[:, :1]), a[:, :-1]], axis=1)


def stress_image(field, visc):
    vel_u = field[0]
    vel_v = field[1]
    a_x = upper(vel_u, 0) - vel_u
    a_y = upper(vel_u, 1) - vel_u
    b_x = upper(vel_v, 0) - vel_v
    b_y = upper(vel_v, 1) - vel_v
    sxx = visc * (4.0 * a_x + 2.0 * b_y)
    syy = visc * (4.0 * b_y + 2.0 * a_x)
    sxy = visc * (a_y + b_x)
    push_u = lower(sxx, 0) - sxx + lower(sxy, 1) - sxy
    push_v = lower(sxy, 0) - sxy + lower(syy, 1) - syy
    return jnp.stack([push_u, push_v])


def reference(vel0, visc, fric, drive, scene_obs, scene_weight, scene_owner, scene_slot, ice_mask):
    visc_x = lower(visc, 0)
    visc_y = lower(visc, 1)
    diag = jnp.stack([5.0 * visc + 4.0 * visc_x + visc_y, 5.0 * visc + visc_x + 4.0 * visc_y])
    relax = 1.0 / (diag + fric)
    start = vel0.astype(jnp.float32)
    force = drive.astype(jnp.float32)
    first_res = force - stress_image(start, visc) - fric * start
    first = start + 0.6 * relax * first_res
    second_res = force - stress_image(first, visc) - fric * first
    second = first + 0.6 * relax * second_res

    owner = scene_owner[:, :, 0].astype(jnp.int32)
    slot = scene_slot.astype(jnp.int32)
    rows = jnp.arange(N_GY, dtype=jnp.int32)[:, None]
    tile_row = (owner * SX + slot // SY).astype(jnp.int32)
    tile_col = (rows * SY + slot % SY).astype(jnp.int32)
    weight = scene_weight.astype(jnp.float32)
    tile_weight = jnp.zeros((NX // TILE, NY // TILE), jnp.float32).at[tile_row, tile_col].add(weight)

    def add_row(index, total):
        index = jnp.asarray(index).astype(jnp.int32)
        obs_row = lax.dynamic_index_in_dim(scene_obs, index, 0, keepdims=False).astype(jnp.float32)
        row_t = lax.dynamic_index_in_dim(tile_row, index, 0, keepdims=False)
        col_t = lax.dynamic_index_in_dim(tile_col, index, 0, keepdims=False)
        weight_row = lax.dynamic_index_in_dim(weight, index, 0, keepdims=False)
        return total.at[row_t, col_t].add(weight_row[:, None, None, None] * obs_row)

    obs_tiles = lax.fori_loop(0, N_GY, add_row, jnp.zeros((NX // TILE, NY // TILE, 2, TILE, TILE), jnp.float32))
    obs_sum = obs_tiles.transpose(2, 0, 3, 1, 4).reshape(2, NX, NY)
    weight_cell = jnp.repeat(jnp.repeat(tile_weight, TILE, axis=0), TILE, axis=1)
    ice = jnp.repeat(jnp.repeat(ice_mask.astype(jnp.float32), TILE, axis=0), TILE, axis=1)

    misfit_grad = ice * (weight_cell * second - obs_sum)
    lift_two = 0.6 * relax * misfit_grad
    back = misfit_grad - stress_image(lift_two, visc) - fric * lift_two
    lift_one = 0.6 * relax * back
    part_one = jnp.sum(lift_one * (relax * first_res + start), axis=0)
    part_two = jnp.sum(lift_two * (relax * second_res + first), axis=0)
    return -ice * (part_one + part_two)
```

```python
import functools

import jax
import jax.numpy as jnp
from jax import lax
from jax.experimental import pallas as pl
from jax.experimental.pallas import tpu as pltpu
from jax.sharding import PartitionSpec as P

CAP = 2
OMEGA = 0.6
LANE = 128
PAD = 16
PACK = 16
FIELDS = ((0, 3), (3, 3), (6, 3), (9, 2), (11, 2), (13, 2), (15, 1))
U, V, VISC, FRIC, DRIVE_U, DRIVE_V, ICE = range(7)

VMEM = pl.BlockSpec(memory_space=pltpu.VMEM)
SMEM = pl.BlockSpec(memory_space=pltpu.SMEM)
ANY = pl.BlockSpec(memory_space=pl.ANY)


def partner(me, step, count):
    if count & (count - 1) == 0:
        return me ^ step
    return (me + step) % count


def from_behind(value, axis, steps):
    count = lax.axis_size(axis)
    first, last = (max(0, -steps), min(count, count - steps))
    return lax.ppermute(value, axis, [(source, source + steps) for source in range(first, last)])


def own_field(index, vel, visc, fric, drive, rows):
    if index in (U, V):
        return vel[index, rows, :].astype(jnp.float32)
    if index == VISC:
        return visc[rows, :]
    if index == FRIC:
        return fric[rows, :]
    return drive[index - DRIVE_U, rows, :].astype(jnp.float32)


def ice_row(ice, tile_row, shape, tile):
    lane = lax.broadcasted_iota(jnp.int32, shape, 1)
    row = jnp.zeros(shape, jnp.float32)
    for column in range(shape[1] // tile):
        row = jnp.where(lane // tile == column, ice[tile_row, column].astype(jnp.float32), row)
    return row


def send_kernel(groups, count, tile, *refs):
    owner, slot, weight, ice, obs, vel, visc, fric, drive = refs[:9]
    pays = refs[9 : 9 + groups]
    to_low, to_high = refs[9 + groups : 11 + groups]
    place, filled, edges, extra, scene_sem, edge_sem, extra_sem = refs[11 + groups :]
    blocks = tile // PACK
    me = lax.axis_index("gx")
    edge_copies = [
        pltpu.make_async_copy(obs.at[:, at], edges.at[number], edge_sem.at[number])
        for number, at in enumerate((0, blocks, blocks - 1, 2 * blocks - 1))
    ]
    for copy in edge_copies:
        copy.start()
    for index in range((groups + 2) * CAP):
        place[index] = -1
    for index in range(groups):
        filled[index] = 0
    for scene in range(count):
        who = owner[scene]
        rank = filled[who]
        place[(who + 1) * CAP + rank] = scene
        filled[who] = rank + 1
    copies = []
    for step in range(groups):
        to = partner(me, step, groups)
        for rank in range(CAP):
            scene = jnp.maximum(place[(to + 1) * CAP + rank], 0)
            copy = pltpu.make_async_copy(
                obs.at[scene],
                pays[step].at[pl.ds(rank * 2 * blocks, 2 * blocks)],
                scene_sem.at[step * CAP + rank],
            )
            copy.start()
            copies.append(copy)
    cells = visc.shape[0]
    for index, (at, depth) in enumerate(FIELDS[:-1]):
        to_low[at : at + depth, :] = own_field(index, vel, visc, fric, drive, slice(0, depth))
        to_high[at : at + depth, :] = own_field(index, vel, visc, fric, drive, slice(cells - depth, cells))
    at = FIELDS[ICE][0]
    to_low[at : at + 1, :] = ice_row(ice, 0, (1, visc.shape[1]), tile)
    to_high[at : at + 1, :] = ice_row(ice, cells // tile - 1, (1, visc.shape[1]), tile)
    for copy in edge_copies:
        copy.wait()
    row = lax.broadcasted_iota(jnp.int32, (PACK, LANE), 0)
    lane = lax.broadcasted_iota(jnp.int32, (PACK, LANE), 1)
    for step in range(groups):
        to = partner(me, step, groups)
        block = jnp.zeros((PACK, LANE), jnp.float32)
        for side in range(2):
            for rank in range(CAP):
                spot = place[(to + (2 if side == 0 else 0)) * CAP + rank]
                scene = jnp.maximum(spot, 0)
                amount = jnp.where(spot >= 0, weight[scene], 0.0)
                where = slot[scene]
                for part in range(2):
                    line = edges[side * 2 + part, scene].astype(jnp.float32)
                    line = line[0:1] if side == 0 else line[PACK - 1 : PACK]
                    block = jnp.where(row == (side * CAP + rank) * 2 + part, line, block)
                    value = jnp.where(where == side * 2 + part, amount, 0.0)
                    block = jnp.where((row == 8) & (lane == 8 + (side * CAP + rank) * 2 + part), value, block)
        for rank in range(CAP):
            spot = place[(to + 1) * CAP + rank]
            scene = jnp.maximum(spot, 0)
            amount = jnp.where(spot >= 0, weight[scene], 0.0)
            for position in range(4):
                value = jnp.where(slot[scene] == position, amount, 0.0)
                block = jnp.where((row == 8) & (lane == rank * 4 + position), value, block)
        extra[step] = block.astype(jnp.bfloat16)
        copy = pltpu.make_async_copy(
            extra.at[pl.ds(step, 1)], pays[step].at[pl.ds(CAP * 2 * blocks, 1)], extra_sem.at[step]
        )
        copy.start()
        copies.append(copy)
    for copy in copies:
        copy.wait()


def columns_of(block, first):
    picked = lax.broadcasted_iota(jnp.int32, (8, LANE), 0) + first
    pick = (picked == lax.broadcasted_iota(jnp.int32, (8, LANE), 1)).astype(jnp.float32)
    return lax.dot_general(
        pick, block, (((1,), (1,)), ((), ())),
        precision=lax.Precision.HIGHEST, preferred_element_type=jnp.float32,
    )


def widen_kernel(tile, ice, vel, visc, fric, drive, low, high, ext, to_low, to_high):
    cells = visc.shape[0]
    rows = ext.shape[1]
    own = slice(PAD, PAD + cells)
    to_low[...] = jnp.zeros_like(to_low)
    to_high[...] = jnp.zeros_like(to_high)
    for index, (at, depth) in enumerate(FIELDS):
        ext[index, 0:PAD, :] = jnp.zeros((PAD, ext.shape[2]), jnp.float32)
        ext[index, PAD + cells :, :] = jnp.zeros((PAD, ext.shape[2]), jnp.float32)
        if index == ICE:
            for tile_row in range(cells // tile):
                ext[index, PAD + tile_row * tile : PAD + (tile_row + 1) * tile, :] = ice_row(
                    ice, tile_row, (tile, ext.shape[2]), tile
                )
        else:
            ext[index, own, :] = own_field(index, vel, visc, fric, drive, slice(None))
        ext[index, PAD - depth : PAD, :] = low[at : at + depth, :]
        ext[index, PAD + cells : PAD + cells + depth, :] = high[at : at + depth, :]
        if index != ICE:
            first = columns_of(ext[index, :, 0:LANE], 0)
            last = columns_of(ext[index, :, ext.shape[2] - LANE :], LANE - depth)
            to_low[at : at + depth, 0:rows] = first[0:depth]
            to_high[at : at + depth, 0:rows] = last[0:depth]


def stress_block(u, v, visc, low, rows, wide):
    here, after = pl.ds(low, rows), pl.ds(low + 1, rows)
    vel_u, vel_v = u[here, :], v[here, :]
    a_x = u[after, :] - vel_u
    b_x = v[after, :] - vel_v
    a_y = pltpu.roll(vel_u, wide - 1, 1) - vel_u
    b_y = pltpu.roll(vel_v, wide - 1, 1) - vel_v
    nu = visc[here, :]
    return nu * (4.0 * a_x + 2.0 * b_y), nu * (4.0 * b_y + 2.0 * a_x), nu * (a_y + b_x)


def image_block(sxx, syy, sxy, low, rows):
    here, before = pl.ds(low, rows), pl.ds(low - 1, rows)
    mid = sxy[here, :]
    push_u = sxx[before, :] - sxx[here, :] + pltpu.roll(mid, 1, 1) - mid
    side = syy[here, :]
    push_v = sxy[before, :] - mid + pltpu.roll(side, 1, 1) - side
    return push_u, push_v


def sweep_kernel(ext, left, right, second, ease, lead, trail, wide_visc, *scratch):
    rows, cells_y = ext.shape[1], ext.shape[2]
    wide = cells_y + LANE
    u, v, fric, drive_u, drive_v, next_u, next_v, relax_u, relax_v, sxx, syy, sxy, turned = scratch
    turned[...] = jnp.zeros_like(turned)
    turned[0:PACK, :] = right[...]
    turned[PACK : 2 * PACK, :] = left[...]
    upright = jnp.transpose(turned[...])[0:rows]
    lane = lax.broadcasted_iota(jnp.int32, (rows, LANE), 1)
    fields = (u, v, wide_visc, fric, drive_u, drive_v)
    for index, field in enumerate(fields):
        at, depth = FIELDS[index]
        field[:, 0:cells_y] = ext[index]
        after = pltpu.roll(upright, (LANE - at) % LANE, 1)
        before = pltpu.roll(upright, (LANE - depth - PACK - at) % LANE, 1)
        field[:, cells_y:wide] = jnp.where(
            lane < depth, after, jnp.where(lane >= LANE - depth, before, 0.0)
        )
    blocks = range(8, rows - 8, 8)
    own = range(PAD, rows - PAD, 8)
    for low in blocks:
        here = pl.ds(low, 8)
        nu, drag = wide_visc[here, :], fric[here, :]
        nu_x = wide_visc[pl.ds(low - 1, 8), :]
        nu_y = pltpu.roll(nu, 1, 1)
        inside = drag > 0.0
        for out, diag in ((relax_u, 5.0 * nu + 4.0 * nu_x + nu_y), (relax_v, 5.0 * nu + nu_x + 4.0 * nu_y)):
            out[here, :] = jnp.where(inside, 1.0 / jnp.where(inside, diag + drag, 1.0), 0.0)
    for low in blocks:
        here = pl.ds(low, 8)
        sxx[here, :], syy[here, :], sxy[here, :] = stress_block(u, v, wide_visc, low, 8, wide)
    for low in blocks:
        here = pl.ds(low, 8)
        pushes = image_block(sxx, syy, sxy, low, 8)
        for part, (push, vel, force, relax, after) in enumerate(
            zip(pushes, (u, v), (drive_u, drive_v), (relax_u, relax_v), (next_u, next_v))
        ):
            now, soft = vel[here, :], relax[here, :]
            move = soft * (force[here, :] - push - fric[here, :] * now)
            after[here, :] = now + OMEGA * move
            slack = OMEGA * soft
            ease[part, here, :] = slack[:, 0:cells_y]
            if low in own:
                lead[part, pl.ds(low - PAD, 8), :] = (slack * (move + now))[:, 0:cells_y]
    for low in blocks:
        here = pl.ds(low, 8)
        sxx[here, :], syy[here, :], sxy[here, :] = stress_block(next_u, next_v, wide_visc, low, 8, wide)
    for low in blocks:
        here = pl.ds(low, 8)
        pushes = image_block(sxx, syy, sxy, low, 8)
        for part, (push, vel, force, relax) in enumerate(
            zip(pushes, (next_u, next_v), (drive_u, drive_v), (relax_u, relax_v))
        ):
            now = vel[here, :]
            move = relax[here, :] * (force[here, :] - push - fric[here, :] * now)
            second[part, here, :] = (now + OMEGA * move)[:, 0:cells_y]
            if low in own:
                trail[part, pl.ds(low - PAD, 8), :] = (move + now)[:, 0:cells_y]


def misfit_kernel(groups, tile, *refs):
    pays = refs[:groups]
    second, ease, ext, misfit, lift, to_low, to_high, table, total = refs[groups:]
    rows, cells_y = second.shape[1], second.shape[2]
    cells = rows - 2 * PAD
    blocks = tile // PACK
    tiles_y = cells_y // tile
    slots = cells // tile * tiles_y
    places = groups * CAP
    total[...] = jnp.zeros_like(total)
    ring = [[[jnp.zeros((1, LANE), jnp.float32) for _ in range(2)] for _ in range(2)] for _ in range(2)]
    ring_weight = [[jnp.zeros((1, LANE), jnp.float32) for _ in range(2)] for _ in range(2)]
    for group in range(groups):
        block = pays[group][CAP * 2 * blocks].astype(jnp.float32)
        meta = block[8:9]
        for index in range(CAP * slots):
            line = jnp.broadcast_to(meta[:, index : index + 1], (1, LANE))
            table[pl.ds(group * CAP * slots + index, 1), :] = line
            total[pl.ds(index % slots, 1), :] += line
        for side in range(2):
            for rank in range(CAP):
                for column in range(2):
                    index = 8 + (side * CAP + rank) * 2 + column
                    line = jnp.broadcast_to(meta[:, index : index + 1], (1, LANE))
                    ring_weight[side][column] += line
                    for part in range(2):
                        at = (side * CAP + rank) * 2 + part
                        ring[side][part][column] += line * block[at : at + 1]
    lift[:, 0:PAD, :] = jnp.zeros((2, PAD, cells_y), jnp.float32)
    lift[:, PAD + cells :, :] = jnp.zeros((2, PAD, cells_y), jnp.float32)
    for side, at in enumerate((PAD + cells, PAD - 1)):
        for column in range(2):
            lanes = slice(column * tile, (column + 1) * tile)
            for part in range(2):
                cold = ext[ICE, at : at + 1, lanes]
                gap = cold * (ring_weight[side][column] * second[part, at : at + 1, lanes] - ring[side][part][column])
                lift[part, at : at + 1, lanes] = ease[part, at : at + 1, lanes] * gap

    def step(index, carry):
        part, chunk = index // blocks, index % blocks
        sums = [jnp.zeros((PACK, LANE), jnp.float32) for _ in range(slots)]
        for spot in range(places):
            got = pays[spot // CAP][(spot % CAP) * 2 * blocks + index].astype(jnp.float32)
            for position in range(slots):
                sums[position] += table[pl.ds(spot * slots + position, 1), :] * got
        for position in range(slots):
            lanes = slice((position % tiles_y) * tile, (position % tiles_y + 1) * tile)
            at = pl.multiple_of((position // tiles_y) * tile + chunk * PACK, PACK)
            wide_at = pl.multiple_of(at + PAD, PACK)
            cold = ext[ICE, pl.ds(wide_at, PACK), lanes]
            gap = cold * (
                total[pl.ds(position, 1), :] * second[part, pl.ds(wide_at, PACK), lanes] - sums[position]
            )
            misfit[part, pl.ds(at, PACK), lanes] = gap
            lift[part, pl.ds(wide_at, PACK), lanes] = ease[part, pl.ds(wide_at, PACK), lanes] * gap
        return carry

    lax.fori_loop(0, 2 * blocks, step, 0)
    to_low[...] = jnp.zeros_like(to_low)
    to_high[...] = jnp.zeros_like(to_high)
    for part in range(2):
        to_low[part : part + 1, 0:rows] = columns_of(lift[part, :, 0:LANE], 0)[0:1]
        to_high[part : part + 1, 0:rows] = columns_of(lift[part, :, cells_y - LANE :], LANE - 1)[0:1]


def grad_kernel(lift, misfit, left, right, ext, visc, lead, trail, grad, u, v, sxx, syy, sxy, turned):
    rows, cells_y = lift.shape[1], lift.shape[2]
    wide = cells_y + LANE
    turned[...] = jnp.zeros_like(turned)
    turned[0:8, :] = right[...]
    turned[8:16, :] = left[...]
    upright = jnp.transpose(turned[...])[0:rows]
    lane = lax.broadcasted_iota(jnp.int32, (rows, LANE), 1)
    for part, field in enumerate((u, v)):
        field[:, 0:cells_y] = lift[part]
        after = pltpu.roll(upright, (LANE - part) % LANE, 1)
        before = pltpu.roll(upright, LANE - 1 - 8 - part, 1)
        field[:, cells_y:wide] = jnp.where(lane == 0, after, jnp.where(lane == LANE - 1, before, 0.0))
    for low in range(8, rows - PAD, 8):
        here = pl.ds(low, 8)
        sxx[here, :], syy[here, :], sxy[here, :] = stress_block(u, v, visc, low, 8, wide)
    for low in range(PAD, rows - PAD, 8):
        own = pl.ds(low - PAD, 8)
        here = pl.ds(low, 8)
        drag = ext[FRIC, here, :]
        sums = jnp.zeros((8, cells_y), jnp.float32)
        for part, push in enumerate(image_block(sxx, syy, sxy, low, 8)):
            now = lift[part, here, :]
            back = misfit[part, own, :] - push[:, 0:cells_y] - drag * now
            sums += back * lead[part, own, :] + now * trail[part, own, :]
        grad[own, :] = -ext[ICE, here, :] * sums


def body(vel0, visc, fric, drive, scene_obs, scene_weight, scene_owner, scene_slot, ice_mask):
    cells_x, cells_y = visc.shape
    tile = scene_obs.shape[-1]
    count = scene_obs.shape[1]
    groups = lax.axis_size("gx")
    blocks = tile // PACK
    rows, wide = cells_x + 2 * PAD, cells_y + LANE
    long = -(-rows // LANE) * LANE
    f32 = jnp.float32
    obs = scene_obs.reshape(count, 2 * blocks, PACK, LANE)
    limit = 32 << 20

    def shape(*dims, dtype=f32):
        return jax.ShapeDtypeStruct(dims, dtype)

    pay = shape(CAP * 2 * blocks + 1, PACK, LANE, dtype=jnp.bfloat16)
    *pays, x_low, x_high = pl.pallas_call(
        functools.partial(send_kernel, groups, count, tile),
        out_shape=[pay] * groups + [shape(PACK, cells_y)] * 2,
        in_specs=[SMEM] * 4 + [ANY] + [VMEM] * 4,
        out_specs=[ANY] * groups + [VMEM] * 2,
        scratch_shapes=[
            pltpu.SMEM(((groups + 2) * CAP,), jnp.int32),
            pltpu.SMEM((groups,), jnp.int32),
            pltpu.VMEM((4, count, PACK, LANE), jnp.bfloat16),
            pltpu.VMEM((groups, PACK, LANE), jnp.bfloat16),
            pltpu.SemaphoreType.DMA((groups * CAP,)),
            pltpu.SemaphoreType.DMA((4,)),
            pltpu.SemaphoreType.DMA((groups,)),
        ],
        compiler_params=pltpu.CompilerParams(vmem_limit_bytes=limit),
        name="send",
    )(
        scene_owner.reshape(count), scene_slot.reshape(count), scene_weight.reshape(count).astype(f32),
        ice_mask, obs, vel0, visc, fric, drive,
    )
    from_high = from_behind(x_low, "gx", -1)
    from_low = from_behind(x_high, "gx", 1)
    got = [pays[0]]
    for step in range(1, groups):
        pairs = [(me, partner(me, step, groups)) for me in range(groups)]
        got.append(lax.ppermute(pays[step], "gx", pairs))
    ext, y_low, y_high = pl.pallas_call(
        functools.partial(widen_kernel, tile),
        out_shape=[shape(len(FIELDS), rows, cells_y), shape(PACK, long), shape(PACK, long)],
        in_specs=[SMEM] + [VMEM] * 6,
        out_specs=[VMEM] * 3,
        compiler_params=pltpu.CompilerParams(vmem_limit_bytes=limit),
        name="widen",
    )(ice_mask, vel0, visc, fric, drive, from_low, from_high)
    y_right = from_behind(y_low, "gy", -1)
    y_left = from_behind(y_high, "gy", 1)
    second, ease, lead, trail, wide_visc = pl.pallas_call(
        sweep_kernel,
        out_shape=[
            shape(2, rows, cells_y), shape(2, rows, cells_y), shape(2, cells_x, cells_y),
            shape(2, cells_x, cells_y), shape(rows, wide),
        ],
        in_specs=[VMEM] * 3,
        out_specs=[VMEM] * 5,
        scratch_shapes=[pltpu.VMEM((rows, wide), f32)] * 12 + [pltpu.VMEM((LANE, long), f32)],
        compiler_params=pltpu.CompilerParams(vmem_limit_bytes=limit),
        name="sweep",
    )(ext, y_left, y_right)
    misfit, lift, lift_low, lift_high = pl.pallas_call(
        functools.partial(misfit_kernel, groups, tile),
        out_shape=[shape(2, cells_x, cells_y), shape(2, rows, cells_y), shape(8, long), shape(8, long)],
        in_specs=[VMEM] * (groups + 3),
        out_specs=[VMEM] * 4,
        scratch_shapes=[pltpu.VMEM((groups * CAP * 4, LANE), f32), pltpu.VMEM((8, LANE), f32)],
        compiler_params=pltpu.CompilerParams(vmem_limit_bytes=limit),
        name="misfit",
    )(*got, second, ease, ext)
    lift_right = from_behind(lift_low, "gy", -1)
    lift_left = from_behind(lift_high, "gy", 1)
    return pl.pallas_call(
        grad_kernel,
        out_shape=shape(cells_x, cells_y),
        in_specs=[VMEM] * 8,
        out_specs=VMEM,
        scratch_shapes=[pltpu.VMEM((rows, wide), f32)] * 5 + [pltpu.VMEM((LANE, long), f32)],
        compiler_params=pltpu.CompilerParams(vmem_limit_bytes=limit),
        name="grad",
    )(lift, misfit, lift_left, lift_right, ext, wide_visc, lead, trail)


def solution(mesh):
    placed = (
        P(None, "gx", "gy"),
        P("gx", "gy"),
        P("gx", "gy"),
        P(None, "gx", "gy"),
        P("gy", "gx", None, None, None),
        P("gy", "gx"),
        P("gy", "gx", None),
        P("gy", "gx"),
        P("gx", "gy"),
    )
    return jax.shard_map(body, mesh=mesh, in_specs=placed, out_specs=P("gx", "gy"), check_vma=False)
```

```python
import functools

import jax
import jax.numpy as jnp
from jax import lax
from jax.experimental import pallas as pl
from jax.experimental.pallas import tpu as pltpu
from jax.sharding import PartitionSpec as P

CAP = 2
OMEGA = 0.6
LANE = 128
PAD = 16
PACK = 16
FIELDS = ((0, 3), (3, 3), (6, 3), (9, 2), (11, 2), (13, 2), (15, 1))
U, V, VISC, FRIC, DRIVE_U, DRIVE_V, ICE = range(7)
SCENES = PACK

VMEM = pl.BlockSpec(memory_space=pltpu.VMEM)
HBM = pl.BlockSpec(memory_space=pltpu.HBM)
F32 = jnp.float32


def partner(me, step, count):
    if count & (count - 1) == 0:
        return me ^ step
    return (me + step) % count


def from_behind(value, axis, steps):
    count = lax.axis_size(axis)
    first, last = (max(0, -steps), min(count, count - steps))
    return lax.ppermute(value, axis, [(source, source + steps) for source in range(first, last)])


def after(value, *others):
    return lax.optimization_barrier((value, *others))[0]


def in_place(*values):
    return [pltpu.with_memory_space_constraint(value, pltpu.HBM) for value in values]


def copy_all(pairs, sems, first=0):
    copies = [
        pltpu.make_async_copy(source, target, sems.at[first + number])
        for number, (source, target) in enumerate(pairs)
    ]
    for copy in copies:
        copy.start()
    return copies


def wait_all(copies):
    for copy in copies:
        copy.wait()


def ice_line(values, shape, tile):
    lane = lax.broadcasted_iota(jnp.int32, shape, 1)
    line = jnp.zeros(shape, F32)
    for number, value in enumerate(values):
        line = jnp.where(lane // tile == number, value.astype(F32), line)
    return line


def fill_places(place, filled, groups, count, owner_of):
    for index in range((groups + 2) * CAP):
        place[index] = -1
    for index in range(groups):
        filled[index] = 0
    for scene in range(count):
        who = owner_of(scene)
        rank = filled[who]
        place[(who + 1) * CAP + rank] = scene
        filled[who] = rank + 1


def columns_of(pick, block, precision):
    return lax.dot_general(
        pick, block, (((1,), (1,)), ((), ())), precision=precision, preferred_element_type=F32
    )


def load_scalars(owner, slot, weight, owner_s, slot_s, weight_b, weight_v, weight_s, sems):
    loads = copy_all([(owner, owner_s), (slot, slot_s), (weight, weight_b)], sems)
    loads[2].wait()
    weight_v[...] = weight_b[...].astype(F32)
    loads[2] = pltpu.make_async_copy(weight_v, weight_s, sems.at[2])
    loads[2].start()
    return loads


def easting_block(to, place, slot_s, weight_s, edge):
    row = lax.broadcasted_iota(jnp.int32, (PACK, LANE), 0)
    lane = lax.broadcasted_iota(jnp.int32, (PACK, LANE), 1)
    block = jnp.zeros((PACK, LANE), F32)
    for side in range(2):
        for rank in range(CAP):
            spot = place[(to + (2 if side == 0 else 0)) * CAP + rank]
            scene = jnp.maximum(spot, 0)
            amount = jnp.where(spot >= 0, weight_s[0, scene], 0.0)
            where = slot_s[0, scene]
            for part in range(2):
                line = edge(scene, part, side).astype(F32)
                line = line[0:1] if side == 0 else line[PACK - 1 : PACK]
                block = jnp.where(row == (side * CAP + rank) * 2 + part, line, block)
                value = jnp.where(where == side * 2 + part, amount, 0.0)
                block = jnp.where((row == 8) & (lane == 8 + (side * CAP + rank) * 2 + part), value, block)
    for rank in range(CAP):
        spot = place[(to + 1) * CAP + rank]
        scene = jnp.maximum(spot, 0)
        amount = jnp.where(spot >= 0, weight_s[0, scene], 0.0)
        for position in range(4):
            value = jnp.where(slot_s[0, scene] == position, amount, 0.0)
            block = jnp.where((row == 8) & (lane == rank * 4 + position), value, block)
    return block.astype(jnp.bfloat16)


def gather_scenes(obs, pays, steps, place, groups, blocks, me, sems):
    copies = []
    for number, step in enumerate(steps):
        to = partner(me, step, groups)
        for rank in range(CAP):
            scene = jnp.maximum(place[(to + 1) * CAP + rank], 0)
            target = pays[number].at[pl.ds(rank * 2 * blocks, 2 * blocks)]
            copies += copy_all([(obs.at[scene], target)], sems, number * CAP + rank)
    return copies


def send_kernel(groups, count, tile, steps, *refs):
    owner, slot, weight, obs = refs[:4]
    pays = refs[4 : 4 + len(steps)]
    owner_s, slot_s, weight_b, weight_v, weight_s, edges, place, filled, scalar_sem, edge_sem, scene_sem = refs[
        4 + len(steps) :
    ]
    blocks = tile // PACK
    me = lax.axis_index("gx")
    loads = copy_all(
        [(obs.at[:, at], edges.at[number]) for number, at in enumerate((0, blocks, blocks - 1, 2 * blocks - 1))], edge_sem
    )
    scalars = load_scalars(owner, slot, weight, owner_s, slot_s, weight_b, weight_v, weight_s, scalar_sem)
    scalars[0].wait()
    fill_places(place, filled, groups, count, lambda scene: owner_s[0, scene])
    copies = gather_scenes(obs, pays, steps, place, groups, blocks, me, scene_sem)
    wait_all(scalars[1:] + loads)
    for number, step in enumerate(steps):
        to = partner(me, step, groups)
        pays[number][CAP * 2 * blocks] = easting_block(
            to, place, slot_s, weight_s, lambda scene, part, side: edges[side * 2 + part, scene]
        )
    wait_all(copies)


def pack_kernel(groups, count, tile, steps, *refs):
    owner, slot, weight, ice, obs_h, vel_h, visc_h, fric_h, drive_h = refs[:9]
    pays = refs[9 : 9 + len(steps)]
    to_low, to_high = refs[9 + len(steps) : 11 + len(steps)]
    (
        owner_s, slot_s, weight_b, weight_v, weight_s, ice_s, owner_v, slot_v, obs, vel, visc, fric, drive,
        place, filled, scalar_sem, more_sem, load_sem, scene_sem,
    ) = refs[11 + len(steps) :]
    blocks = tile // PACK
    me = lax.axis_index("gx")
    loads = copy_all([(vel_h, vel), (drive_h, drive), (visc_h, visc), (fric_h, fric), (obs_h, obs)], load_sem)
    more = copy_all([(ice, ice_s), (owner, owner_v), (slot, slot_v)], more_sem)
    scalars = load_scalars(owner, slot, weight, owner_s, slot_s, weight_b, weight_v, weight_s, scalar_sem)
    scalars[0].wait()
    fill_places(place, filled, groups, count, lambda scene: owner_s[0, scene])
    copies = gather_scenes(obs_h, pays, steps, place, groups, blocks, me, scene_sem)
    picked = lax.broadcasted_iota(jnp.int32, (8, LANE), 0)
    across = lax.broadcasted_iota(jnp.int32, (8, LANE), 1)
    cells_y = visc.shape[1]

    def pick(first, kind):
        return (across == picked + first).astype(kind)

    wait_all(loads[:4])
    for index, (at, depth) in enumerate(FIELDS[:-1]):
        for target, low, first in ((to_low, 0, 0), (to_high, cells_y - LANE, LANE - depth)):
            lanes = slice(low, low + LANE)
            if index in (VISC, FRIC):
                field = (visc if index == VISC else fric)[:, lanes]
                rows = columns_of(pick(first, F32), field, lax.Precision.HIGHEST)
            else:
                field = vel[index, :, lanes] if index in (U, V) else drive[index - DRIVE_U, :, lanes]
                rows = columns_of(pick(first, jnp.bfloat16), field, None)
            target[at : at + depth, :] = rows[0:depth]
    loads[4].wait()
    both = (across == jnp.where(picked == 0, 0, LANE - 1)).astype(jnp.bfloat16)
    for scene in range(count):
        rows = columns_of(both, obs[scene].reshape(2 * tile, LANE), None)
        to_low[SCENES + scene : SCENES + scene + 1, :] = rows[0:1]
        to_high[SCENES + scene : SCENES + scene + 1, :] = rows[1:2]
    wait_all(scalars[1:] + more)
    for target, at in ((to_low, 0), (to_high, ice_s.shape[1] - 1)):
        target[SCENES + count :, :] = jnp.zeros((8, target.shape[1]), F32)
        for number, values in enumerate((owner_v, slot_v, weight_v)):
            target[SCENES + count + number : SCENES + count + number + 1, 0:count] = values[...].astype(F32)
        row = FIELDS[ICE][0]
        target[row : row + 1, :] = ice_line(
            [ice_s[number, at] for number in range(ice_s.shape[0])], (1, target.shape[1]), tile
        )
    for number, step in enumerate(steps):
        to = partner(me, step, groups)
        pays[number][CAP * 2 * blocks] = easting_block(
            to, place, slot_s, weight_s,
            lambda scene, part, side: obs[scene, part * blocks + (0 if side == 0 else blocks - 1)],
        )
    wait_all(copies)


def side_tiles(right, left, turned):
    turned[...] = jnp.zeros_like(turned)
    turned[0:PACK, :] = right[0:PACK, :]
    turned[PACK : 2 * PACK, :] = left[0:PACK, :]
    return jnp.transpose(turned[...])


def side_tile(upright, index):
    at, depth = FIELDS[index]
    lane = lax.broadcasted_iota(jnp.int32, upright.shape, 1)
    after = pltpu.roll(upright, (LANE - at) % LANE, 1)
    before = pltpu.roll(upright, LANE - depth - PACK - at, 1)
    return jnp.where(lane < depth, after, jnp.where(lane >= LANE - depth, before, 0.0))


def widen_kernel(groups, count, tile, early, late, *refs):
    ice, vel, visc, fric, drive, right, left = refs[:7]
    pays = refs[7 + len(late) : 7 + 2 * len(late)]
    apart = refs[7 + 2 * len(late) : 7 + 2 * len(late) + len(early)]
    to_low, to_high = refs[7 + 2 * len(late) + len(early) : 9 + 2 * len(late) + len(early)]
    ice_s, notes, first_b, last_b, first_f, last_f, turned, place, filled, sems = refs[
        9 + 2 * len(late) + len(early) :
    ]
    cells = visc.shape[0]
    cells_y = visc.shape[1]
    blocks = tile // PACK
    me = lax.axis_index("gx")
    tail = pl.ds(SCENES + count, 8)
    loads = copy_all(
        [
            (right.at[tail], notes.at[0]), (left.at[tail], notes.at[1]), (ice, ice_s),
            (vel.at[:, 0:16], first_b.at[0:2]), (drive.at[:, 0:16], first_b.at[2:4]),
            (vel.at[:, cells - 16 : cells], last_b.at[0:2]), (drive.at[:, cells - 16 : cells], last_b.at[2:4]),
            (visc.at[0:8], first_f.at[0]), (fric.at[0:8], first_f.at[1]),
            (visc.at[cells - 8 : cells], last_f.at[0]), (fric.at[cells - 8 : cells], last_f.at[1]),
        ],
        sems,
    )
    upright = side_tiles(right, left, turned)
    wait_all(loads)
    for index, (at, depth) in enumerate(FIELDS):
        if index == ICE:
            first, last = (
                ice_line([ice_s[number, column] for column in range(ice_s.shape[1])], (1, cells_y), tile)
                for number in (0, ice_s.shape[0] - 1)
            )
        elif index in (VISC, FRIC):
            first, last = first_f[index - VISC], last_f[index - VISC]
        else:
            number = index if index in (U, V) else index - DRIVE_U + 2
            first, last = first_b[number].astype(F32), last_b[number].astype(F32)
        to_low[at : at + depth, 0:cells_y] = first[0:depth]
        to_high[at : at + depth, 0:cells_y] = last[last.shape[0] - depth :]
        to_low[at : at + depth, cells_y:] = side_tile(upright[0:8], index)[0:depth]
        to_high[at : at + depth, cells_y:] = side_tile(upright[cells - 8 :], index)[8 - depth : 8]
    packs = (right, left)
    for side in range(2):
        fill_places(place.at[side], filled, groups, count, lambda scene: notes[side, 0, scene].astype(jnp.int32))
    row = lax.broadcasted_iota(jnp.int32, (PACK, LANE), 0)
    lane = lax.broadcasted_iota(jnp.int32, (PACK, LANE), 1)
    for number, step in enumerate(late + early):
        to = partner(me, step, groups)
        block = jnp.zeros((PACK, LANE), F32)
        for side in range(2):
            for rank in range(CAP):
                spot = place[side, (to + 1) * CAP + rank]
                scene = jnp.maximum(spot, 0)
                amount = jnp.where(spot >= 0, notes[side, 2, scene], 0.0)
                where = notes[side, 1, scene].astype(jnp.int32)
                line = packs[side][pl.ds(SCENES + scene, 1), :]
                for part in range(2):
                    block = jnp.where(
                        row == (side * CAP + rank) * 2 + part, line[:, part * LANE : (part + 1) * LANE], block
                    )
                    value = jnp.where(where == part * 2 + side, amount, 0.0)
                    block = jnp.where((row == 8) & (lane == (side * CAP + rank) * 2 + part), value, block)
                spot = place[side, (to + (0 if side == 0 else 2)) * CAP + rank]
                scene = jnp.maximum(spot, 0)
                amount = jnp.where(spot >= 0, notes[side, 2, scene], 0.0)
                where = notes[side, 1, scene].astype(jnp.int32)
                line = packs[side][pl.ds(SCENES + scene, 1), :]
                at = tile - 1 if side == 0 else 0
                base = 8 + side * 6 + rank * 3
                for part in range(2):
                    value = jnp.broadcast_to(line[:, part * LANE + at : part * LANE + at + 1], (1, LANE))
                    block = jnp.where((row == 8) & (lane == base + part), value, block)
                value = jnp.where(where == (2 if side == 0 else 1), amount, 0.0)
                block = jnp.where((row == 8) & (lane == base + 2), value, block)
        if number < len(late):
            pays[number][CAP * 2 * blocks + 1] = block.astype(jnp.bfloat16)
        else:
            apart[number - len(late)][0] = block.astype(jnp.bfloat16)


def stress_block(u, v, visc, low, rows, wide):
    here, after = pl.ds(low, rows), pl.ds(low + 1, rows)
    vel_u, vel_v = u[here, :], v[here, :]
    a_x = u[after, :] - vel_u
    b_x = v[after, :] - vel_v
    a_y = pltpu.roll(vel_u, wide - 1, 1) - vel_u
    b_y = pltpu.roll(vel_v, wide - 1, 1) - vel_v
    nu = visc[here, :]
    return nu * (4.0 * a_x + 2.0 * b_y), nu * (4.0 * b_y + 2.0 * a_x), nu * (a_y + b_x)


def image_block(sxx, syy, sxy, low, rows):
    here, before = pl.ds(low, rows), pl.ds(low - 1, rows)
    mid = sxy[here, :]
    push_u = sxx[before, :] - sxx[here, :] + pltpu.roll(mid, 1, 1) - mid
    side = syy[here, :]
    push_v = sxy[before, :] - mid + pltpu.roll(side, 1, 1) - side
    return push_u, push_v


def sweep_kernel(tile, ice, vel, visc, fric, drive, right, left, low_pack, high_pack, *refs):
    second, ease, lead, trail, wide_visc, wide_ice = refs[:6]
    (
        u, v, wide_fric, drive_u, drive_v, next_u, next_v, relax_u, relax_v, sxx, syy, sxy, turned,
        ice_s, sems,
    ) = refs[6:]
    cells, cells_y = visc.shape
    rows, wide = wide_visc.shape
    loads = copy_all([(ice, ice_s)], sems)
    upright = side_tiles(right, left, turned)
    wait_all(loads)
    own_rows = slice(PAD, PAD + cells)
    for index, field in enumerate((u, v, wide_visc, wide_fric, drive_u, drive_v, wide_ice)):
        at, depth = FIELDS[index]
        field[0:PAD, :] = jnp.zeros((PAD, wide), F32)
        field[PAD + cells :, :] = jnp.zeros((PAD, wide), F32)
        if index == ICE:
            for number in range(cells // tile):
                field[PAD + number * tile : PAD + (number + 1) * tile, 0:cells_y] = ice_line(
                    [ice_s[number, column] for column in range(ice_s.shape[1])], (tile, cells_y), tile
                )
        elif index in (VISC, FRIC):
            field[own_rows, 0:cells_y] = (visc if index == VISC else fric)[...]
        else:
            source = vel if index in (U, V) else drive
            field[own_rows, 0:cells_y] = source[index % DRIVE_U].astype(F32)
        field[own_rows, cells_y:wide] = side_tile(upright, index)
        field[PAD - depth : PAD, :] = low_pack[at : at + depth, :]
        field[PAD + cells : PAD + cells + depth, :] = high_pack[at : at + depth, :]
    blocks = range(8, rows - 8, 8)
    own = range(PAD, rows - PAD, 8)
    for low in blocks:
        here = pl.ds(low, 8)
        nu, drag = wide_visc[here, :], wide_fric[here, :]
        nu_x = wide_visc[pl.ds(low - 1, 8), :]
        nu_y = pltpu.roll(nu, 1, 1)
        inside = drag > 0.0
        for out, diag in ((relax_u, 5.0 * nu + 4.0 * nu_x + nu_y), (relax_v, 5.0 * nu + nu_x + 4.0 * nu_y)):
            out[here, :] = jnp.where(inside, 1.0 / jnp.where(inside, diag + drag, 1.0), 0.0)
    for low in blocks:
        here = pl.ds(low, 8)
        sxx[here, :], syy[here, :], sxy[here, :] = stress_block(u, v, wide_visc, low, 8, wide)
    for low in blocks:
        here = pl.ds(low, 8)
        pushes = image_block(sxx, syy, sxy, low, 8)
        for part, (push, speed, force, relax, after) in enumerate(
            zip(pushes, (u, v), (drive_u, drive_v), (relax_u, relax_v), (next_u, next_v))
        ):
            now, soft = speed[here, :], relax[here, :]
            move = soft * (force[here, :] - push - wide_fric[here, :] * now)
            after[here, :] = now + OMEGA * move
            slack = OMEGA * soft
            ease[part, here, :] = slack
            if low in own:
                factor = -wide_ice[here, 0:cells_y] * (slack * (move + now))[:, 0:cells_y]
                lead[part, pl.ds(low - PAD, 8), :] = factor
    for low in blocks:
        here = pl.ds(low, 8)
        sxx[here, :], syy[here, :], sxy[here, :] = stress_block(next_u, next_v, wide_visc, low, 8, wide)
    for low in blocks:
        here = pl.ds(low, 8)
        pushes = image_block(sxx, syy, sxy, low, 8)
        for part, (push, speed, force, relax) in enumerate(
            zip(pushes, (next_u, next_v), (drive_u, drive_v), (relax_u, relax_v))
        ):
            now = speed[here, :]
            move = relax[here, :] * (force[here, :] - push - wide_fric[here, :] * now)
            second[part, here, :] = wide_ice[here, :] * (now + OMEGA * move)
            if low in own:
                mine = pl.ds(low - PAD, 8)
                trail[part, mine, :] = (
                    -wide_ice[here, 0:cells_y] * (move + now)[:, 0:cells_y]
                    - wide_fric[here, 0:cells_y] * lead[part, mine, :]
                )


def final_kernel(groups, tile, early, *refs):
    pays = refs[:groups]
    apart = dict(zip(early, refs[groups : groups + len(early)]))
    second, ease, lead, trail, visc, ice = refs[groups + len(early) : groups + len(early) + 6]
    grad = refs[groups + len(early) + 6]
    misfit, u, v, sxx, syy, sxy, table, total, rows_x, rows_y, turned = refs[groups + len(early) + 7 :]
    rows, wide = visc.shape
    cells_y = wide - LANE
    cells = rows - 2 * PAD
    blocks = tile // PACK
    tiles_y = cells_y // tile
    slots = cells // tile * tiles_y
    lift = (u, v)
    for group in range(groups):
        rows_x[pl.ds(group, PACK, stride=groups), :] = pays[group][CAP * 2 * blocks].astype(F32)
        side = apart[group][0] if group in apart else pays[group][CAP * 2 * blocks + 1]
        rows_y[pl.ds(group, PACK, stride=groups), :] = side.astype(F32)

    def raw(source, number):
        return source[number * groups : (number + 1) * groups, :]

    def spread(source, number):
        return jnp.broadcast_to(raw(source, 8)[:, number : number + 1], (groups, LANE))

    def gathered(value):
        return jnp.sum(value, axis=0, keepdims=True)

    for position in range(slots):
        weights = [spread(rows_x, rank * slots + position) for rank in range(CAP)]
        for rank in range(CAP):
            at = (rank * slots + position) * groups
            table[at : at + groups, :] = weights[rank]
        total[position : position + 1, :] = gathered(sum(weights))
    for field in lift:
        field[0:PAD, :] = jnp.zeros((PAD, wide), F32)
        field[PAD + cells :, :] = jnp.zeros((PAD, wide), F32)
    turned[...] = jnp.zeros_like(turned)
    for side in range(2):
        at = PAD + cells if side == 0 else PAD - 1
        for column in range(2):
            lanes = slice(column * tile, (column + 1) * tile)
            weights = [spread(rows_x, 8 + (side * CAP + rank) * 2 + column) for rank in range(CAP)]
            weight = gathered(sum(weights))
            for part in range(2):
                seen = gathered(sum(weights[rank] * raw(rows_x, (side * CAP + rank) * 2 + part) for rank in range(CAP)))
                gap = weight * second[part, at : at + 1, lanes] - ice[at : at + 1, lanes] * seen
                lift[part][at : at + 1, lanes] = ease[part, at : at + 1, lanes] * gap
        lines = [[None] * 2 for _ in range(3)]
        for column in range(2):
            weights = [spread(rows_y, (side * CAP + rank) * 2 + column) for rank in range(CAP)]
            lines[2][column] = gathered(sum(weights))
            for part in range(2):
                lines[part][column] = gathered(
                    sum(weights[rank] * raw(rows_y, (side * CAP + rank) * 2 + part) for rank in range(CAP))
                )
        weights = [spread(rows_y, 8 + side * 6 + rank * 3 + 2) for rank in range(CAP)]
        corners = [
            gathered(sum(weights[rank] * spread(rows_y, 8 + side * 6 + rank * 3 + part) for rank in range(CAP)))
            for part in range(2)
        ] + [gathered(sum(weights))]
        lane = lax.broadcasted_iota(jnp.int32, (1, turned.shape[1]), 1)
        for number in range(3):
            line = jnp.concatenate(
                lines[number] + [jnp.zeros((1, turned.shape[1] - 2 * tile), F32)], axis=1
            )
            line = pltpu.roll(jnp.broadcast_to(line, (8, turned.shape[1])), PAD, 1)[0:1]
            corner = jnp.concatenate([corners[number]] * (turned.shape[1] // LANE), axis=1)
            line = jnp.where(lane == (PAD - 1 if side == 0 else PAD + cells), corner, line)
            at = number if side == 0 else LANE - 1 - number
            turned[at : at + 1, :] = line
    upright = jnp.transpose(turned[...])[0:rows]
    lane = lax.broadcasted_iota(jnp.int32, (rows, LANE), 1)

    def sides(number):
        after = pltpu.roll(upright, (LANE - number) % LANE, 1)
        before = pltpu.roll(upright, number, 1)
        return jnp.where(lane == 0, after, jnp.where(lane == LANE - 1, before, 0.0))

    weight = sides(2)
    for part in range(2):
        gap = weight * second[part, :, cells_y:wide] - ice[:, cells_y:wide] * sides(part)
        lift[part][:, cells_y:wide] = ease[part, :, cells_y:wide] * gap

    def step(index, carry):
        part, chunk = index // blocks, index % blocks
        sums = [jnp.zeros((PACK, LANE), F32) for _ in range(slots)]
        for group in range(groups):
            for rank in range(CAP):
                got = pays[group][rank * 2 * blocks + index].astype(F32)
                for position in range(slots):
                    sums[position] += table[pl.ds((rank * slots + position) * groups + group, 1), :] * got
        for position in range(slots):
            lanes = slice((position % tiles_y) * tile, (position % tiles_y + 1) * tile)
            at = pl.multiple_of((position // tiles_y) * tile + chunk * PACK, PACK)
            here = pl.ds(pl.multiple_of(at + PAD, PACK), PACK)
            gap = total[position : position + 1, :] * second[part, here, lanes] - ice[here, lanes] * sums[position]
            misfit[part, pl.ds(at, PACK), lanes] = gap
            sums[position] = ease[part, here, lanes] * gap

        for number, field in enumerate(lift):

            @pl.when(part == number)
            def _():
                for position in range(slots):
                    lanes = slice((position % tiles_y) * tile, (position % tiles_y + 1) * tile)
                    at = pl.multiple_of((position // tiles_y) * tile + chunk * PACK + PAD, PACK)
                    field[pl.ds(at, PACK), lanes] = sums[position]

        return carry

    lax.fori_loop(0, 2 * blocks, step, 0)
    for low in range(8, rows - PAD, 8):
        here = pl.ds(low, 8)
        sxx[here, :], syy[here, :], sxy[here, :] = stress_block(u, v, visc, low, 8, wide)
    for low in range(PAD, rows - PAD, 8):
        mine = pl.ds(low - PAD, 8)
        here = pl.ds(low, 8)
        sums = jnp.zeros((8, cells_y), F32)
        for part, push in enumerate(image_block(sxx, syy, sxy, low, 8)):
            sums += (misfit[part, mine, :] - push[:, 0:cells_y]) * lead[part, mine, :]
            sums += lift[part][here, 0:cells_y] * trail[part, mine, :]
        grad[mine, :] = sums


def body(vel0, visc, fric, drive, scene_obs, scene_weight, scene_owner, scene_slot, ice_mask):
    cells_x, cells_y = visc.shape
    tile = scene_obs.shape[-1]
    count = scene_obs.shape[1]
    groups = lax.axis_size("gx")
    blocks = tile // PACK
    rows, wide = cells_x + 2 * PAD, cells_y + LANE
    long = -(-rows // LANE) * LANE
    obs = scene_obs.reshape(count, 2 * blocks, PACK, LANE)
    owner, slot, weight = scene_owner.reshape(1, count), scene_slot, scene_weight
    limit = pltpu.CompilerParams(vmem_limit_bytes=40 << 20)
    dma = pltpu.SemaphoreType.DMA
    early = (groups // 2, groups // 2 + 1)
    late = tuple(step for step in range(groups) if step not in early)

    def shape(*dims, dtype=F32):
        return jax.ShapeDtypeStruct(dims, dtype)

    def short(*dims):
        return pltpu.VMEM(dims, jnp.bfloat16)

    def full(*dims):
        return pltpu.VMEM(dims, F32)

    bf16, i32 = jnp.bfloat16, jnp.int32
    deep = CAP * 2 * blocks
    tall = SCENES + count + 8
    pairs = {step: [(me, partner(me, step, groups)) for me in range(groups)] for step in range(1, groups)}
    scalars = [
        pltpu.SMEM((1, count), i32), pltpu.SMEM((1, count), i32), short(1, count), full(1, count),
        pltpu.SMEM((1, count), F32),
    ]
    places = [pltpu.SMEM(((groups + 2) * CAP,), i32), pltpu.SMEM((groups,), i32)]
    sent = pl.pallas_call(
        functools.partial(send_kernel, groups, count, tile, early),
        out_shape=[pltpu.VMEM((deep + 1, PACK, LANE), bf16)] * len(early),
        in_specs=[HBM] * 4,
        out_specs=[VMEM] * len(early),
        scratch_shapes=scalars + [short(4, count, PACK, LANE)] + places
        + [dma((3,)), dma((4,)), dma((len(early) * CAP,))],
        compiler_params=limit,
        name="send",
    )(*in_place(owner, slot, weight, obs))
    got = {step: lax.ppermute(value, "gx", pairs[step]) for step, value in zip(early, sent)}
    *pays, y_low, y_high = pl.pallas_call(
        functools.partial(pack_kernel, groups, count, tile, late),
        out_shape=[pltpu.VMEM((deep + 2, PACK, LANE), bf16)] * len(late) + [pltpu.VMEM((tall, cells_x), F32)] * 2,
        in_specs=[HBM] * 9,
        out_specs=[VMEM] * (len(late) + 2),
        scratch_shapes=scalars
        + [pltpu.SMEM(ice_mask.shape, i32), pltpu.VMEM((1, count), i32), pltpu.VMEM((1, count), i32)]
        + [short(*obs.shape), short(*vel0.shape), full(*visc.shape), full(*fric.shape), short(*drive.shape)] + places
        + [dma((3,)), dma((3,)), dma((5,)), dma((len(late) * CAP,))],
        compiler_params=limit,
        name="pack",
    )(*in_place(owner, slot, weight, ice_mask, obs, vel0, visc, fric, drive))
    right = from_behind(y_low, "gy", -1)
    left = from_behind(y_high, "gy", 1)
    outs = pl.pallas_call(
        functools.partial(widen_kernel, groups, count, tile, early, late),
        out_shape=[pltpu.VMEM((deep + 2, PACK, LANE), bf16)] * len(late)
        + [pltpu.VMEM((1, PACK, LANE), bf16)] * len(early)
        + [pltpu.VMEM((PACK, wide), F32)] * 2,
        in_specs=[HBM] * 5 + [VMEM] * (2 + len(late)),
        out_specs=[VMEM] * (len(late) + len(early) + 2),
        input_output_aliases={7 + number: number for number in range(len(late))},
        scratch_shapes=[
            pltpu.SMEM(ice_mask.shape, i32), pltpu.SMEM((2, 8, cells_x), F32), short(4, 16, cells_y),
            short(4, 16, cells_y), full(2, 8, cells_y), full(2, 8, cells_y), full(LANE, cells_x),
            pltpu.SMEM((2, (groups + 2) * CAP), i32), pltpu.SMEM((groups,), i32), dma((11,)),
        ],
        compiler_params=limit,
        name="widen",
    )(*in_place(ice_mask, vel0, visc, fric, drive), right, left, *pays)
    ready = dict(zip(late, outs))
    x_low, x_high = outs[-2:]
    high_pack = from_behind(x_low, "gx", -1)
    low_pack = from_behind(x_high, "gx", 1)
    got[0] = ready[0]
    for step in late[1:]:
        value = ready[step] if step > groups // 2 else after(ready[step], got[early[0]])
        got[step] = lax.ppermute(value, "gx", pairs[step])
    apart = [
        lax.ppermute(after(value, got[early[1]]), "gx", pairs[step])
        for step, value in zip(early, outs[len(late) :])
    ]
    base = pl.pallas_call(
        functools.partial(sweep_kernel, tile),
        out_shape=[shape(2, rows, wide)] * 2 + [shape(2, cells_x, cells_y)] * 2 + [shape(rows, wide)] * 2,
        in_specs=[HBM] + [VMEM] * 8,
        out_specs=[VMEM] * 6,
        scratch_shapes=[full(rows, wide)] * 12
        + [full(LANE, cells_x), pltpu.SMEM(ice_mask.shape, i32), dma((1,))],
        compiler_params=limit,
        name="sweep",
    )(ice_mask, vel0, visc, fric, drive, right, left, low_pack, high_pack)
    return pl.pallas_call(
        functools.partial(final_kernel, groups, tile, early),
        out_shape=shape(cells_x, cells_y),
        in_specs=[VMEM] * (groups + len(early) + 6),
        out_specs=VMEM,
        scratch_shapes=[full(2, cells_x, cells_y)] + [full(rows, wide)] * 5
        + [
            full(groups * CAP * 4, LANE), full(8, LANE), full(PACK * groups, LANE), full(PACK * groups, LANE),
            full(LANE, long),
        ],
        compiler_params=limit,
        name="final",
    )(*(got[step] for step in range(groups)), *apart, *base)


def solution(mesh):
    placed = (
        P(None, "gx", "gy"),
        P("gx", "gy"),
        P("gx", "gy"),
        P(None, "gx", "gy"),
        P("gy", "gx", None, None, None),
        P("gy", "gx"),
        P("gy", "gx", None),
        P("gy", "gx"),
        P("gx", "gy"),
    )
    return jax.shard_map(body, mesh=mesh, in_specs=placed, out_specs=P("gx", "gy"), check_vma=False)
```

```python
import functools

import jax
import jax.numpy as jnp
from jax import lax
from jax.experimental import pallas as pl
from jax.experimental.pallas import tpu as pltpu
from jax.sharding import PartitionSpec as P

CAP = 2
OMEGA = 0.6
LANE = 128
PAD = 16
PACK = 16
FIELDS = ((0, 3), (3, 3), (6, 3), (9, 2), (11, 2), (13, 2), (15, 1))
U, V, VISC, FRIC, DRIVE_U, DRIVE_V, ICE = range(7)
SCENES = PACK

VMEM = pl.BlockSpec(memory_space=pltpu.VMEM)
HBM = pl.BlockSpec(memory_space=pltpu.HBM)
F32 = jnp.float32


def partner(me, step, count):
    return lax.rem(me + step, count) if isinstance(me, jax.Array) else (me + step) % count


def from_behind(value, axis, steps):
    count = lax.axis_size(axis)
    first, last = (max(0, -steps), min(count, count - steps))
    return lax.ppermute(value, axis, [(source, source + steps) for source in range(first, last)])


def after(value, *others):
    return lax.optimization_barrier((value, *others))[0]


def in_place(*values):
    return [pltpu.with_memory_space_constraint(value, pltpu.HBM) for value in values]


def copy_all(pairs, sems, first=0):
    copies = [
        pltpu.make_async_copy(source, target, sems.at[first + number])
        for number, (source, target) in enumerate(pairs)
    ]
    for copy in copies:
        copy.start()
    return copies


def wait_all(copies):
    for copy in copies:
        copy.wait()


def ice_line(values, shape, tile):
    lane = lax.broadcasted_iota(jnp.int32, shape, 1)
    line = jnp.zeros(shape, F32)
    for number, value in enumerate(values):
        line = jnp.where(lane // tile == number, value.astype(F32), line)
    return line


def fill_places(place, filled, groups, count, owner_of):
    for index in range((groups + 2) * CAP):
        place[index] = -1
    for index in range(groups):
        filled[index] = 0
    for scene in range(count):
        who = owner_of(scene)
        rank = filled[who]
        place[(who + 1) * CAP + rank] = scene
        filled[who] = rank + 1


def columns_of(pick, block, precision):
    return lax.dot_general(
        pick, block, (((1,), (1,)), ((), ())), precision=precision, preferred_element_type=F32
    )


def load_scalars(owner, slot, weight, owner_s, slot_s, weight_b, weight_v, weight_s, sems):
    loads = copy_all([(owner, owner_s), (slot, slot_s), (weight, weight_b)], sems)
    loads[2].wait()
    weight_v[...] = weight_b[...].astype(F32)
    loads[2] = pltpu.make_async_copy(weight_v, weight_s, sems.at[2])
    loads[2].start()
    return loads


def easting_block(to, place, slot_s, weight_s, edge):
    row = lax.broadcasted_iota(jnp.int32, (PACK, LANE), 0)
    lane = lax.broadcasted_iota(jnp.int32, (PACK, LANE), 1)
    block = jnp.zeros((PACK, LANE), F32)
    for side in range(2):
        for rank in range(CAP):
            spot = place[(to + (2 if side == 0 else 0)) * CAP + rank]
            scene = jnp.maximum(spot, 0)
            amount = jnp.where(spot >= 0, weight_s[0, scene], 0.0)
            where = slot_s[0, scene]
            for part in range(2):
                line = edge(scene, part, side).astype(F32)
                line = line[0:1] if side == 0 else line[PACK - 1 : PACK]
                block = jnp.where(row == (side * CAP + rank) * 2 + part, line, block)
                value = jnp.where(where == side * 2 + part, amount, 0.0)
                block = jnp.where((row == 8) & (lane == 8 + (side * CAP + rank) * 2 + part), value, block)
    for rank in range(CAP):
        spot = place[(to + 1) * CAP + rank]
        scene = jnp.maximum(spot, 0)
        amount = jnp.where(spot >= 0, weight_s[0, scene], 0.0)
        for position in range(4):
            value = jnp.where(slot_s[0, scene] == position, amount, 0.0)
            block = jnp.where((row == 8) & (lane == rank * 4 + position), value, block)
    return block.astype(jnp.bfloat16)


def gather_scenes(obs, pays, steps, place, groups, blocks, me, sems):
    copies = []
    for number, step in enumerate(steps):
        to = partner(me, step, groups)
        for rank in range(CAP):
            scene = jnp.maximum(place[(to + 1) * CAP + rank], 0)
            target = pays[number].at[pl.ds(rank * 2 * blocks, 2 * blocks)]
            copies += copy_all([(obs.at[scene], target)], sems, number * CAP + rank)
    return copies


def gather_kernel(groups, count, tile, *refs):
    owner, slot, weight, obs = refs[:4]
    pays = refs[4 : 4 + groups]
    owner_s, slot_s, weight_b, weight_v, weight_s, edges, place, filled, scalar_sem, edge_sem, scene_sem = refs[
        4 + groups :
    ]
    blocks = tile // PACK
    me = lax.axis_index("gx")
    loads = copy_all(
        [(obs.at[:, at], edges.at[number]) for number, at in enumerate((0, blocks, blocks - 1, 2 * blocks - 1))], edge_sem
    )
    scalars = load_scalars(owner, slot, weight, owner_s, slot_s, weight_b, weight_v, weight_s, scalar_sem)
    scalars[0].wait()
    fill_places(place, filled, groups, count, lambda scene: owner_s[0, scene])
    copies = gather_scenes(obs, pays, range(groups), place, groups, blocks, me, scene_sem)
    wait_all(scalars[1:] + loads)
    for step in range(groups):
        to = partner(me, step, groups)
        pays[step][CAP * 2 * blocks] = easting_block(
            to, place, slot_s, weight_s, lambda scene, part, side: edges[side * 2 + part, scene]
        )
    wait_all(copies)


def pack_kernel(count, tile, *refs):
    owner, slot, weight, ice, obs_h, vel_h, visc_h, fric_h, drive_h, to_low, to_high = refs[:11]
    ice_s, owner_v, slot_v, weight_v, obs, vel, visc, fric, drive, more_sem, load_sem = refs[11:]
    loads = copy_all([(vel_h, vel), (drive_h, drive), (visc_h, visc), (fric_h, fric), (obs_h, obs)], load_sem)
    more = copy_all([(ice, ice_s), (owner, owner_v), (slot, slot_v), (weight, weight_v)], more_sem)
    picked = lax.broadcasted_iota(jnp.int32, (8, LANE), 0)
    across = lax.broadcasted_iota(jnp.int32, (8, LANE), 1)
    cells_y = visc.shape[1]

    def pick(first, kind):
        return (across == picked + first).astype(kind)

    wait_all(loads[:4])
    for index, (at, depth) in enumerate(FIELDS[:-1]):
        for target, low, first in ((to_low, 0, 0), (to_high, cells_y - LANE, LANE - depth)):
            lanes = slice(low, low + LANE)
            if index in (VISC, FRIC):
                field = (visc if index == VISC else fric)[:, lanes]
                rows = columns_of(pick(first, F32), field, lax.Precision.HIGHEST)
            else:
                field = vel[index, :, lanes] if index in (U, V) else drive[index - DRIVE_U, :, lanes]
                rows = columns_of(pick(first, jnp.bfloat16), field, None)
            target[at : at + depth, :] = rows[0:depth]
    wait_all(more)
    for target, at in ((to_low, 0), (to_high, ice_s.shape[1] - 1)):
        target[SCENES + count :, :] = jnp.zeros((8, target.shape[1]), F32)
        for number, values in enumerate((owner_v, slot_v, weight_v)):
            target[SCENES + count + number : SCENES + count + number + 1, 0:count] = values[...].astype(F32)
        row = FIELDS[ICE][0]
        target[row : row + 1, :] = ice_line(
            [ice_s[number, at] for number in range(ice_s.shape[0])], (1, target.shape[1]), tile
        )
    loads[4].wait()
    both = (across == jnp.where(picked == 0, 0, LANE - 1)).astype(jnp.bfloat16)
    for scene in range(count):
        rows = columns_of(both, obs[scene].reshape(2 * tile, LANE), None)
        to_low[SCENES + scene : SCENES + scene + 1, :] = rows[0:1]
        to_high[SCENES + scene : SCENES + scene + 1, :] = rows[1:2]


def side_tiles(right, left, turned):
    turned[...] = jnp.zeros_like(turned)
    turned[0:PACK, :] = right[0:PACK, :]
    turned[PACK : 2 * PACK, :] = left[0:PACK, :]
    return jnp.transpose(turned[...])


def side_tile(upright, index):
    at, depth = FIELDS[index]
    lane = lax.broadcasted_iota(jnp.int32, upright.shape, 1)
    after = pltpu.roll(upright, (LANE - at) % LANE, 1)
    before = pltpu.roll(upright, LANE - depth - PACK - at, 1)
    return jnp.where(lane < depth, after, jnp.where(lane >= LANE - depth, before, 0.0))


def write_halo(pay, base, pack):
    first = FIELDS[VISC][0]
    last = FIELDS[FRIC][0] + FIELDS[FRIC][1]
    for number in range(pack.shape[1] // LANE):
        whole = pack[:, number * LANE : (number + 1) * LANE]
        high = whole.astype(jnp.bfloat16)
        rest = whole - high.astype(F32)
        middle = rest.astype(jnp.bfloat16).astype(F32)
        pay[base + 2 * number] = high
        both = jnp.concatenate([middle[first:last], (rest - middle)[first:last]], axis=0)
        fill = jnp.zeros((PACK - both.shape[0], LANE), F32)
        pay[base + 2 * number + 1] = jnp.concatenate([both, fill], axis=0).astype(jnp.bfloat16)


def read_halo(pay, base, pack, keep):
    first = FIELDS[VISC][0]
    count = FIELDS[FRIC][0] + FIELDS[FRIC][1] - first
    for number in range(pack.shape[1] // LANE):
        lanes = slice(number * LANE, (number + 1) * LANE)
        more = pay[base + 2 * number + 1].astype(F32)
        pack[:, lanes] = pay[base + 2 * number].astype(F32)
        pack[first : first + count, lanes] += more[0:count]
        pack[first : first + count, lanes] += more[count : 2 * count]
    pack[...] = jnp.where(keep, pack[...], 0.0)


def widen_kernel(groups, count, tile, *refs):
    ice, vel, visc, fric, drive, right, left = refs[:7]
    pays = refs[7 + groups : 7 + 2 * groups]
    ice_s, notes, first_b, last_b, first_f, last_f, turned, to_low, to_high, place, filled, sems = refs[7 + 2 * groups :]
    cells = visc.shape[0]
    cells_y = visc.shape[1]
    blocks = tile // PACK
    me = lax.axis_index("gx")
    tail = pl.ds(SCENES + count, 8)
    loads = copy_all(
        [
            (right.at[tail], notes.at[0]), (left.at[tail], notes.at[1]), (ice, ice_s),
            (vel.at[:, 0:16], first_b.at[0:2]), (drive.at[:, 0:16], first_b.at[2:4]),
            (vel.at[:, cells - 16 : cells], last_b.at[0:2]), (drive.at[:, cells - 16 : cells], last_b.at[2:4]),
            (visc.at[0:8], first_f.at[0]), (fric.at[0:8], first_f.at[1]),
            (visc.at[cells - 8 : cells], last_f.at[0]), (fric.at[cells - 8 : cells], last_f.at[1]),
        ],
        sems,
    )
    upright = side_tiles(right, left, turned)
    wait_all(loads)
    for index, (at, depth) in enumerate(FIELDS):
        if index == ICE:
            first, last = (
                ice_line([ice_s[number, column] for column in range(ice_s.shape[1])], (1, cells_y), tile)
                for number in (0, ice_s.shape[0] - 1)
            )
        elif index in (VISC, FRIC):
            first, last = first_f[index - VISC], last_f[index - VISC]
        else:
            number = index if index in (U, V) else index - DRIVE_U + 2
            first, last = first_b[number].astype(F32), last_b[number].astype(F32)
        to_low[at : at + depth, 0:cells_y] = first[0:depth]
        to_high[at : at + depth, 0:cells_y] = last[last.shape[0] - depth :]
        to_low[at : at + depth, cells_y:] = side_tile(upright[0:8], index)[0:depth]
        to_high[at : at + depth, cells_y:] = side_tile(upright[cells - 8 :], index)[8 - depth : 8]
    base = CAP * 2 * blocks + 2
    write_halo(pays[1], base, to_high[...])
    write_halo(pays[groups - 1], base, to_low[...])
    packs = (right, left)
    for side in range(2):
        fill_places(place.at[side], filled, groups, count, lambda scene: notes[side, 0, scene].astype(jnp.int32))
    row = lax.broadcasted_iota(jnp.int32, (PACK, LANE), 0)
    lane = lax.broadcasted_iota(jnp.int32, (PACK, LANE), 1)
    for step in range(groups):
        to = partner(me, step, groups)
        block = jnp.zeros((PACK, LANE), F32)
        for side in range(2):
            for rank in range(CAP):
                spot = place[side, (to + 1) * CAP + rank]
                scene = jnp.maximum(spot, 0)
                amount = jnp.where(spot >= 0, notes[side, 2, scene], 0.0)
                where = notes[side, 1, scene].astype(jnp.int32)
                line = packs[side][pl.ds(SCENES + scene, 1), :]
                for part in range(2):
                    block = jnp.where(
                        row == (side * CAP + rank) * 2 + part, line[:, part * LANE : (part + 1) * LANE], block
                    )
                    value = jnp.where(where == part * 2 + side, amount, 0.0)
                    block = jnp.where((row == 8) & (lane == (side * CAP + rank) * 2 + part), value, block)
                spot = place[side, (to + (0 if side == 0 else 2)) * CAP + rank]
                scene = jnp.maximum(spot, 0)
                amount = jnp.where(spot >= 0, notes[side, 2, scene], 0.0)
                where = notes[side, 1, scene].astype(jnp.int32)
                line = packs[side][pl.ds(SCENES + scene, 1), :]
                at = tile - 1 if side == 0 else 0
                base = 8 + side * 6 + rank * 3
                for part in range(2):
                    value = jnp.broadcast_to(line[:, part * LANE + at : part * LANE + at + 1], (1, LANE))
                    block = jnp.where((row == 8) & (lane == base + part), value, block)
                value = jnp.where(where == (2 if side == 0 else 1), amount, 0.0)
                block = jnp.where((row == 8) & (lane == base + 2), value, block)
        pays[step][CAP * 2 * blocks + 1] = block.astype(jnp.bfloat16)


def stress_block(u, v, visc, low, rows, wide):
    here, after = pl.ds(low, rows), pl.ds(low + 1, rows)
    vel_u, vel_v = u[here, :], v[here, :]
    a_x = u[after, :] - vel_u
    b_x = v[after, :] - vel_v
    a_y = pltpu.roll(vel_u, wide - 1, 1) - vel_u
    b_y = pltpu.roll(vel_v, wide - 1, 1) - vel_v
    nu = visc[here, :]
    return nu * (4.0 * a_x + 2.0 * b_y), nu * (4.0 * b_y + 2.0 * a_x), nu * (a_y + b_x)


def image_block(sxx, syy, sxy, low, rows):
    here, before = pl.ds(low, rows), pl.ds(low - 1, rows)
    mid = sxy[here, :]
    push_u = sxx[before, :] - sxx[here, :] + pltpu.roll(mid, 1, 1) - mid
    side = syy[here, :]
    push_v = sxy[before, :] - mid + pltpu.roll(side, 1, 1) - side
    return push_u, push_v


def sweep_kernel(groups, tile, ice, vel, visc, fric, drive, right, left, from_low, from_high, *refs):
    second, ease, lead, trail, wide_visc, wide_ice = refs[:6]
    (
        u, v, wide_fric, drive_u, drive_v, next_u, next_v, relax_u, relax_v, sxx, syy, sxy, turned,
        low_pack, high_pack, ice_s, sems,
    ) = refs[6:]
    cells, cells_y = visc.shape
    rows, wide = wide_visc.shape
    loads = copy_all([(ice, ice_s)], sems)
    upright = side_tiles(right, left, turned)
    base = CAP * 2 * (tile // PACK) + 2
    me = lax.axis_index("gx")
    read_halo(from_low, base, low_pack, me > 0)
    read_halo(from_high, base, high_pack, me < groups - 1)
    wait_all(loads)
    own_rows = slice(PAD, PAD + cells)
    for index, field in enumerate((u, v, wide_visc, wide_fric, drive_u, drive_v, wide_ice)):
        at, depth = FIELDS[index]
        field[0:PAD, :] = jnp.zeros((PAD, wide), F32)
        field[PAD + cells :, :] = jnp.zeros((PAD, wide), F32)
        if index == ICE:
            for number in range(cells // tile):
                field[PAD + number * tile : PAD + (number + 1) * tile, 0:cells_y] = ice_line(
                    [ice_s[number, column] for column in range(ice_s.shape[1])], (tile, cells_y), tile
                )
        elif index in (VISC, FRIC):
            field[own_rows, 0:cells_y] = (visc if index == VISC else fric)[...]
        else:
            source = vel if index in (U, V) else drive
            field[own_rows, 0:cells_y] = source[index % DRIVE_U].astype(F32)
        field[own_rows, cells_y:wide] = side_tile(upright, index)
        field[PAD - depth : PAD, :] = low_pack[at : at + depth, :]
        field[PAD + cells : PAD + cells + depth, :] = high_pack[at : at + depth, :]
    blocks = range(8, rows - 8, 8)
    own = range(PAD, rows - PAD, 8)
    for low in blocks:
        here = pl.ds(low, 8)
        nu, drag = wide_visc[here, :], wide_fric[here, :]
        nu_x = wide_visc[pl.ds(low - 1, 8), :]
        nu_y = pltpu.roll(nu, 1, 1)
        inside = drag > 0.0
        for out, diag in ((relax_u, 5.0 * nu + 4.0 * nu_x + nu_y), (relax_v, 5.0 * nu + nu_x + 4.0 * nu_y)):
            out[here, :] = jnp.where(inside, 1.0 / jnp.where(inside, diag + drag, 1.0), 0.0)
    for low in blocks:
        here = pl.ds(low, 8)
        sxx[here, :], syy[here, :], sxy[here, :] = stress_block(u, v, wide_visc, low, 8, wide)
    for low in blocks:
        here = pl.ds(low, 8)
        pushes = image_block(sxx, syy, sxy, low, 8)
        for part, (push, speed, force, relax, after) in enumerate(
            zip(pushes, (u, v), (drive_u, drive_v), (relax_u, relax_v), (next_u, next_v))
        ):
            now, soft = speed[here, :], relax[here, :]
            move = soft * (force[here, :] - push - wide_fric[here, :] * now)
            after[here, :] = now + OMEGA * move
            slack = OMEGA * soft
            ease[part, here, :] = slack
            if low in own:
                factor = -wide_ice[here, 0:cells_y] * (slack * (move + now))[:, 0:cells_y]
                lead[part, pl.ds(low - PAD, 8), :] = factor
    for low in blocks:
        here = pl.ds(low, 8)
        sxx[here, :], syy[here, :], sxy[here, :] = stress_block(next_u, next_v, wide_visc, low, 8, wide)
    for low in blocks:
        here = pl.ds(low, 8)
        pushes = image_block(sxx, syy, sxy, low, 8)
        for part, (push, speed, force, relax) in enumerate(
            zip(pushes, (next_u, next_v), (drive_u, drive_v), (relax_u, relax_v))
        ):
            now = speed[here, :]
            move = relax[here, :] * (force[here, :] - push - wide_fric[here, :] * now)
            second[part, here, :] = wide_ice[here, :] * (now + OMEGA * move)
            if low in own:
                mine = pl.ds(low - PAD, 8)
                trail[part, mine, :] = (
                    -wide_ice[here, 0:cells_y] * (move + now)[:, 0:cells_y]
                    - wide_fric[here, 0:cells_y] * lead[part, mine, :]
                )


def final_kernel(groups, tile, *refs):
    pays = refs[:groups]
    second, ease, lead, trail, visc, ice, grad = refs[groups : groups + 7]
    misfit, u, v, sxx, syy, sxy, table, total, rows_x, rows_y, turned = refs[groups + 7 :]
    rows, wide = visc.shape
    cells_y = wide - LANE
    cells = rows - 2 * PAD
    blocks = tile // PACK
    tiles_y = cells_y // tile
    slots = cells // tile * tiles_y
    lift = (u, v)
    for group in range(groups):
        rows_x[pl.ds(group, PACK, stride=groups), :] = pays[group][CAP * 2 * blocks].astype(F32)
        rows_y[pl.ds(group, PACK, stride=groups), :] = pays[group][CAP * 2 * blocks + 1].astype(F32)

    def raw(source, number):
        return source[number * groups : (number + 1) * groups, :]

    def spread(source, number):
        return jnp.broadcast_to(raw(source, 8)[:, number : number + 1], (groups, LANE))

    def gathered(value):
        return jnp.sum(value, axis=0, keepdims=True)

    for position in range(slots):
        weights = [spread(rows_x, rank * slots + position) for rank in range(CAP)]
        for rank in range(CAP):
            at = (rank * slots + position) * groups
            table[at : at + groups, :] = weights[rank]
        total[position : position + 1, :] = gathered(sum(weights))
    for field in lift:
        field[0:PAD, :] = jnp.zeros((PAD, wide), F32)
        field[PAD + cells :, :] = jnp.zeros((PAD, wide), F32)
    turned[...] = jnp.zeros_like(turned)
    for side in range(2):
        at = PAD + cells if side == 0 else PAD - 1
        for column in range(2):
            lanes = slice(column * tile, (column + 1) * tile)
            weights = [spread(rows_x, 8 + (side * CAP + rank) * 2 + column) for rank in range(CAP)]
            weight = gathered(sum(weights))
            for part in range(2):
                seen = gathered(sum(weights[rank] * raw(rows_x, (side * CAP + rank) * 2 + part) for rank in range(CAP)))
                gap = weight * second[part, at : at + 1, lanes] - ice[at : at + 1, lanes] * seen
                lift[part][at : at + 1, lanes] = ease[part, at : at + 1, lanes] * gap
        lines = [[None] * 2 for _ in range(3)]
        for column in range(2):
            weights = [spread(rows_y, (side * CAP + rank) * 2 + column) for rank in range(CAP)]
            lines[2][column] = gathered(sum(weights))
            for part in range(2):
                lines[part][column] = gathered(
                    sum(weights[rank] * raw(rows_y, (side * CAP + rank) * 2 + part) for rank in range(CAP))
                )
        weights = [spread(rows_y, 8 + side * 6 + rank * 3 + 2) for rank in range(CAP)]
        corners = [
            gathered(sum(weights[rank] * spread(rows_y, 8 + side * 6 + rank * 3 + part) for rank in range(CAP)))
            for part in range(2)
        ] + [gathered(sum(weights))]
        lane = lax.broadcasted_iota(jnp.int32, (1, turned.shape[1]), 1)
        for number in range(3):
            line = jnp.concatenate(
                lines[number] + [jnp.zeros((1, turned.shape[1] - 2 * tile), F32)], axis=1
            )
            line = pltpu.roll(jnp.broadcast_to(line, (8, turned.shape[1])), PAD, 1)[0:1]
            corner = jnp.concatenate([corners[number]] * (turned.shape[1] // LANE), axis=1)
            line = jnp.where(lane == (PAD - 1 if side == 0 else PAD + cells), corner, line)
            at = number if side == 0 else LANE - 1 - number
            turned[at : at + 1, :] = line
    upright = jnp.transpose(turned[...])[0:rows]
    lane = lax.broadcasted_iota(jnp.int32, (rows, LANE), 1)

    def sides(number):
        after = pltpu.roll(upright, (LANE - number) % LANE, 1)
        before = pltpu.roll(upright, number, 1)
        return jnp.where(lane == 0, after, jnp.where(lane == LANE - 1, before, 0.0))

    weight = sides(2)
    for part in range(2):
        gap = weight * second[part, :, cells_y:wide] - ice[:, cells_y:wide] * sides(part)
        lift[part][:, cells_y:wide] = ease[part, :, cells_y:wide] * gap

    def step(index, carry):
        part, chunk = index // blocks, index % blocks
        sums = [jnp.zeros((PACK, LANE), F32) for _ in range(slots)]
        for group in range(groups):
            for rank in range(CAP):
                got = pays[group][rank * 2 * blocks + index].astype(F32)
                for position in range(slots):
                    sums[position] += table[pl.ds((rank * slots + position) * groups + group, 1), :] * got
        for position in range(slots):
            lanes = slice((position % tiles_y) * tile, (position % tiles_y + 1) * tile)
            at = pl.multiple_of((position // tiles_y) * tile + chunk * PACK, PACK)
            here = pl.ds(pl.multiple_of(at + PAD, PACK), PACK)
            gap = total[position : position + 1, :] * second[part, here, lanes] - ice[here, lanes] * sums[position]
            misfit[part, pl.ds(at, PACK), lanes] = gap
            sums[position] = ease[part, here, lanes] * gap

        for number, field in enumerate(lift):

            @pl.when(part == number)
            def _():
                for position in range(slots):
                    lanes = slice((position % tiles_y) * tile, (position % tiles_y + 1) * tile)
                    at = pl.multiple_of((position // tiles_y) * tile + chunk * PACK + PAD, PACK)
                    field[pl.ds(at, PACK), lanes] = sums[position]

        return carry

    lax.fori_loop(0, 2 * blocks, step, 0)
    for low in range(8, rows - PAD, 8):
        here = pl.ds(low, 8)
        sxx[here, :], syy[here, :], sxy[here, :] = stress_block(u, v, visc, low, 8, wide)
    for low in range(PAD, rows - PAD, 8):
        mine = pl.ds(low - PAD, 8)
        here = pl.ds(low, 8)
        sums = jnp.zeros((8, cells_y), F32)
        for part, push in enumerate(image_block(sxx, syy, sxy, low, 8)):
            sums += (misfit[part, mine, :] - push[:, 0:cells_y]) * lead[part, mine, :]
            sums += lift[part][here, 0:cells_y] * trail[part, mine, :]
        grad[mine, :] = sums


def body(vel0, visc, fric, drive, scene_obs, scene_weight, scene_owner, scene_slot, ice_mask):
    cells_x, cells_y = visc.shape
    tile = scene_obs.shape[-1]
    count = scene_obs.shape[1]
    groups = lax.axis_size("gx")
    blocks = tile // PACK
    rows, wide = cells_x + 2 * PAD, cells_y + LANE
    long = -(-rows // LANE) * LANE
    obs = scene_obs.reshape(count, 2 * blocks, PACK, LANE)
    owner, slot, weight = scene_owner.reshape(1, count), scene_slot, scene_weight
    limit = pltpu.CompilerParams(vmem_limit_bytes=40 << 20)
    dma = pltpu.SemaphoreType.DMA
    def shape(*dims, dtype=F32):
        return jax.ShapeDtypeStruct(dims, dtype)

    def short(*dims):
        return pltpu.VMEM(dims, jnp.bfloat16)

    def full(*dims):
        return pltpu.VMEM(dims, F32)

    bf16, i32 = jnp.bfloat16, jnp.int32
    deep = CAP * 2 * blocks
    tall = SCENES + count + 8
    halo = 2 * (wide // LANE)
    pay_shapes = [
        pltpu.VMEM((deep + 2 + (halo if step in (1, groups - 1) else 0), PACK, LANE), bf16) for step in range(groups)
    ]
    places = [pltpu.SMEM(((groups + 2) * CAP,), i32), pltpu.SMEM((groups,), i32)]
    y_low, y_high = pl.pallas_call(
        functools.partial(pack_kernel, count, tile),
        out_shape=[pltpu.VMEM((tall, cells_x), F32)] * 2,
        in_specs=[HBM] * 9,
        out_specs=[VMEM] * 2,
        scratch_shapes=[
            pltpu.SMEM(ice_mask.shape, i32), pltpu.VMEM((1, count), i32), pltpu.VMEM((1, count), i32), short(1, count),
            short(*obs.shape), short(*vel0.shape), full(*visc.shape), full(*fric.shape), short(*drive.shape),
            dma((4,)), dma((5,)),
        ],
        compiler_params=limit,
        name="pack",
    )(*in_place(owner, slot, weight, ice_mask, obs, vel0, visc, fric, drive))
    right = from_behind(y_low, "gy", -1)
    left = from_behind(y_high, "gy", 1)
    pays = pl.pallas_call(
        functools.partial(gather_kernel, groups, count, tile),
        out_shape=pay_shapes,
        in_specs=[HBM] * 4,
        out_specs=[VMEM] * groups,
        scratch_shapes=[
            pltpu.SMEM((1, count), i32), pltpu.SMEM((1, count), i32), short(1, count), full(1, count),
            pltpu.SMEM((1, count), F32), short(4, count, PACK, LANE), *places, dma((3,)), dma((4,)),
            dma((groups * CAP,)),
        ],
        compiler_params=limit,
        name="gather",
    )(*in_place(after(owner, y_low), slot, weight, obs))
    ready = pl.pallas_call(
        functools.partial(widen_kernel, groups, count, tile),
        out_shape=pay_shapes,
        in_specs=[HBM] * 5 + [VMEM] * (2 + groups),
        out_specs=[VMEM] * groups,
        input_output_aliases={7 + step: step for step in range(groups)},
        scratch_shapes=[
            pltpu.SMEM(ice_mask.shape, i32), pltpu.SMEM((2, 8, cells_x), F32), short(4, 16, cells_y),
            short(4, 16, cells_y), full(2, 8, cells_y), full(2, 8, cells_y), full(LANE, cells_x), full(PACK, wide),
            full(PACK, wide), pltpu.SMEM((2, (groups + 2) * CAP), i32), pltpu.SMEM((groups,), i32), dma((11,)),
        ],
        compiler_params=limit,
        name="widen",
    )(*in_place(ice_mask, vel0, visc, fric, drive), right, left, *pays)
    got = [ready[0]]
    for step in range(1, groups):
        pairs = [(me, partner(me, step, groups)) for me in range(groups)]
        got.append(lax.ppermute(ready[step], "gx", pairs))
    base = pl.pallas_call(
        functools.partial(sweep_kernel, groups, tile),
        out_shape=[shape(2, rows, wide)] * 2 + [shape(2, cells_x, cells_y)] * 2 + [shape(rows, wide)] * 2,
        in_specs=[HBM] + [VMEM] * 8,
        out_specs=[VMEM] * 6,
        scratch_shapes=[full(rows, wide)] * 12
        + [full(LANE, cells_x), full(PACK, wide), full(PACK, wide), pltpu.SMEM(ice_mask.shape, i32), dma((1,))],
        compiler_params=limit,
        name="sweep",
    )(ice_mask, vel0, visc, fric, drive, right, left, got[1], got[groups - 1])
    return pl.pallas_call(
        functools.partial(final_kernel, groups, tile),
        out_shape=shape(cells_x, cells_y),
        in_specs=[VMEM] * (groups + 6),
        out_specs=VMEM,
        scratch_shapes=[full(2, cells_x, cells_y)] + [full(rows, wide)] * 5
        + [
            full(groups * CAP * 4, LANE), full(8, LANE), full(PACK * groups, LANE), full(PACK * groups, LANE),
            full(LANE, long),
        ],
        compiler_params=limit,
        name="final",
    )(*got, *base)


def solution(mesh):
    placed = (
        P(None, "gx", "gy"),
        P("gx", "gy"),
        P("gx", "gy"),
        P(None, "gx", "gy"),
        P("gy", "gx", None, None, None),
        P("gy", "gx"),
        P("gy", "gx", None),
        P("gy", "gx"),
        P("gx", "gy"),
    )
    return jax.shard_map(body, mesh=mesh, in_specs=placed, out_specs=P("gx", "gy"), check_vma=False)
```

```python
import functools

import jax
import jax.numpy as jnp
from jax import lax
from jax.experimental import pallas as pl
from jax.experimental.pallas import tpu as pltpu
from jax.sharding import PartitionSpec as P

CAP = 2
OMEGA = 0.6
LANE = 128
PAD = 16
PACK = 16
FIELDS = ((0, 3), (3, 3), (6, 3), (9, 2), (11, 2), (13, 2), (15, 1))
U, V, VISC, FRIC, DRIVE_U, DRIVE_V, ICE = range(7)
SCENES = PACK

VMEM = pl.BlockSpec(memory_space=pltpu.VMEM)
HBM = pl.BlockSpec(memory_space=pltpu.HBM)
F32 = jnp.float32


def partner(me, step):
    return me ^ step


def halo_steps(groups):
    return [step for step in range(1, groups) if step & (step + 1) == 0]


def from_behind(value, axis, steps):
    count = lax.axis_size(axis)
    first, last = (max(0, -steps), min(count, count - steps))
    return lax.ppermute(value, axis, [(source, source + steps) for source in range(first, last)])


def after(value, *others):
    return lax.optimization_barrier((value, *others))[0]


def in_place(*values):
    return [pltpu.with_memory_space_constraint(value, pltpu.HBM) for value in values]


def copy_all(pairs, sems, first=0):
    copies = [
        pltpu.make_async_copy(source, target, sems.at[first + number])
        for number, (source, target) in enumerate(pairs)
    ]
    for copy in copies:
        copy.start()
    return copies


def wait_all(copies):
    for copy in copies:
        copy.wait()


def ice_line(values, shape, tile):
    lane = lax.broadcasted_iota(jnp.int32, shape, 1)
    line = jnp.zeros(shape, F32)
    for number, value in enumerate(values):
        line = jnp.where(lane // tile == number, value.astype(F32), line)
    return line


def fill_places(place, filled, groups, count, owner_of):
    for index in range((groups + 2) * CAP):
        place[index] = -1
    for index in range(groups):
        filled[index] = 0
    for scene in range(count):
        who = owner_of(scene)
        rank = filled[who]
        place[(who + 1) * CAP + rank] = scene
        filled[who] = rank + 1


def columns_of(pick, block, precision):
    return lax.dot_general(
        pick, block, (((1,), (1,)), ((), ())), precision=precision, preferred_element_type=F32
    )


def load_scalars(owner, slot, weight, owner_s, slot_s, weight_b, weight_v, weight_s, sems):
    loads = copy_all([(owner, owner_s), (slot, slot_s), (weight, weight_b)], sems)
    loads[2].wait()
    weight_v[...] = weight_b[...].astype(F32)
    loads[2] = pltpu.make_async_copy(weight_v, weight_s, sems.at[2])
    loads[2].start()
    return loads


def easting_block(to, place, slot_s, weight_s, edge):
    row = lax.broadcasted_iota(jnp.int32, (PACK, LANE), 0)
    lane = lax.broadcasted_iota(jnp.int32, (PACK, LANE), 1)
    block = jnp.zeros((PACK, LANE), F32)
    for side in range(2):
        for rank in range(CAP):
            spot = place[(to + (2 if side == 0 else 0)) * CAP + rank]
            scene = jnp.maximum(spot, 0)
            amount = jnp.where(spot >= 0, weight_s[0, scene], 0.0)
            where = slot_s[0, scene]
            for part in range(2):
                line = edge(scene, part, side).astype(F32)
                line = line[0:1] if side == 0 else line[PACK - 1 : PACK]
                block = jnp.where(row == (side * CAP + rank) * 2 + part, line, block)
                value = jnp.where(where == side * 2 + part, amount, 0.0)
                block = jnp.where((row == 8) & (lane == 8 + (side * CAP + rank) * 2 + part), value, block)
    for rank in range(CAP):
        spot = place[(to + 1) * CAP + rank]
        scene = jnp.maximum(spot, 0)
        amount = jnp.where(spot >= 0, weight_s[0, scene], 0.0)
        for position in range(4):
            value = jnp.where(slot_s[0, scene] == position, amount, 0.0)
            block = jnp.where((row == 8) & (lane == rank * 4 + position), value, block)
    return block.astype(jnp.bfloat16)


def gather_scenes(obs, pays, steps, place, groups, blocks, me, sems):
    copies = []
    for number, step in enumerate(steps):
        to = partner(me, step)
        for rank in range(CAP):
            scene = jnp.maximum(place[(to + 1) * CAP + rank], 0)
            target = pays[number].at[pl.ds(rank * 2 * blocks, 2 * blocks)]
            copies += copy_all([(obs.at[scene], target)], sems, number * CAP + rank)
    return copies


def gather_kernel(groups, count, tile, *refs):
    owner, slot, weight, obs = refs[:4]
    pays = refs[4 : 4 + groups]
    owner_s, slot_s, weight_b, weight_v, weight_s, edges, place, filled, scalar_sem, edge_sem, scene_sem = refs[
        4 + groups :
    ]
    blocks = tile // PACK
    me = lax.axis_index("gx")
    loads = copy_all(
        [(obs.at[:, at], edges.at[number]) for number, at in enumerate((0, blocks, blocks - 1, 2 * blocks - 1))], edge_sem
    )
    scalars = load_scalars(owner, slot, weight, owner_s, slot_s, weight_b, weight_v, weight_s, scalar_sem)
    scalars[0].wait()
    fill_places(place, filled, groups, count, lambda scene: owner_s[0, scene])
    copies = gather_scenes(obs, pays, range(groups), place, groups, blocks, me, scene_sem)
    wait_all(scalars[1:] + loads)
    for step in range(groups):
        to = partner(me, step)
        pays[step][CAP * 2 * blocks] = easting_block(
            to, place, slot_s, weight_s, lambda scene, part, side: edges[side * 2 + part, scene]
        )
    wait_all(copies)


def pack_kernel(count, tile, *refs):
    owner, slot, weight, ice, obs_h, vel_h, visc_h, fric_h, drive_h, to_low, to_high = refs[:11]
    ice_s, owner_v, slot_v, weight_v, obs, vel, visc, fric, drive, more_sem, load_sem = refs[11:]
    loads = copy_all([(vel_h, vel), (drive_h, drive), (visc_h, visc), (fric_h, fric), (obs_h, obs)], load_sem)
    more = copy_all([(ice, ice_s), (owner, owner_v), (slot, slot_v), (weight, weight_v)], more_sem)
    picked = lax.broadcasted_iota(jnp.int32, (8, LANE), 0)
    across = lax.broadcasted_iota(jnp.int32, (8, LANE), 1)
    cells_y = visc.shape[1]

    def pick(first, kind):
        return (across == picked + first).astype(kind)

    wait_all(loads[:4])
    for index, (at, depth) in enumerate(FIELDS[:-1]):
        for target, low, first in ((to_low, 0, 0), (to_high, cells_y - LANE, LANE - depth)):
            lanes = slice(low, low + LANE)
            if index in (VISC, FRIC):
                field = (visc if index == VISC else fric)[:, lanes]
                rows = columns_of(pick(first, F32), field, lax.Precision.HIGHEST)
            else:
                field = vel[index, :, lanes] if index in (U, V) else drive[index - DRIVE_U, :, lanes]
                rows = columns_of(pick(first, jnp.bfloat16), field, None)
            target[at : at + depth, :] = rows[0:depth]
    wait_all(more)
    for target, at in ((to_low, 0), (to_high, ice_s.shape[1] - 1)):
        target[SCENES + count :, :] = jnp.zeros((8, target.shape[1]), F32)
        for number, values in enumerate((owner_v, slot_v, weight_v)):
            target[SCENES + count + number : SCENES + count + number + 1, 0:count] = values[...].astype(F32)
        row = FIELDS[ICE][0]
        target[row : row + 1, :] = ice_line(
            [ice_s[number, at] for number in range(ice_s.shape[0])], (1, target.shape[1]), tile
        )
    loads[4].wait()
    both = (across == jnp.where(picked == 0, 0, LANE - 1)).astype(jnp.bfloat16)
    for scene in range(count):
        rows = columns_of(both, obs[scene].reshape(2 * tile, LANE), None)
        to_low[SCENES + scene : SCENES + scene + 1, :] = rows[0:1]
        to_high[SCENES + scene : SCENES + scene + 1, :] = rows[1:2]


def side_tiles(right, left, turned):
    turned[...] = jnp.zeros_like(turned)
    turned[0:PACK, :] = right[0:PACK, :]
    turned[PACK : 2 * PACK, :] = left[0:PACK, :]
    return jnp.transpose(turned[...])


def side_tile(upright, index):
    at, depth = FIELDS[index]
    lane = lax.broadcasted_iota(jnp.int32, upright.shape, 1)
    after = pltpu.roll(upright, (LANE - at) % LANE, 1)
    before = pltpu.roll(upright, LANE - depth - PACK - at, 1)
    return jnp.where(lane < depth, after, jnp.where(lane >= LANE - depth, before, 0.0))


def write_halo(pay, base, pack):
    first = FIELDS[VISC][0]
    last = FIELDS[FRIC][0] + FIELDS[FRIC][1]
    for number in range(pack.shape[1] // LANE):
        whole = pack[:, number * LANE : (number + 1) * LANE]
        high = whole.astype(jnp.bfloat16)
        rest = whole - high.astype(F32)
        middle = rest.astype(jnp.bfloat16).astype(F32)
        pay[base + 2 * number] = high
        both = jnp.concatenate([middle[first:last], (rest - middle)[first:last]], axis=0)
        fill = jnp.zeros((PACK - both.shape[0], LANE), F32)
        pay[base + 2 * number + 1] = jnp.concatenate([both, fill], axis=0).astype(jnp.bfloat16)


def read_halo(pays, base, pack, me, beside):
    first = FIELDS[VISC][0]
    count = FIELDS[FRIC][0] + FIELDS[FRIC][1] - first
    for number in range(pack.shape[1] // LANE):
        lanes = slice(number * LANE, (number + 1) * LANE)
        high, more = jnp.zeros((PACK, LANE), F32), jnp.zeros((PACK, LANE), F32)
        for step, pay in pays.items():
            here = partner(me, step) == beside
            high = jnp.where(here, pay[base + 2 * number].astype(F32), high)
            more = jnp.where(here, pay[base + 2 * number + 1].astype(F32), more)
        pack[:, lanes] = high
        pack[first : first + count, lanes] += more[0:count]
        pack[first : first + count, lanes] += more[count : 2 * count]


def widen_kernel(groups, count, tile, early, late, *refs):
    ice, vel, visc, fric, drive, right, left = refs[:7]
    pays = dict(zip(late, refs[7 + len(late) :]))
    refs = refs[7 + 2 * len(late) :]
    apart = dict(zip(early, refs))
    ice_s, notes, first_b, last_b, first_f, last_f, turned, to_low, to_high, place, filled, sems = refs[len(early) :]
    cells = visc.shape[0]
    cells_y = visc.shape[1]
    blocks = tile // PACK
    me = lax.axis_index("gx")
    tail = pl.ds(SCENES + count, 8)
    loads = copy_all(
        [
            (right.at[tail], notes.at[0]), (left.at[tail], notes.at[1]), (ice, ice_s),
            (vel.at[:, 0:16], first_b.at[0:2]), (drive.at[:, 0:16], first_b.at[2:4]),
            (vel.at[:, cells - 16 : cells], last_b.at[0:2]), (drive.at[:, cells - 16 : cells], last_b.at[2:4]),
            (visc.at[0:8], first_f.at[0]), (fric.at[0:8], first_f.at[1]),
            (visc.at[cells - 8 : cells], last_f.at[0]), (fric.at[cells - 8 : cells], last_f.at[1]),
        ],
        sems,
    )
    upright = side_tiles(right, left, turned)
    wait_all(loads)
    for index, (at, depth) in enumerate(FIELDS):
        if index == ICE:
            first, last = (
                ice_line([ice_s[number, column] for column in range(ice_s.shape[1])], (1, cells_y), tile)
                for number in (0, ice_s.shape[0] - 1)
            )
        elif index in (VISC, FRIC):
            first, last = first_f[index - VISC], last_f[index - VISC]
        else:
            number = index if index in (U, V) else index - DRIVE_U + 2
            first, last = first_b[number].astype(F32), last_b[number].astype(F32)
        to_low[at : at + depth, 0:cells_y] = first[0:depth]
        to_high[at : at + depth, 0:cells_y] = last[last.shape[0] - depth :]
        to_low[at : at + depth, cells_y:] = side_tile(upright[0:8], index)[0:depth]
        to_high[at : at + depth, cells_y:] = side_tile(upright[cells - 8 :], index)[8 - depth : 8]
    base = CAP * 2 * blocks + 2
    for step in halo_steps(groups):
        write_halo(pays[step], base, jnp.where(partner(me, step) > me, to_high[...], to_low[...]))
    packs = (right, left)
    for side in range(2):
        fill_places(place.at[side], filled, groups, count, lambda scene: notes[side, 0, scene].astype(jnp.int32))
    row = lax.broadcasted_iota(jnp.int32, (PACK, LANE), 0)
    lane = lax.broadcasted_iota(jnp.int32, (PACK, LANE), 1)
    for step in range(groups):
        to = partner(me, step)
        block = jnp.zeros((PACK, LANE), F32)
        for side in range(2):
            for rank in range(CAP):
                spot = place[side, (to + 1) * CAP + rank]
                scene = jnp.maximum(spot, 0)
                amount = jnp.where(spot >= 0, notes[side, 2, scene], 0.0)
                where = notes[side, 1, scene].astype(jnp.int32)
                line = packs[side][pl.ds(SCENES + scene, 1), :]
                for part in range(2):
                    block = jnp.where(
                        row == (side * CAP + rank) * 2 + part, line[:, part * LANE : (part + 1) * LANE], block
                    )
                    value = jnp.where(where == part * 2 + side, amount, 0.0)
                    block = jnp.where((row == 8) & (lane == (side * CAP + rank) * 2 + part), value, block)
                spot = place[side, (to + (0 if side == 0 else 2)) * CAP + rank]
                scene = jnp.maximum(spot, 0)
                amount = jnp.where(spot >= 0, notes[side, 2, scene], 0.0)
                where = notes[side, 1, scene].astype(jnp.int32)
                line = packs[side][pl.ds(SCENES + scene, 1), :]
                at = tile - 1 if side == 0 else 0
                base = 8 + side * 6 + rank * 3
                for part in range(2):
                    value = jnp.broadcast_to(line[:, part * LANE + at : part * LANE + at + 1], (1, LANE))
                    block = jnp.where((row == 8) & (lane == base + part), value, block)
                value = jnp.where(where == (2 if side == 0 else 1), amount, 0.0)
                block = jnp.where((row == 8) & (lane == base + 2), value, block)
        if step in early:
            apart[step][0] = block.astype(jnp.bfloat16)
        else:
            pays[step][CAP * 2 * blocks + 1] = block.astype(jnp.bfloat16)


def stress_block(u, v, visc, low, rows, wide):
    here, after = pl.ds(low, rows), pl.ds(low + 1, rows)
    vel_u, vel_v = u[here, :], v[here, :]
    a_x = u[after, :] - vel_u
    b_x = v[after, :] - vel_v
    a_y = pltpu.roll(vel_u, wide - 1, 1) - vel_u
    b_y = pltpu.roll(vel_v, wide - 1, 1) - vel_v
    nu = visc[here, :]
    return nu * (4.0 * a_x + 2.0 * b_y), nu * (4.0 * b_y + 2.0 * a_x), nu * (a_y + b_x)


def image_block(sxx, syy, sxy, low, rows):
    here, before = pl.ds(low, rows), pl.ds(low - 1, rows)
    mid = sxy[here, :]
    push_u = sxx[before, :] - sxx[here, :] + pltpu.roll(mid, 1, 1) - mid
    side = syy[here, :]
    push_v = sxy[before, :] - mid + pltpu.roll(side, 1, 1) - side
    return push_u, push_v


def sweep_kernel(groups, tile, ice, vel, visc, fric, drive, right, left, *refs):
    steps = halo_steps(groups)
    pays = dict(zip(steps, refs))
    refs = refs[len(steps) :]
    second, ease, lead, trail, wide_visc, wide_ice = refs[:6]
    (
        u, v, wide_fric, drive_u, drive_v, next_u, next_v, relax_u, relax_v, sxx, syy, sxy, turned,
        low_pack, high_pack, ice_s, sems,
    ) = refs[6:]
    cells, cells_y = visc.shape
    rows, wide = wide_visc.shape
    loads = copy_all([(ice, ice_s)], sems)
    upright = side_tiles(right, left, turned)
    base = CAP * 2 * (tile // PACK) + 2
    me = lax.axis_index("gx")
    read_halo(pays, base, low_pack, me, me - 1)
    read_halo(pays, base, high_pack, me, me + 1)
    wait_all(loads)
    own_rows = slice(PAD, PAD + cells)
    for index, field in enumerate((u, v, wide_visc, wide_fric, drive_u, drive_v, wide_ice)):
        at, depth = FIELDS[index]
        field[0:PAD, :] = jnp.zeros((PAD, wide), F32)
        field[PAD + cells :, :] = jnp.zeros((PAD, wide), F32)
        if index == ICE:
            for number in range(cells // tile):
                field[PAD + number * tile : PAD + (number + 1) * tile, 0:cells_y] = ice_line(
                    [ice_s[number, column] for column in range(ice_s.shape[1])], (tile, cells_y), tile
                )
        elif index in (VISC, FRIC):
            field[own_rows, 0:cells_y] = (visc if index == VISC else fric)[...]
        else:
            source = vel if index in (U, V) else drive
            field[own_rows, 0:cells_y] = source[index % DRIVE_U].astype(F32)
        field[own_rows, cells_y:wide] = side_tile(upright, index)
        field[PAD - depth : PAD, :] = low_pack[at : at + depth, :]
        field[PAD + cells : PAD + cells + depth, :] = high_pack[at : at + depth, :]
    blocks = range(8, rows - 8, 8)
    own = range(PAD, rows - PAD, 8)
    for low in blocks:
        here = pl.ds(low, 8)
        nu, drag = wide_visc[here, :], wide_fric[here, :]
        nu_x = wide_visc[pl.ds(low - 1, 8), :]
        nu_y = pltpu.roll(nu, 1, 1)
        inside = drag > 0.0
        for out, diag in ((relax_u, 5.0 * nu + 4.0 * nu_x + nu_y), (relax_v, 5.0 * nu + nu_x + 4.0 * nu_y)):
            out[here, :] = jnp.where(inside, 1.0 / jnp.where(inside, diag + drag, 1.0), 0.0)
    for low in blocks:
        here = pl.ds(low, 8)
        sxx[here, :], syy[here, :], sxy[here, :] = stress_block(u, v, wide_visc, low, 8, wide)
    for low in blocks:
        here = pl.ds(low, 8)
        pushes = image_block(sxx, syy, sxy, low, 8)
        for part, (push, speed, force, relax, after) in enumerate(
            zip(pushes, (u, v), (drive_u, drive_v), (relax_u, relax_v), (next_u, next_v))
        ):
            now, soft = speed[here, :], relax[here, :]
            move = soft * (force[here, :] - push - wide_fric[here, :] * now)
            after[here, :] = now + OMEGA * move
            slack = OMEGA * soft
            ease[part, here, :] = slack
            if low in own:
                factor = -wide_ice[here, 0:cells_y] * (slack * (move + now))[:, 0:cells_y]
                lead[part, pl.ds(low - PAD, 8), :] = factor
    for low in blocks:
        here = pl.ds(low, 8)
        sxx[here, :], syy[here, :], sxy[here, :] = stress_block(next_u, next_v, wide_visc, low, 8, wide)
    for low in blocks:
        here = pl.ds(low, 8)
        pushes = image_block(sxx, syy, sxy, low, 8)
        for part, (push, speed, force, relax) in enumerate(
            zip(pushes, (next_u, next_v), (drive_u, drive_v), (relax_u, relax_v))
        ):
            now = speed[here, :]
            move = relax[here, :] * (force[here, :] - push - wide_fric[here, :] * now)
            second[part, here, :] = wide_ice[here, :] * (now + OMEGA * move)
            if low in own:
                mine = pl.ds(low - PAD, 8)
                trail[part, mine, :] = (
                    -wide_ice[here, 0:cells_y] * (move + now)[:, 0:cells_y]
                    - wide_fric[here, 0:cells_y] * lead[part, mine, :]
                )


def final_kernel(groups, tile, early, *refs):
    pays = refs[:groups]
    apart = dict(zip(early, refs[groups:]))
    refs = refs[len(early) :]
    second, ease, lead, trail, visc, ice, grad = refs[groups : groups + 7]
    misfit, u, v, sxx, syy, sxy, table, total, rows_x, rows_y, turned = refs[groups + 7 :]
    rows, wide = visc.shape
    cells_y = wide - LANE
    cells = rows - 2 * PAD
    blocks = tile // PACK
    tiles_y = cells_y // tile
    slots = cells // tile * tiles_y
    lift = (u, v)
    for group in range(groups):
        rows_x[pl.ds(group, PACK, stride=groups), :] = pays[group][CAP * 2 * blocks].astype(F32)
        side = apart[group][0] if group in early else pays[group][CAP * 2 * blocks + 1]
        rows_y[pl.ds(group, PACK, stride=groups), :] = side.astype(F32)

    def raw(source, number):
        return source[number * groups : (number + 1) * groups, :]

    def spread(source, number):
        return jnp.broadcast_to(raw(source, 8)[:, number : number + 1], (groups, LANE))

    def gathered(value):
        return jnp.sum(value, axis=0, keepdims=True)

    for position in range(slots):
        weights = [spread(rows_x, rank * slots + position) for rank in range(CAP)]
        for rank in range(CAP):
            at = (rank * slots + position) * groups
            table[at : at + groups, :] = weights[rank]
        total[position : position + 1, :] = gathered(sum(weights))
    for field in lift:
        field[0:PAD, :] = jnp.zeros((PAD, wide), F32)
        field[PAD + cells :, :] = jnp.zeros((PAD, wide), F32)
    turned[...] = jnp.zeros_like(turned)
    for side in range(2):
        at = PAD + cells if side == 0 else PAD - 1
        for column in range(2):
            lanes = slice(column * tile, (column + 1) * tile)
            weights = [spread(rows_x, 8 + (side * CAP + rank) * 2 + column) for rank in range(CAP)]
            weight = gathered(sum(weights))
            for part in range(2):
                seen = gathered(sum(weights[rank] * raw(rows_x, (side * CAP + rank) * 2 + part) for rank in range(CAP)))
                gap = weight * second[part, at : at + 1, lanes] - ice[at : at + 1, lanes] * seen
                lift[part][at : at + 1, lanes] = ease[part, at : at + 1, lanes] * gap
        lines = [[None] * 2 for _ in range(3)]
        for column in range(2):
            weights = [spread(rows_y, (side * CAP + rank) * 2 + column) for rank in range(CAP)]
            lines[2][column] = gathered(sum(weights))
            for part in range(2):
                lines[part][column] = gathered(
                    sum(weights[rank] * raw(rows_y, (side * CAP + rank) * 2 + part) for rank in range(CAP))
                )
        weights = [spread(rows_y, 8 + side * 6 + rank * 3 + 2) for rank in range(CAP)]
        corners = [
            gathered(sum(weights[rank] * spread(rows_y, 8 + side * 6 + rank * 3 + part) for rank in range(CAP)))
            for part in range(2)
        ] + [gathered(sum(weights))]
        lane = lax.broadcasted_iota(jnp.int32, (1, turned.shape[1]), 1)
        for number in range(3):
            line = jnp.concatenate(
                lines[number] + [jnp.zeros((1, turned.shape[1] - 2 * tile), F32)], axis=1
            )
            line = pltpu.roll(jnp.broadcast_to(line, (8, turned.shape[1])), PAD, 1)[0:1]
            corner = jnp.concatenate([corners[number]] * (turned.shape[1] // LANE), axis=1)
            line = jnp.where(lane == (PAD - 1 if side == 0 else PAD + cells), corner, line)
            at = number if side == 0 else LANE - 1 - number
            turned[at : at + 1, :] = line
    upright = jnp.transpose(turned[...])[0:rows]
    lane = lax.broadcasted_iota(jnp.int32, (rows, LANE), 1)

    def sides(number):
        after = pltpu.roll(upright, (LANE - number) % LANE, 1)
        before = pltpu.roll(upright, number, 1)
        return jnp.where(lane == 0, after, jnp.where(lane == LANE - 1, before, 0.0))

    weight = sides(2)
    for part in range(2):
        gap = weight * second[part, :, cells_y:wide] - ice[:, cells_y:wide] * sides(part)
        lift[part][:, cells_y:wide] = ease[part, :, cells_y:wide] * gap

    def step(index, carry):
        part, chunk = index // blocks, index % blocks
        sums = [jnp.zeros((PACK, LANE), F32) for _ in range(slots)]
        for group in range(groups):
            for rank in range(CAP):
                got = pays[group][rank * 2 * blocks + index].astype(F32)
                for position in range(slots):
                    sums[position] += table[pl.ds((rank * slots + position) * groups + group, 1), :] * got
        for position in range(slots):
            lanes = slice((position % tiles_y) * tile, (position % tiles_y + 1) * tile)
            at = pl.multiple_of((position // tiles_y) * tile + chunk * PACK, PACK)
            here = pl.ds(pl.multiple_of(at + PAD, PACK), PACK)
            gap = total[position : position + 1, :] * second[part, here, lanes] - ice[here, lanes] * sums[position]
            misfit[part, pl.ds(at, PACK), lanes] = gap
            sums[position] = ease[part, here, lanes] * gap

        for number, field in enumerate(lift):

            @pl.when(part == number)
            def _():
                for position in range(slots):
                    lanes = slice((position % tiles_y) * tile, (position % tiles_y + 1) * tile)
                    at = pl.multiple_of((position // tiles_y) * tile + chunk * PACK + PAD, PACK)
                    field[pl.ds(at, PACK), lanes] = sums[position]

        return carry

    lax.fori_loop(0, 2 * blocks, step, 0)
    for low in range(8, rows - PAD, 8):
        here = pl.ds(low, 8)
        sxx[here, :], syy[here, :], sxy[here, :] = stress_block(u, v, visc, low, 8, wide)
    for low in range(PAD, rows - PAD, 8):
        mine = pl.ds(low - PAD, 8)
        here = pl.ds(low, 8)
        sums = jnp.zeros((8, cells_y), F32)
        for part, push in enumerate(image_block(sxx, syy, sxy, low, 8)):
            sums += (misfit[part, mine, :] - push[:, 0:cells_y]) * lead[part, mine, :]
            sums += lift[part][here, 0:cells_y] * trail[part, mine, :]
        grad[mine, :] = sums


def body(vel0, visc, fric, drive, scene_obs, scene_weight, scene_owner, scene_slot, ice_mask):
    cells_x, cells_y = visc.shape
    tile = scene_obs.shape[-1]
    count = scene_obs.shape[1]
    groups = lax.axis_size("gx")
    blocks = tile // PACK
    rows, wide = cells_x + 2 * PAD, cells_y + LANE
    long = -(-rows // LANE) * LANE
    obs = scene_obs.reshape(count, 2 * blocks, PACK, LANE)
    owner, slot, weight = scene_owner.reshape(1, count), scene_slot, scene_weight
    limit = pltpu.CompilerParams(vmem_limit_bytes=40 << 20)
    dma = pltpu.SemaphoreType.DMA
    def shape(*dims, dtype=F32):
        return jax.ShapeDtypeStruct(dims, dtype)

    def short(*dims):
        return pltpu.VMEM(dims, jnp.bfloat16)

    def full(*dims):
        return pltpu.VMEM(dims, F32)

    bf16, i32 = jnp.bfloat16, jnp.int32
    deep = CAP * 2 * blocks
    tall = SCENES + count + 8
    half = groups // 2
    early = (half, half + 1)
    late = tuple(step for step in range(groups) if step not in early)
    halo = 2 * (wide // LANE)

    def pay(step):
        more = 0 if step in early else 1 + (halo if step in halo_steps(groups) else 0)
        return pltpu.VMEM((deep + 1 + more, PACK, LANE), bf16)

    def move(step, value, *others):
        pairs = [(me, partner(me, step)) for me in range(groups)]
        return lax.ppermute(after(value, *others) if others else value, "gx", pairs)

    places = [pltpu.SMEM(((groups + 2) * CAP,), i32), pltpu.SMEM((groups,), i32)]
    pays = pl.pallas_call(
        functools.partial(gather_kernel, groups, count, tile),
        out_shape=[pay(step) for step in range(groups)],
        in_specs=[HBM] * 4,
        out_specs=[VMEM] * groups,
        scratch_shapes=[
            pltpu.SMEM((1, count), i32), pltpu.SMEM((1, count), i32), short(1, count), full(1, count),
            pltpu.SMEM((1, count), F32), short(4, count, PACK, LANE), *places, dma((3,)), dma((4,)),
            dma((groups * CAP,)),
        ],
        compiler_params=limit,
        name="gather",
    )(*in_place(owner, slot, weight, obs))
    got = [pays[0]] * groups
    for step in early:
        got[step] = move(step, pays[step])
    y_low, y_high = pl.pallas_call(
        functools.partial(pack_kernel, count, tile),
        out_shape=[pltpu.VMEM((tall, cells_x), F32)] * 2,
        in_specs=[HBM] * 9,
        out_specs=[VMEM] * 2,
        scratch_shapes=[
            pltpu.SMEM(ice_mask.shape, i32), pltpu.VMEM((1, count), i32), pltpu.VMEM((1, count), i32), short(1, count),
            short(*obs.shape), short(*vel0.shape), full(*visc.shape), full(*fric.shape), short(*drive.shape),
            dma((4,)), dma((5,)),
        ],
        compiler_params=limit,
        name="pack",
    )(*in_place(after(owner, pays[half]), slot, weight, ice_mask, obs, vel0, visc, fric, drive))
    right = from_behind(y_low, "gy", -1)
    left = from_behind(y_high, "gy", 1)
    outs = pl.pallas_call(
        functools.partial(widen_kernel, groups, count, tile, early, late),
        out_shape=[pay(step) for step in late] + [pltpu.VMEM((1, PACK, LANE), bf16)] * len(early),
        in_specs=[HBM] * 5 + [VMEM] * (2 + len(late)),
        out_specs=[VMEM] * groups,
        input_output_aliases={7 + number: number for number in range(len(late))},
        scratch_shapes=[
            pltpu.SMEM(ice_mask.shape, i32), pltpu.SMEM((2, 8, cells_x), F32), short(4, 16, cells_y),
            short(4, 16, cells_y), full(2, 8, cells_y), full(2, 8, cells_y), full(LANE, cells_x), full(PACK, wide),
            full(PACK, wide), pltpu.SMEM((2, (groups + 2) * CAP), i32), pltpu.SMEM((groups,), i32), dma((11,)),
        ],
        compiler_params=limit,
        name="widen",
    )(*in_place(ice_mask, vel0, visc, fric, drive), after(right, got[half]), left, *(pays[step] for step in late))
    ready = dict(zip(late, outs))
    got[0] = ready[0]
    order = [groups - 1, 1, *range(half + 2, groups - 1), half - 1, *(step for step in range(2, half - 1))]
    waits = {half + 2: half + 1}
    for step in order:
        got[step] = move(step, ready[step], *([got[waits[step]]] if step in waits else []))
    apart = [
        move(step, value, got[wait]) for step, value, wait in zip(early, outs[len(late) :], (1, half - 1))
    ]
    base = pl.pallas_call(
        functools.partial(sweep_kernel, groups, tile),
        out_shape=[shape(2, rows, wide)] * 2 + [shape(2, cells_x, cells_y)] * 2 + [shape(rows, wide)] * 2,
        in_specs=[HBM] + [VMEM] * (6 + len(halo_steps(groups))),
        out_specs=[VMEM] * 6,
        scratch_shapes=[full(rows, wide)] * 12
        + [full(LANE, cells_x), full(PACK, wide), full(PACK, wide), pltpu.SMEM(ice_mask.shape, i32), dma((1,))],
        compiler_params=limit,
        name="sweep",
    )(ice_mask, vel0, visc, fric, drive, right, left, *(got[step] for step in halo_steps(groups)))
    return pl.pallas_call(
        functools.partial(final_kernel, groups, tile, early),
        out_shape=shape(cells_x, cells_y),
        in_specs=[VMEM] * (groups + len(early) + 6),
        out_specs=VMEM,
        scratch_shapes=[full(2, cells_x, cells_y)] + [full(rows, wide)] * 5
        + [
            full(groups * CAP * 4, LANE), full(8, LANE), full(PACK * groups, LANE), full(PACK * groups, LANE),
            full(LANE, long),
        ],
        compiler_params=limit,
        name="final",
    )(*got, *apart, *base)


def solution(mesh):
    placed = (
        P(None, "gx", "gy"),
        P("gx", "gy"),
        P("gx", "gy"),
        P(None, "gx", "gy"),
        P("gy", "gx", None, None, None),
        P("gy", "gx"),
        P("gy", "gx", None),
        P("gy", "gx"),
        P("gx", "gy"),
    )
    return jax.shard_map(body, mesh=mesh, in_specs=placed, out_specs=P("gx", "gy"), check_vma=False)
```

```python
import functools

import jax
import jax.numpy as jnp
from jax import lax
from jax.experimental import pallas as pl
from jax.experimental.pallas import tpu as pltpu
from jax.sharding import PartitionSpec as P

CAP = 2
OMEGA = 0.6
LANE = 128
PAD = 16
PACK = 16
FIELDS = ((0, 3), (3, 3), (6, 3), (9, 2), (11, 2), (13, 2), (15, 1))
U, V, VISC, FRIC, DRIVE_U, DRIVE_V, ICE = range(7)

VMEM = pl.BlockSpec(memory_space=pltpu.VMEM)
HBM = pl.BlockSpec(memory_space=pltpu.HBM)
F32 = jnp.float32


def partner(me, step):
    return me ^ step


def halo_steps(groups):
    return [step for step in range(1, groups) if step & (step + 1) == 0]


def after(value, *others):
    return lax.optimization_barrier((value, *others))[0]


def in_place(*values):
    return [pltpu.with_memory_space_constraint(value, pltpu.HBM) for value in values]


def swap(even, odd):
    count = lax.axis_size("gy")
    near = [(me, me ^ 1) for me in range(count)]
    far = [(me, me + 1 if me % 2 else me - 1) for me in range(1, count - 1)]
    return lax.ppermute(even, "gy", near), lax.ppermute(odd, "gy", far)


def both_sides(first, second):
    even = lax.rem(lax.axis_index("gy"), 2) == 0
    return jnp.where(even, first, second), jnp.where(even, second, first)


def copy_all(pairs, sems, first=0):
    copies = [
        pltpu.make_async_copy(source, target, sems.at[first + number])
        for number, (source, target) in enumerate(pairs)
    ]
    for copy in copies:
        copy.start()
    return copies


def wait_all(copies):
    for copy in copies:
        copy.wait()


def ice_line(values, shape, tile):
    lane = lax.broadcasted_iota(jnp.int32, shape, 1)
    line = jnp.zeros(shape, F32)
    for number, value in enumerate(values):
        line = jnp.where(lane // tile == number, value.astype(F32), line)
    return line


def fill_places(place, filled, groups, count, owner_of):
    for index in range((groups + 2) * CAP):
        place[index] = -1
    for index in range(groups):
        filled[index] = 0
    for scene in range(count):
        who = owner_of(scene)
        rank = filled[who]
        place[(who + 1) * CAP + rank] = scene
        filled[who] = rank + 1


def columns_of(pick, block, precision):
    return lax.dot_general(
        pick, block, (((1,), (1,)), ((), ())), precision=precision, preferred_element_type=F32
    )


def load_scalars(owner, slot, weight, owner_s, slot_s, weight_b, weight_v, weight_s, sems):
    loads = copy_all([(owner, owner_s), (slot, slot_s), (weight, weight_b)], sems)
    loads[2].wait()
    weight_v[...] = weight_b[...].astype(F32)
    loads[2] = pltpu.make_async_copy(weight_v, weight_s, sems.at[2])
    loads[2].start()
    return loads


def easting_block(to, place, slot_s, weight_s, edge):
    row = lax.broadcasted_iota(jnp.int32, (PACK, LANE), 0)
    lane = lax.broadcasted_iota(jnp.int32, (PACK, LANE), 1)
    block = jnp.zeros((PACK, LANE), F32)
    for side in range(2):
        for rank in range(CAP):
            spot = place[(to + (2 if side == 0 else 0)) * CAP + rank]
            scene = jnp.maximum(spot, 0)
            amount = jnp.where(spot >= 0, weight_s[0, scene], 0.0)
            where = slot_s[0, scene]
            for part in range(2):
                line = edge(scene, part, side).astype(F32)
                line = line[0:1] if side == 0 else line[PACK - 1 : PACK]
                block = jnp.where(row == (side * CAP + rank) * 2 + part, line, block)
                value = jnp.where(where == side * 2 + part, amount, 0.0)
                block = jnp.where((row == 8) & (lane == 8 + (side * CAP + rank) * 2 + part), value, block)
    for rank in range(CAP):
        spot = place[(to + 1) * CAP + rank]
        scene = jnp.maximum(spot, 0)
        amount = jnp.where(spot >= 0, weight_s[0, scene], 0.0)
        for position in range(4):
            value = jnp.where(slot_s[0, scene] == position, amount, 0.0)
            block = jnp.where((row == 8) & (lane == rank * 4 + position), value, block)
    return block.astype(jnp.bfloat16)


def gather_scenes(obs, pays, steps, place, groups, blocks, me, sems):
    copies = []
    for number, step in enumerate(steps):
        to = partner(me, step)
        for rank in range(CAP):
            scene = jnp.maximum(place[(to + 1) * CAP + rank], 0)
            target = pays[number].at[pl.ds(rank * 2 * blocks, 2 * blocks)]
            copies += copy_all([(obs.at[scene], target)], sems, number * CAP + rank)
    return copies


def gather_kernel(groups, count, tile, *refs):
    owner, slot, weight, obs = refs[:4]
    pays = refs[4 : 4 + groups]
    owner_s, slot_s, weight_b, weight_v, weight_s, edges, place, filled, scalar_sem, edge_sem, scene_sem = refs[
        4 + groups :
    ]
    blocks = tile // PACK
    me = lax.axis_index("gx")
    loads = copy_all(
        [(obs.at[:, at], edges.at[number]) for number, at in enumerate((0, blocks, blocks - 1, 2 * blocks - 1))], edge_sem
    )
    scalars = load_scalars(owner, slot, weight, owner_s, slot_s, weight_b, weight_v, weight_s, scalar_sem)
    scalars[0].wait()
    fill_places(place, filled, groups, count, lambda scene: owner_s[0, scene])
    copies = gather_scenes(obs, pays, range(groups), place, groups, blocks, me, scene_sem)
    wait_all(scalars[1:] + loads)
    for step in range(groups):
        to = partner(me, step)
        pays[step][CAP * 2 * blocks] = easting_block(
            to, place, slot_s, weight_s, lambda scene, part, side: edges[side * 2 + part, scene]
        )
    wait_all(copies)


def northing_block(side, to, place, slot_s, weight_s, lines, tile):
    row = lax.broadcasted_iota(jnp.int32, (8, LANE), 0)
    lane = lax.broadcasted_iota(jnp.int32, (8, LANE), 1)
    block = jnp.zeros((8, LANE), F32)
    for rank in range(CAP):
        spot = place[(to + 1) * CAP + rank]
        scene = jnp.maximum(spot, 0)
        amount = jnp.where(spot >= 0, weight_s[0, scene], 0.0)
        where = slot_s[0, scene]
        line = lines[pl.ds(scene, 1), :]
        for part in range(2):
            block = jnp.where(row == rank * 2 + part, line[:, part * LANE : (part + 1) * LANE], block)
            value = jnp.where(where == part * 2 + side, amount, 0.0)
            block = jnp.where((row == 4) & (lane == rank * 2 + part), value, block)
        spot = place[(to + (0 if side == 0 else 2)) * CAP + rank]
        scene = jnp.maximum(spot, 0)
        amount = jnp.where(spot >= 0, weight_s[0, scene], 0.0)
        line = lines[pl.ds(scene, 1), :]
        at = tile - 1 if side == 0 else 0
        base = 8 + rank * 3
        for part in range(2):
            value = jnp.broadcast_to(line[:, part * LANE + at : part * LANE + at + 1], (1, LANE))
            block = jnp.where((row == 4) & (lane == base + part), value, block)
        value = jnp.where(slot_s[0, scene] == (2 if side == 0 else 1), amount, 0.0)
        block = jnp.where((row == 4) & (lane == base + 2), value, block)
    return block


def pack_kernel(groups, count, tile, *refs):
    owner, slot, weight, ice, obs_h, vel_h, visc_h, fric_h, drive_h, first, second, edge = refs[:12]
    (
        owner_s, slot_s, weight_b, weight_v, weight_s, ice_s, obs, vel, visc, fric, drive, to_low, to_high, lines,
        place, filled, scalar_sem, more_sem, load_sem,
    ) = refs[12:]
    loads = copy_all([(vel_h, vel), (drive_h, drive), (visc_h, visc), (fric_h, fric), (obs_h, obs)], load_sem)
    more = copy_all([(ice, ice_s)], more_sem)
    scalars = load_scalars(owner, slot, weight, owner_s, slot_s, weight_b, weight_v, weight_s, scalar_sem)
    picked = lax.broadcasted_iota(jnp.int32, (8, LANE), 0)
    across = lax.broadcasted_iota(jnp.int32, (8, LANE), 1)
    cells, cells_y = visc.shape
    scalars[0].wait()
    fill_places(place, filled, groups, count, lambda scene: owner_s[0, scene])

    def pick(start, kind):
        return (across == picked + start).astype(kind)

    wait_all(loads[:4] + more)
    for index, (at, depth) in enumerate(FIELDS):
        if index == ICE:
            for target, column in ((to_low, 0), (to_high, ice_s.shape[1] - 1)):
                target[at : at + 1, :] = ice_line([ice_s[row, column] for row in range(ice_s.shape[0])], (1, cells), tile)
            for number, row in enumerate((0, ice_s.shape[0] - 1)):
                edge[number, at : at + 1, :] = ice_line(
                    [ice_s[row, column] for column in range(ice_s.shape[1])], (1, cells_y), tile
                )
            continue
        field = {VISC: visc, FRIC: fric}.get(index)
        if field is None:
            field = vel.at[index] if index in (U, V) else drive.at[index - DRIVE_U]
        precise = index in (VISC, FRIC)
        for target, low, start in ((to_low, 0, 0), (to_high, cells_y - LANE, LANE - depth)):
            rows = columns_of(
                pick(start, F32 if precise else jnp.bfloat16), field[:, low : low + LANE],
                lax.Precision.HIGHEST if precise else None,
            )
            target[at : at + depth, :] = rows[0:depth]
        edge[0, at : at + depth, :] = field[0:16, :].astype(F32)[0:depth]
        edge[1, at : at + depth, :] = field[cells - 16 : cells, :].astype(F32)[16 - depth : 16]
    loads[4].wait()
    both = (across == jnp.where(picked == 0, 0, LANE - 1)).astype(jnp.bfloat16)
    for scene in range(count):
        rows = columns_of(both, obs[scene].reshape(2 * tile, LANE), None)
        lines[0, scene : scene + 1, :] = rows[0:1]
        lines[1, scene : scene + 1, :] = rows[1:2]
    wait_all(scalars[1:])
    half = groups // 2
    for side, target in enumerate((to_low, to_high)):
        for to in range(groups):
            at = PACK + to % half * 8
            lanes = slice(to // half * LANE, (to // half + 1) * LANE)
            target[at : at + 8, lanes] = northing_block(side, to, place, slot_s, weight_s, lines.at[side], tile)
    even = lax.rem(lax.axis_index("gy"), 2) == 0
    first[...] = jnp.where(even, to_high[...], to_low[...])
    second[...] = jnp.where(even, to_low[...], to_high[...])


def side_tiles(right, left, turned):
    turned[...] = jnp.zeros_like(turned)
    turned[0:PACK, :] = right
    turned[PACK : 2 * PACK, :] = left
    return jnp.transpose(turned[...])


def side_tile(upright, index):
    at, depth = FIELDS[index]
    lane = lax.broadcasted_iota(jnp.int32, upright.shape, 1)
    after = pltpu.roll(upright, (LANE - at) % LANE, 1)
    before = pltpu.roll(upright, LANE - depth - PACK - at, 1)
    return jnp.where(lane < depth, after, jnp.where(lane >= LANE - depth, before, 0.0))


def write_halo(pay, base, pack):
    first = FIELDS[VISC][0]
    last = FIELDS[FRIC][0] + FIELDS[FRIC][1]
    for number in range(pack.shape[1] // LANE):
        whole = pack[:, number * LANE : (number + 1) * LANE]
        high = whole.astype(jnp.bfloat16)
        rest = whole - high.astype(F32)
        middle = rest.astype(jnp.bfloat16).astype(F32)
        pay[base + 2 * number] = high
        both = jnp.concatenate([middle[first:last], (rest - middle)[first:last]], axis=0)
        fill = jnp.zeros((PACK - both.shape[0], LANE), F32)
        pay[base + 2 * number + 1] = jnp.concatenate([both, fill], axis=0).astype(jnp.bfloat16)


def read_halo(pays, base, pack, me, beside):
    first = FIELDS[VISC][0]
    count = FIELDS[FRIC][0] + FIELDS[FRIC][1] - first
    for number in range(pack.shape[1] // LANE):
        lanes = slice(number * LANE, (number + 1) * LANE)
        high, more = jnp.zeros((PACK, LANE), F32), jnp.zeros((PACK, LANE), F32)
        for step, pay in pays.items():
            here = partner(me, step) == beside
            high = jnp.where(here, pay[base + 2 * number].astype(F32), high)
            more = jnp.where(here, pay[base + 2 * number + 1].astype(F32), more)
        pack[:, lanes] = high
        pack[first : first + count, lanes] += more[0:count]
        pack[first : first + count, lanes] += more[count : 2 * count]


def widen_kernel(groups, tile, early, late, *refs):
    first, second, edge = refs[:3]
    pays = dict(zip(late, refs[3 + len(late) :]))
    refs = refs[3 + 2 * len(late) :]
    apart = dict(zip(early, refs))
    turned, to_low, to_high = refs[len(early) :]
    cells_y = edge.shape[2]
    blocks = tile // PACK
    me = lax.axis_index("gx")
    half = groups // 2
    for step in late + early:
        to = partner(me, step)
        here = pl.ds(pl.multiple_of(PACK + lax.rem(to, half) * 8, 8), 8)
        sides = both_sides(first[here, :], second[here, :])
        block = jnp.concatenate([jnp.where(to < half, side[:, 0:LANE], side[:, LANE:]) for side in sides], axis=0)
        if step in early:
            apart[step][0] = block.astype(jnp.bfloat16)
        else:
            pays[step][CAP * 2 * blocks + 1] = block.astype(jnp.bfloat16)
    upright = side_tiles(*both_sides(first[0:PACK, :], second[0:PACK, :]), turned)
    cells = upright.shape[0]
    to_low[:, 0:cells_y] = edge[0]
    to_high[:, 0:cells_y] = edge[1]
    for index, (at, depth) in enumerate(FIELDS):
        to_low[at : at + depth, cells_y:] = side_tile(upright[0:8], index)[0:depth]
        to_high[at : at + depth, cells_y:] = side_tile(upright[cells - 8 :], index)[8 - depth : 8]
    base = CAP * 2 * blocks + 2
    for step in halo_steps(groups):
        write_halo(pays[step], base, jnp.where(partner(me, step) > me, to_high[...], to_low[...]))


def stress_block(u, v, visc, low, rows, wide):
    here, after = pl.ds(low, rows), pl.ds(low + 1, rows)
    vel_u, vel_v = u[here, :], v[here, :]
    a_x = u[after, :] - vel_u
    b_x = v[after, :] - vel_v
    a_y = pltpu.roll(vel_u, wide - 1, 1) - vel_u
    b_y = pltpu.roll(vel_v, wide - 1, 1) - vel_v
    nu = visc[here, :]
    return nu * (4.0 * a_x + 2.0 * b_y), nu * (4.0 * b_y + 2.0 * a_x), nu * (a_y + b_x)


def image_block(sxx, syy, sxy, low, rows):
    here, before = pl.ds(low, rows), pl.ds(low - 1, rows)
    mid = sxy[here, :]
    push_u = sxx[before, :] - sxx[here, :] + pltpu.roll(mid, 1, 1) - mid
    side = syy[here, :]
    push_v = sxy[before, :] - mid + pltpu.roll(side, 1, 1) - side
    return push_u, push_v


def relaxation(fields, work, wide, cells_y, spans, outs, shift, own_of):
    u, v, visc, fric, drive_u, drive_v, ice = fields
    next_u, next_v, relax_u, relax_v, sxx, syy, sxy = work
    second, ease, lead, trail = outs
    for low in spans[0]:
        here = pl.ds(low, 8)
        nu, drag = visc[here, :], fric[here, :]
        nu_x = visc[pl.ds(low - 1, 8), :]
        nu_y = pltpu.roll(nu, 1, 1)
        inside = drag > 0.0
        for out, diag in ((relax_u, 5.0 * nu + 4.0 * nu_x + nu_y), (relax_v, 5.0 * nu + nu_x + 4.0 * nu_y)):
            out[here, :] = jnp.where(inside, 1.0 / jnp.where(inside, diag + drag, 1.0), 0.0)
    for low in spans[1]:
        here = pl.ds(low, 8)
        sxx[here, :], syy[here, :], sxy[here, :] = stress_block(u, v, visc, low, 8, wide)
    for low in spans[2]:
        here, there = pl.ds(low, 8), pl.ds(low + shift, 8)
        pushes = image_block(sxx, syy, sxy, low, 8)
        for part, (push, speed, force, relax, then) in enumerate(
            zip(pushes, (u, v), (drive_u, drive_v), (relax_u, relax_v), (next_u, next_v))
        ):
            now, soft = speed[here, :], relax[here, :]
            move = soft * (force[here, :] - push - fric[here, :] * now)
            then[here, :] = now + OMEGA * move
            if low in spans[4]:
                slack = OMEGA * soft
                ease[part, there, :] = slack
                if own_of(low) is not None:
                    factor = -ice[here, 0:cells_y] * (slack * (move + now))[:, 0:cells_y]
                    lead[part, pl.ds(own_of(low), 8), :] = factor
    for low in spans[3]:
        here = pl.ds(low, 8)
        sxx[here, :], syy[here, :], sxy[here, :] = stress_block(next_u, next_v, visc, low, 8, wide)
    for low in spans[4]:
        here, there = pl.ds(low, 8), pl.ds(low + shift, 8)
        pushes = image_block(sxx, syy, sxy, low, 8)
        for part, (push, speed, force, relax) in enumerate(
            zip(pushes, (next_u, next_v), (drive_u, drive_v), (relax_u, relax_v))
        ):
            now = speed[here, :]
            move = relax[here, :] * (force[here, :] - push - fric[here, :] * now)
            second[part, there, :] = ice[here, :] * (now + OMEGA * move)
            if own_of(low) is not None:
                mine = pl.ds(own_of(low), 8)
                trail[part, mine, :] = (
                    -ice[here, 0:cells_y] * (move + now)[:, 0:cells_y] - fric[here, 0:cells_y] * lead[part, mine, :]
                )


STRIP = 32


def sweep_kernel(tile, ice, vel, visc, fric, drive, first, then, *refs):
    second, ease, lead, trail, wide_visc, wide_ice, strips = refs[:7]
    u, v, wide_fric, drive_u, drive_v = refs[7:12]
    work = refs[12:19]
    turned, ice_s, sems = refs[19:]
    cells, cells_y = visc.shape
    rows, wide = wide_visc.shape
    loads = copy_all([(ice, ice_s)], sems)
    upright = side_tiles(*both_sides(first[0:PACK, :], then[0:PACK, :]), turned)
    wait_all(loads)
    own_rows = slice(PAD, PAD + cells)
    fields = (u, v, wide_visc, wide_fric, drive_u, drive_v, wide_ice)
    for index, field in enumerate(fields):
        field[0:PAD, :] = jnp.zeros((PAD, wide), F32)
        field[PAD + cells :, :] = jnp.zeros((PAD, wide), F32)
        if index == ICE:
            for number in range(cells // tile):
                field[PAD + number * tile : PAD + (number + 1) * tile, 0:cells_y] = ice_line(
                    [ice_s[number, column] for column in range(ice_s.shape[1])], (tile, cells_y), tile
                )
        elif index in (VISC, FRIC):
            field[own_rows, 0:cells_y] = (visc if index == VISC else fric)[...]
        else:
            source = vel if index in (U, V) else drive
            field[own_rows, 0:cells_y] = source[index % DRIVE_U].astype(F32)
        field[own_rows, cells_y:wide] = side_tile(upright, index)
        strips[index, 0] = field[8 : 8 + STRIP, :]
        strips[index, 1] = field[rows - 8 - STRIP : rows - 8, :]
    blocks = range(8, rows - 8, 8)
    relaxation(
        fields, work, wide, cells_y, [blocks] * 5, (second, ease, lead, trail), 0,
        lambda low: low - PAD if PAD <= low < PAD + cells else None,
    )


def trim_kernel(groups, tile, *refs):
    steps = halo_steps(groups)
    pays = dict(zip(steps, refs))
    strips = refs[len(steps)]
    second, ease, lead, trail, visc, ice = refs[len(steps) + 7 : len(steps) + 13]
    refs = refs[len(steps) + 13 :]
    fields, work, pack = refs[:7], refs[7:14], refs[14]
    rows, wide = visc.shape
    cells_y = wide - LANE
    cells = rows - 2 * PAD
    base = CAP * 2 * (tile // PACK) + 2
    me = lax.axis_index("gx")
    spans = (
        [(8, 16, 24), (8, 16, 24), (8, 16, 24), (8, 16), (8, 16)],
        [(16, 24, 32), (8, 16, 24, 32), (16, 24, 32), (16, 24, 32), (24, 32)],
    )
    for strip in range(2):
        read_halo(pays, base, pack, me, me - 1 if strip == 0 else me + 1)
        shift = 0 if strip == 0 else rows - 16 - STRIP
        edge = PAD if strip == 0 else PAD + cells - shift
        for index, field in enumerate(fields):
            at, depth = FIELDS[index]
            field[8 : 8 + STRIP, :] = strips[index, strip]
            target = slice(edge - depth, edge) if strip == 0 else slice(edge, edge + depth)
            field[target, :] = pack[at : at + depth, :]
            if index in (VISC, ICE):
                (visc if index == VISC else ice)[target.start + shift : target.stop + shift, :] = pack[at : at + depth, :]
        own = {0: (16, 0), 1: (24, cells - 8)}[strip]
        relaxation(
            fields, work, wide, cells_y, spans[strip], (second, ease, lead, trail), shift,
            lambda low, own=own: own[1] if low == own[0] else None,
        )


def final_kernel(groups, tile, early, *refs):
    pays = refs[:groups]
    apart = dict(zip(early, refs[groups:]))
    refs = refs[len(early) :]
    second, ease, lead, trail, visc, ice, grad = refs[groups : groups + 7]
    misfit, u, v, sxx, syy, sxy, table, total, rows_x, rows_y, turned = refs[groups + 7 :]
    rows, wide = visc.shape
    cells_y = wide - LANE
    cells = rows - 2 * PAD
    blocks = tile // PACK
    tiles_y = cells_y // tile
    slots = cells // tile * tiles_y
    lift = (u, v)
    for group in range(groups):
        rows_x[pl.ds(group, PACK, stride=groups), :] = pays[group][CAP * 2 * blocks].astype(F32)
        side = apart[group][0] if group in early else pays[group][CAP * 2 * blocks + 1]
        rows_y[pl.ds(group, PACK, stride=groups), :] = side.astype(F32)

    def raw(source, number):
        return source[number * groups : (number + 1) * groups, :]

    def spread(source, number, row=8):
        return jnp.broadcast_to(raw(source, row)[:, number : number + 1], (groups, LANE))

    def gathered(value):
        return jnp.sum(value, axis=0, keepdims=True)

    for position in range(slots):
        weights = [spread(rows_x, rank * slots + position) for rank in range(CAP)]
        for rank in range(CAP):
            at = (rank * slots + position) * groups
            table[at : at + groups, :] = weights[rank]
        total[position : position + 1, :] = gathered(sum(weights))
    for field in lift:
        field[0:PAD, :] = jnp.zeros((PAD, wide), F32)
        field[PAD + cells :, :] = jnp.zeros((PAD, wide), F32)
    turned[...] = jnp.zeros_like(turned)
    for side in range(2):
        at = PAD + cells if side == 0 else PAD - 1
        for column in range(2):
            lanes = slice(column * tile, (column + 1) * tile)
            weights = [spread(rows_x, 8 + (side * CAP + rank) * 2 + column) for rank in range(CAP)]
            weight = gathered(sum(weights))
            for part in range(2):
                seen = gathered(sum(weights[rank] * raw(rows_x, (side * CAP + rank) * 2 + part) for rank in range(CAP)))
                gap = weight * second[part, at : at + 1, lanes] - ice[at : at + 1, lanes] * seen
                lift[part][at : at + 1, lanes] = ease[part, at : at + 1, lanes] * gap
        lines = [[None] * 2 for _ in range(3)]
        for column in range(2):
            weights = [spread(rows_y, rank * 2 + column, side * 8 + 4) for rank in range(CAP)]
            lines[2][column] = gathered(sum(weights))
            for part in range(2):
                lines[part][column] = gathered(
                    sum(weights[rank] * raw(rows_y, side * 8 + rank * 2 + part) for rank in range(CAP))
                )
        weights = [spread(rows_y, 8 + rank * 3 + 2, side * 8 + 4) for rank in range(CAP)]
        corners = [
            gathered(sum(weights[rank] * spread(rows_y, 8 + rank * 3 + part, side * 8 + 4) for rank in range(CAP)))
            for part in range(2)
        ] + [gathered(sum(weights))]
        lane = lax.broadcasted_iota(jnp.int32, (1, turned.shape[1]), 1)
        for number in range(3):
            line = jnp.concatenate(
                lines[number] + [jnp.zeros((1, turned.shape[1] - 2 * tile), F32)], axis=1
            )
            line = pltpu.roll(jnp.broadcast_to(line, (8, turned.shape[1])), PAD, 1)[0:1]
            corner = jnp.concatenate([corners[number]] * (turned.shape[1] // LANE), axis=1)
            line = jnp.where(lane == (PAD - 1 if side == 0 else PAD + cells), corner, line)
            at = number if side == 0 else LANE - 1 - number
            turned[at : at + 1, :] = line
    upright = jnp.transpose(turned[...])[0:rows]
    lane = lax.broadcasted_iota(jnp.int32, (rows, LANE), 1)

    def sides(number):
        after = pltpu.roll(upright, (LANE - number) % LANE, 1)
        before = pltpu.roll(upright, number, 1)
        return jnp.where(lane == 0, after, jnp.where(lane == LANE - 1, before, 0.0))

    weight = sides(2)
    for part in range(2):
        gap = weight * second[part, :, cells_y:wide] - ice[:, cells_y:wide] * sides(part)
        lift[part][:, cells_y:wide] = ease[part, :, cells_y:wide] * gap

    def step(index, carry):
        part, chunk = index // blocks, index % blocks
        sums = [jnp.zeros((PACK, LANE), F32) for _ in range(slots)]
        for group in range(groups):
            for rank in range(CAP):
                got = pays[group][rank * 2 * blocks + index].astype(F32)
                for position in range(slots):
                    sums[position] += table[pl.ds((rank * slots + position) * groups + group, 1), :] * got
        for position in range(slots):
            lanes = slice((position % tiles_y) * tile, (position % tiles_y + 1) * tile)
            at = pl.multiple_of((position // tiles_y) * tile + chunk * PACK, PACK)
            here = pl.ds(pl.multiple_of(at + PAD, PACK), PACK)
            gap = total[position : position + 1, :] * second[part, here, lanes] - ice[here, lanes] * sums[position]
            misfit[part, pl.ds(at, PACK), lanes] = gap
            sums[position] = ease[part, here, lanes] * gap

        for number, field in enumerate(lift):

            @pl.when(part == number)
            def _():
                for position in range(slots):
                    lanes = slice((position % tiles_y) * tile, (position % tiles_y + 1) * tile)
                    at = pl.multiple_of((position // tiles_y) * tile + chunk * PACK + PAD, PACK)
                    field[pl.ds(at, PACK), lanes] = sums[position]

        return carry

    lax.fori_loop(0, 2 * blocks, step, 0)
    for low in range(8, rows - PAD, 8):
        here = pl.ds(low, 8)
        sxx[here, :], syy[here, :], sxy[here, :] = stress_block(u, v, visc, low, 8, wide)
    for low in range(PAD, rows - PAD, 8):
        mine = pl.ds(low - PAD, 8)
        here = pl.ds(low, 8)
        sums = jnp.zeros((8, cells_y), F32)
        for part, push in enumerate(image_block(sxx, syy, sxy, low, 8)):
            sums += (misfit[part, mine, :] - push[:, 0:cells_y]) * lead[part, mine, :]
            sums += lift[part][here, 0:cells_y] * trail[part, mine, :]
        grad[mine, :] = sums


def body(vel0, visc, fric, drive, scene_obs, scene_weight, scene_owner, scene_slot, ice_mask):
    cells_x, cells_y = visc.shape
    tile = scene_obs.shape[-1]
    count = scene_obs.shape[1]
    groups = lax.axis_size("gx")
    blocks = tile // PACK
    rows, wide = cells_x + 2 * PAD, cells_y + LANE
    long = -(-rows // LANE) * LANE
    obs = scene_obs.reshape(count, 2 * blocks, PACK, LANE)
    owner, slot, weight = scene_owner.reshape(1, count), scene_slot, scene_weight
    limit = pltpu.CompilerParams(vmem_limit_bytes=40 << 20)
    dma = pltpu.SemaphoreType.DMA
    def shape(*dims, dtype=F32):
        return jax.ShapeDtypeStruct(dims, dtype)

    def short(*dims):
        return pltpu.VMEM(dims, jnp.bfloat16)

    def full(*dims):
        return pltpu.VMEM(dims, F32)

    bf16, i32 = jnp.bfloat16, jnp.int32
    deep = CAP * 2 * blocks
    tall = PACK + groups // 2 * 8
    half = groups // 2
    early = (half, half + 1)
    late = tuple(step for step in range(groups) if step not in early)
    halo = 2 * (wide // LANE)

    def pay(step):
        more = 0 if step in early else 1 + (halo if step in halo_steps(groups) else 0)
        return pltpu.VMEM((deep + 1 + more, PACK, LANE), bf16)

    def move(step, value, *others):
        pairs = [(me, partner(me, step)) for me in range(groups)]
        return lax.ppermute(after(value, *others) if others else value, "gx", pairs)

    scalars = [
        pltpu.SMEM((1, count), i32), pltpu.SMEM((1, count), i32), short(1, count), full(1, count),
        pltpu.SMEM((1, count), F32),
    ]
    places = [pltpu.SMEM(((groups + 2) * CAP,), i32), pltpu.SMEM((groups,), i32)]
    pays = pl.pallas_call(
        functools.partial(gather_kernel, groups, count, tile),
        out_shape=[pay(step) for step in range(groups)],
        in_specs=[HBM] * 4,
        out_specs=[VMEM] * groups,
        scratch_shapes=[
            *scalars, short(4, count, PACK, LANE), *places, dma((3,)), dma((4,)),
            dma((groups * CAP,)),
        ],
        compiler_params=limit,
        name="gather",
    )(*in_place(owner, slot, weight, obs))
    got = [pays[0]] * groups
    for step in early:
        got[step] = move(step, pays[step])
    *north, edge = pl.pallas_call(
        functools.partial(pack_kernel, groups, count, tile),
        out_shape=[pltpu.VMEM((tall, cells_x), F32)] * 2 + [pltpu.VMEM((2, PACK, cells_y), F32)],
        in_specs=[HBM] * 9,
        out_specs=[VMEM] * 3,
        scratch_shapes=scalars + [
            pltpu.SMEM(ice_mask.shape, i32), short(*obs.shape), short(*vel0.shape), full(*visc.shape),
            full(*fric.shape), short(*drive.shape), full(tall, cells_x), full(tall, cells_x), full(2, count, cells_x),
            *places, dma((3,)), dma((1,)), dma((5,)),
        ],
        compiler_params=limit,
        name="pack",
    )(*in_place(after(owner, pays[half]), slot, weight, ice_mask, obs, vel0, visc, fric, drive))
    first, second = swap(*north)
    outs = pl.pallas_call(
        functools.partial(widen_kernel, groups, tile, early, late),
        out_shape=[pay(step) for step in late] + [pltpu.VMEM((1, PACK, LANE), bf16)] * len(early),
        in_specs=[VMEM] * (3 + len(late)),
        out_specs=[VMEM] * groups,
        input_output_aliases={3 + number: number for number in range(len(late))},
        scratch_shapes=[full(LANE, cells_x), full(PACK, wide), full(PACK, wide)],
        compiler_params=limit,
        name="widen",
    )(first, second, edge, *(pays[step] for step in late))
    ready = dict(zip(late, outs))
    got[0] = ready[0]
    order = [groups - 1, 1, *range(half + 2, groups - 1), half - 1, *range(2, half - 1)]
    waits = {half + 2: half, 2: half + 1}
    for step in order:
        got[step] = move(step, ready[step], *([got[waits[step]]] if step in waits else []))
    strip = shape(len(FIELDS), 2, STRIP, wide)
    base_shapes = [shape(2, rows, wide)] * 2 + [shape(2, cells_x, cells_y)] * 2 + [shape(rows, wide)] * 2
    *base, strips = pl.pallas_call(
        functools.partial(sweep_kernel, tile),
        out_shape=base_shapes + [strip],
        in_specs=[HBM] + [VMEM] * 6,
        out_specs=[VMEM] * 7,
        scratch_shapes=[full(rows, wide)] * 12 + [full(LANE, cells_x), pltpu.SMEM(ice_mask.shape, i32), dma((1,))],
        compiler_params=limit,
        name="sweep",
    )(ice_mask, vel0, visc, fric, drive, after(first, got[half + 1]), second)
    apart = [move(step, value, strips) for step, value in zip(early, outs[len(late) :])]
    near = [got[step] for step in halo_steps(groups)]
    base = pl.pallas_call(
        functools.partial(trim_kernel, groups, tile),
        out_shape=base_shapes,
        in_specs=[VMEM] * (len(near) + 7),
        out_specs=[VMEM] * 6,
        input_output_aliases={len(near) + 1 + number: number for number in range(6)},
        scratch_shapes=[full(STRIP + 16, wide)] * 14 + [full(PACK, wide)],
        compiler_params=limit,
        name="trim",
    )(*near, strips, *base)
    return pl.pallas_call(
        functools.partial(final_kernel, groups, tile, early),
        out_shape=shape(cells_x, cells_y),
        in_specs=[VMEM] * (groups + len(early) + 6),
        out_specs=VMEM,
        scratch_shapes=[full(2, cells_x, cells_y)] + [full(rows, wide)] * 5
        + [
            full(groups * CAP * 4, LANE), full(8, LANE), full(PACK * groups, LANE), full(PACK * groups, LANE),
            full(LANE, long),
        ],
        compiler_params=limit,
        name="final",
    )(*got, *apart, *base)


def solution(mesh):
    placed = (
        P(None, "gx", "gy"),
        P("gx", "gy"),
        P("gx", "gy"),
        P(None, "gx", "gy"),
        P("gy", "gx", None, None, None),
        P("gy", "gx"),
        P("gy", "gx", None),
        P("gy", "gx"),
        P("gx", "gy"),
    )
    return jax.shard_map(body, mesh=mesh, in_specs=placed, out_specs=P("gx", "gy"), check_vma=False)
```

```python
import functools

import jax
import jax.numpy as jnp
from jax import lax
from jax.experimental import pallas as pl
from jax.experimental.pallas import tpu as pltpu
from jax.sharding import PartitionSpec as P

CAP = 2
OMEGA = 0.6
LANE = 128
PAD = 16
PACK = 16
FIELDS = ((0, 3), (3, 3), (6, 3), (9, 2), (11, 2), (13, 2), (15, 1))
U, V, VISC, FRIC, DRIVE_U, DRIVE_V, ICE = range(7)

VMEM = pl.BlockSpec(memory_space=pltpu.VMEM)
HBM = pl.BlockSpec(memory_space=pltpu.HBM)
F32 = jnp.float32


def partner(me, step):
    return me ^ step


def halo_steps(groups):
    return [step for step in range(1, groups) if step & (step + 1) == 0]


def after(value, *others):
    return lax.optimization_barrier((value, *others))[0]


def in_place(*values):
    return [pltpu.with_memory_space_constraint(value, pltpu.HBM) for value in values]


def swap(even, odd):
    count = lax.axis_size("gy")
    near = [(me, me ^ 1) for me in range(count)]
    far = [(me, me + 1 if me % 2 else me - 1) for me in range(1, count - 1)]
    return lax.ppermute(even, "gy", near), lax.ppermute(odd, "gy", far)


def both_sides(first, second):
    even = lax.rem(lax.axis_index("gy"), 2) == 0
    return jnp.where(even, first, second), jnp.where(even, second, first)


def copy_all(pairs, sems, first=0):
    copies = [
        pltpu.make_async_copy(source, target, sems.at[first + number])
        for number, (source, target) in enumerate(pairs)
    ]
    for copy in copies:
        copy.start()
    return copies


def wait_all(copies):
    for copy in copies:
        copy.wait()


def ice_line(values, shape, tile):
    lane = lax.broadcasted_iota(jnp.int32, shape, 1)
    line = jnp.zeros(shape, F32)
    for number, value in enumerate(values):
        line = jnp.where(lane // tile == number, value.astype(F32), line)
    return line


def fill_places(place, filled, groups, count, owner_of):
    for index in range((groups + 2) * CAP):
        place[index] = -1
    for index in range(groups):
        filled[index] = 0
    for scene in range(count):
        who = owner_of(scene)
        rank = filled[who]
        place[(who + 1) * CAP + rank] = scene
        filled[who] = rank + 1


def split(value):
    high = value.astype(jnp.bfloat16)
    rest = value - high.astype(F32)
    middle = rest.astype(jnp.bfloat16)
    return high, middle, (rest - middle.astype(F32)).astype(jnp.bfloat16)


def columns_of(pick, block):
    return lax.dot_general(pick, block, (((1,), (1,)), ((), ())), preferred_element_type=F32)


def load_scalars(owner, slot, weight, owner_s, slot_s, weight_b, weight_v, weight_s, sems):
    loads = copy_all([(owner, owner_s), (slot, slot_s), (weight, weight_b)], sems)
    loads[2].wait()
    weight_v[...] = weight_b[...].astype(F32)
    loads[2] = pltpu.make_async_copy(weight_v, weight_s, sems.at[2])
    loads[2].start()
    return loads


def easting_block(to, place, slot_s, weight_s, edge):
    row = lax.broadcasted_iota(jnp.int32, (PACK, LANE), 0)
    lane = lax.broadcasted_iota(jnp.int32, (PACK, LANE), 1)
    block = jnp.zeros((PACK, LANE), F32)
    for side in range(2):
        for rank in range(CAP):
            spot = place[(to + (2 if side == 0 else 0)) * CAP + rank]
            scene = jnp.maximum(spot, 0)
            amount = jnp.where(spot >= 0, weight_s[0, scene], 0.0)
            where = slot_s[0, scene]
            for part in range(2):
                line = edge(scene, part, side).astype(F32)
                line = line[0:1] if side == 0 else line[PACK - 1 : PACK]
                block = jnp.where(row == (side * CAP + rank) * 2 + part, line, block)
                value = jnp.where(where == side * 2 + part, amount, 0.0)
                block = jnp.where((row == 8) & (lane == 8 + (side * CAP + rank) * 2 + part), value, block)
    for rank in range(CAP):
        spot = place[(to + 1) * CAP + rank]
        scene = jnp.maximum(spot, 0)
        amount = jnp.where(spot >= 0, weight_s[0, scene], 0.0)
        for position in range(4):
            value = jnp.where(slot_s[0, scene] == position, amount, 0.0)
            block = jnp.where((row == 8) & (lane == rank * 4 + position), value, block)
    return block.astype(jnp.bfloat16)


def gather_scenes(obs, pays, steps, place, groups, blocks, me, sems):
    copies = []
    for number, step in enumerate(steps):
        to = partner(me, step)
        for rank in range(CAP):
            scene = jnp.maximum(place[(to + 1) * CAP + rank], 0)
            target = pays[number].at[pl.ds(rank * 2 * blocks, 2 * blocks)]
            copies += copy_all([(obs.at[scene], target)], sems, number * CAP + rank)
    return copies


def gather_kernel(groups, count, tile, *refs):
    owner, slot, weight, obs = refs[:4]
    pays = refs[4 : 4 + groups]
    owner_s, slot_s, weight_b, weight_v, weight_s, edges, place, filled, scalar_sem, edge_sem, scene_sem = refs[
        4 + groups :
    ]
    blocks = tile // PACK
    me = lax.axis_index("gx")
    loads = copy_all(
        [(obs.at[:, at], edges.at[number]) for number, at in enumerate((0, blocks, blocks - 1, 2 * blocks - 1))], edge_sem
    )
    scalars = load_scalars(owner, slot, weight, owner_s, slot_s, weight_b, weight_v, weight_s, scalar_sem)
    scalars[0].wait()
    fill_places(place, filled, groups, count, lambda scene: owner_s[0, scene])
    copies = gather_scenes(obs, pays, range(groups), place, groups, blocks, me, scene_sem)
    wait_all(scalars[1:] + loads)
    for step in range(groups):
        to = partner(me, step)
        pays[step][CAP * 2 * blocks] = easting_block(
            to, place, slot_s, weight_s, lambda scene, part, side: edges[side * 2 + part, scene]
        )
    wait_all(copies)


def northing_block(side, to, place, slot_s, weight_s, lines, tile):
    row = lax.broadcasted_iota(jnp.int32, (8, LANE), 0)
    lane = lax.broadcasted_iota(jnp.int32, (8, LANE), 1)
    block = jnp.zeros((8, LANE), F32)
    for rank in range(CAP):
        spot = place[(to + 1) * CAP + rank]
        scene = jnp.maximum(spot, 0)
        amount = jnp.where(spot >= 0, weight_s[0, scene], 0.0)
        where = slot_s[0, scene]
        line = lines[pl.ds(scene, 1), :]
        for part in range(2):
            block = jnp.where(row == rank * 2 + part, line[:, part * LANE : (part + 1) * LANE], block)
            value = jnp.where(where == part * 2 + side, amount, 0.0)
            block = jnp.where((row == 4) & (lane == rank * 2 + part), value, block)
        spot = place[(to + (0 if side == 0 else 2)) * CAP + rank]
        scene = jnp.maximum(spot, 0)
        amount = jnp.where(spot >= 0, weight_s[0, scene], 0.0)
        line = lines[pl.ds(scene, 1), :]
        at = tile - 1 if side == 0 else 0
        base = 8 + rank * 3
        for part in range(2):
            value = jnp.broadcast_to(line[:, part * LANE + at : part * LANE + at + 1], (1, LANE))
            block = jnp.where((row == 4) & (lane == base + part), value, block)
        value = jnp.where(slot_s[0, scene] == (2 if side == 0 else 1), amount, 0.0)
        block = jnp.where((row == 4) & (lane == base + 2), value, block)
    return block


def pack_kernel(groups, count, tile, *refs):
    owner, slot, weight, ice, obs_h, vel_h, visc_h, fric_h, drive_h, first, second, edge = refs[:12]
    (
        owner_s, slot_s, weight_b, weight_v, weight_s, ice_s, obs, vel, visc, fric, drive, to_low, to_high, lines,
        place, filled, scalar_sem, more_sem, load_sem,
    ) = refs[12:]
    loads = copy_all([(vel_h, vel), (drive_h, drive), (visc_h, visc), (fric_h, fric), (obs_h, obs)], load_sem)
    more = copy_all([(ice, ice_s)], more_sem)
    scalars = load_scalars(owner, slot, weight, owner_s, slot_s, weight_b, weight_v, weight_s, scalar_sem)
    picked = lax.broadcasted_iota(jnp.int32, (8, LANE), 0)
    across = lax.broadcasted_iota(jnp.int32, (8, LANE), 1)
    cells, cells_y = visc.shape
    scalars[0].wait()
    fill_places(place, filled, groups, count, lambda scene: owner_s[0, scene])

    def pick(depth):
        picked = lax.broadcasted_iota(jnp.int32, (8, cells_y), 0)
        across = lax.broadcasted_iota(jnp.int32, (8, cells_y), 1)
        wanted = jnp.where(picked < depth, picked, picked + cells_y - 2 * depth)
        return (across == wanted).astype(jnp.bfloat16)

    wait_all(loads[:4] + more)
    for index, (at, depth) in enumerate(FIELDS):
        if index == ICE:
            for target, column in ((to_low, 0), (to_high, ice_s.shape[1] - 1)):
                target[at : at + 1, :] = ice_line([ice_s[row, column] for row in range(ice_s.shape[0])], (1, cells), tile)
            for number, row in enumerate((0, ice_s.shape[0] - 1)):
                edge[number, at : at + 1, :] = ice_line(
                    [ice_s[row, column] for column in range(ice_s.shape[1])], (1, cells_y), tile
                )
            continue
        field = {VISC: visc, FRIC: fric}.get(index)
        if field is None:
            field = vel.at[index] if index in (U, V) else drive.at[index - DRIVE_U]
        parts = [field[...]] if index not in (VISC, FRIC) else split(field[...])
        rows = sum(columns_of(pick(depth), part) for part in parts)
        to_low[at : at + depth, :] = rows[0:depth]
        to_high[at : at + depth, :] = rows[depth : 2 * depth]
        edge[0, at : at + depth, :] = field[0:16, :].astype(F32)[0:depth]
        edge[1, at : at + depth, :] = field[cells - 16 : cells, :].astype(F32)[16 - depth : 16]
    loads[4].wait()
    both = (across == jnp.where(picked == 0, 0, LANE - 1)).astype(jnp.bfloat16)
    for scene in range(count):
        rows = columns_of(both, obs[scene].reshape(2 * tile, LANE))
        lines[0, scene : scene + 1, :] = rows[0:1]
        lines[1, scene : scene + 1, :] = rows[1:2]
    wait_all(scalars[1:])
    half = groups // 2
    for side, target in enumerate((to_low, to_high)):
        for to in range(groups):
            at = PACK + to % half * 8
            lanes = slice(to // half * LANE, (to // half + 1) * LANE)
            target[at : at + 8, lanes] = northing_block(side, to, place, slot_s, weight_s, lines.at[side], tile)
    even = lax.rem(lax.axis_index("gy"), 2) == 0
    first[...] = jnp.where(even, to_high[...], to_low[...])
    second[...] = jnp.where(even, to_low[...], to_high[...])


def side_tiles(right, left, turned):
    turned[...] = jnp.zeros_like(turned)
    turned[0:PACK, :] = right
    turned[PACK : 2 * PACK, :] = left
    return jnp.transpose(turned[...])


def side_tile(upright, index):
    at, depth = FIELDS[index]
    lane = lax.broadcasted_iota(jnp.int32, upright.shape, 1)
    after = pltpu.roll(upright, (LANE - at) % LANE, 1)
    before = pltpu.roll(upright, LANE - depth - PACK - at, 1)
    return jnp.where(lane < depth, after, jnp.where(lane >= LANE - depth, before, 0.0))


def write_halo(pay, base, pack):
    first = FIELDS[VISC][0]
    last = FIELDS[FRIC][0] + FIELDS[FRIC][1]
    for number in range(pack.shape[1] // LANE):
        whole = pack[:, number * LANE : (number + 1) * LANE]
        high = whole.astype(jnp.bfloat16)
        rest = whole - high.astype(F32)
        middle = rest.astype(jnp.bfloat16).astype(F32)
        pay[base + 2 * number] = high
        both = jnp.concatenate([middle[first:last], (rest - middle)[first:last]], axis=0)
        fill = jnp.zeros((PACK - both.shape[0], LANE), F32)
        pay[base + 2 * number + 1] = jnp.concatenate([both, fill], axis=0).astype(jnp.bfloat16)


def read_halo(pays, base, pack, me, beside):
    first = FIELDS[VISC][0]
    count = FIELDS[FRIC][0] + FIELDS[FRIC][1] - first
    for number in range(pack.shape[1] // LANE):
        lanes = slice(number * LANE, (number + 1) * LANE)
        high, more = jnp.zeros((PACK, LANE), F32), jnp.zeros((PACK, LANE), F32)
        for step, pay in pays.items():
            here = partner(me, step) == beside
            high = jnp.where(here, pay[base + 2 * number].astype(F32), high)
            more = jnp.where(here, pay[base + 2 * number + 1].astype(F32), more)
        pack[:, lanes] = high
        pack[first : first + count, lanes] += more[0:count]
        pack[first : first + count, lanes] += more[count : 2 * count]


def widen_kernel(groups, tile, early, late, *refs):
    first, second, edge = refs[:3]
    pays = dict(zip(late, refs[3 + len(late) :]))
    refs = refs[3 + 2 * len(late) :]
    apart = dict(zip(early, refs))
    turned, to_low, to_high = refs[len(early) :]
    cells_y = edge.shape[2]
    blocks = tile // PACK
    me = lax.axis_index("gx")
    half = groups // 2
    for step in late + early:
        to = partner(me, step)
        here = pl.ds(pl.multiple_of(PACK + lax.rem(to, half) * 8, 8), 8)
        sides = both_sides(first[here, :], second[here, :])
        block = jnp.concatenate([jnp.where(to < half, side[:, 0:LANE], side[:, LANE:]) for side in sides], axis=0)
        if step in early:
            apart[step][0] = block.astype(jnp.bfloat16)
        else:
            pays[step][CAP * 2 * blocks + 1] = block.astype(jnp.bfloat16)
    upright = side_tiles(*both_sides(first[0:PACK, :], second[0:PACK, :]), turned)
    cells = upright.shape[0]
    to_low[:, 0:cells_y] = edge[0]
    to_high[:, 0:cells_y] = edge[1]
    for index, (at, depth) in enumerate(FIELDS):
        to_low[at : at + depth, cells_y:] = side_tile(upright[0:8], index)[0:depth]
        to_high[at : at + depth, cells_y:] = side_tile(upright[cells - 8 :], index)[8 - depth : 8]
    base = CAP * 2 * blocks + 2
    for step in halo_steps(groups):
        write_halo(pays[step], base, jnp.where(partner(me, step) > me, to_high[...], to_low[...]))


def stress_block(u, v, visc, low, rows, wide):
    here, after = pl.ds(low, rows), pl.ds(low + 1, rows)
    vel_u, vel_v = u[here, :], v[here, :]
    a_x = u[after, :] - vel_u
    b_x = v[after, :] - vel_v
    a_y = pltpu.roll(vel_u, wide - 1, 1) - vel_u
    b_y = pltpu.roll(vel_v, wide - 1, 1) - vel_v
    nu = visc[here, :]
    return nu * (4.0 * a_x + 2.0 * b_y), nu * (4.0 * b_y + 2.0 * a_x), nu * (a_y + b_x)


def image_block(sxx, syy, sxy, low, rows):
    here, before = pl.ds(low, rows), pl.ds(low - 1, rows)
    mid = sxy[here, :]
    push_u = sxx[before, :] - sxx[here, :] + pltpu.roll(mid, 1, 1) - mid
    side = syy[here, :]
    push_v = sxy[before, :] - mid + pltpu.roll(side, 1, 1) - side
    return push_u, push_v


def relaxation(fields, work, wide, cells_y, spans, outs, shift, own_of, size=8):
    u, v, visc, fric, drive_u, drive_v, ice = fields
    next_u, next_v, relax_u, relax_v, sxx, syy, sxy = work
    second, ease, lead, trail = outs
    for low in spans[0]:
        here = pl.ds(low, size)
        nu, drag = visc[here, :], fric[here, :]
        nu_x = visc[pl.ds(low - 1, size), :]
        nu_y = pltpu.roll(nu, 1, 1)
        inside = drag > 0.0
        for out, diag in ((relax_u, 5.0 * nu + 4.0 * nu_x + nu_y), (relax_v, 5.0 * nu + nu_x + 4.0 * nu_y)):
            out[here, :] = jnp.where(inside, 1.0 / jnp.where(inside, diag + drag, 1.0), 0.0)
    for low in spans[1]:
        here = pl.ds(low, size)
        sxx[here, :], syy[here, :], sxy[here, :] = stress_block(u, v, visc, low, size, wide)
    for low in spans[2]:
        here, there = pl.ds(low, size), pl.ds(low + shift, size)
        pushes = image_block(sxx, syy, sxy, low, size)
        for part, (push, speed, force, relax, then) in enumerate(
            zip(pushes, (u, v), (drive_u, drive_v), (relax_u, relax_v), (next_u, next_v))
        ):
            now, soft = speed[here, :], relax[here, :]
            move = soft * (force[here, :] - push - fric[here, :] * now)
            then[here, :] = now + OMEGA * move
            if low in spans[4]:
                slack = OMEGA * soft
                ease[part, there, :] = slack
                if own_of(low) is not None:
                    factor = -ice[here, 0:cells_y] * (slack * (move + now))[:, 0:cells_y]
                    lead[part, pl.ds(own_of(low), size), :] = factor
    for low in spans[3]:
        here = pl.ds(low, size)
        sxx[here, :], syy[here, :], sxy[here, :] = stress_block(next_u, next_v, visc, low, size, wide)
    for low in spans[4]:
        here, there = pl.ds(low, size), pl.ds(low + shift, size)
        pushes = image_block(sxx, syy, sxy, low, size)
        for part, (push, speed, force, relax) in enumerate(
            zip(pushes, (next_u, next_v), (drive_u, drive_v), (relax_u, relax_v))
        ):
            now = speed[here, :]
            move = relax[here, :] * (force[here, :] - push - fric[here, :] * now)
            second[part, there, :] = ice[here, :] * (now + OMEGA * move)
            if own_of(low) is not None:
                mine = pl.ds(own_of(low), size)
                trail[part, mine, :] = (
                    -ice[here, 0:cells_y] * (move + now)[:, 0:cells_y] - fric[here, 0:cells_y] * lead[part, mine, :]
                )


STRIP = 32


def sweep_kernel(tile, ice, vel, visc, fric, drive, first, then, *refs):
    second, ease, lead, trail, wide_visc, wide_ice, strips = refs[:7]
    u, v, wide_fric, drive_u, drive_v = refs[7:12]
    work = refs[12:19]
    turned, ice_s, sems = refs[19:]
    cells, cells_y = visc.shape
    rows, wide = wide_visc.shape
    loads = copy_all([(ice, ice_s)], sems)
    upright = side_tiles(*both_sides(first[0:PACK, :], then[0:PACK, :]), turned)
    wait_all(loads)
    own_rows = slice(PAD, PAD + cells)
    fields = (u, v, wide_visc, wide_fric, drive_u, drive_v, wide_ice)
    for index, field in enumerate(fields):
        field[0:PAD, :] = jnp.zeros((PAD, wide), F32)
        field[PAD + cells :, :] = jnp.zeros((PAD, wide), F32)
        if index == ICE:
            for number in range(cells // tile):
                field[PAD + number * tile : PAD + (number + 1) * tile, 0:cells_y] = ice_line(
                    [ice_s[number, column] for column in range(ice_s.shape[1])], (tile, cells_y), tile
                )
        elif index in (VISC, FRIC):
            field[own_rows, 0:cells_y] = (visc if index == VISC else fric)[...]
        else:
            source = vel if index in (U, V) else drive
            field[own_rows, 0:cells_y] = source[index % DRIVE_U].astype(F32)
        field[own_rows, cells_y:wide] = side_tile(upright, index)
        strips[index, 0] = field[8 : 8 + STRIP, :]
        strips[index, 1] = field[rows - 8 - STRIP : rows - 8, :]
    last = PAD + cells
    spans = [range(PAD, last, 32)] * 5
    relaxation(fields, work, wide, cells_y, spans, (second, ease, lead, trail), 0, lambda low: low - PAD, 32)


def trim_kernel(groups, tile, *refs):
    steps = halo_steps(groups)
    pays = dict(zip(steps, refs))
    strips = refs[len(steps)]
    second, ease, lead, trail, visc, ice = refs[len(steps) + 7 : len(steps) + 13]
    refs = refs[len(steps) + 13 :]
    fields, work, pack = refs[:7], refs[7:14], refs[14]
    rows, wide = visc.shape
    cells_y = wide - LANE
    cells = rows - 2 * PAD
    base = CAP * 2 * (tile // PACK) + 2
    me = lax.axis_index("gx")
    spans = (
        [(8, 16, 24), (8, 16, 24), (8, 16, 24), (8, 16), (8, 16)],
        [(16, 24, 32), (8, 16, 24, 32), (16, 24, 32), (16, 24, 32), (24, 32)],
    )
    for strip in range(2):
        read_halo(pays, base, pack, me, me - 1 if strip == 0 else me + 1)
        shift = 0 if strip == 0 else rows - 16 - STRIP
        edge = PAD if strip == 0 else PAD + cells - shift
        for index, field in enumerate(fields):
            at, depth = FIELDS[index]
            field[8 : 8 + STRIP, :] = strips[index, strip]
            target = slice(edge - depth, edge) if strip == 0 else slice(edge, edge + depth)
            field[target, :] = pack[at : at + depth, :]
            if index in (VISC, ICE):
                (visc if index == VISC else ice)[target.start + shift : target.stop + shift, :] = pack[at : at + depth, :]
        own = {0: (16, 0), 1: (24, cells - 8)}[strip]
        relaxation(
            fields, work, wide, cells_y, spans[strip], (second, ease, lead, trail), shift,
            lambda low, own=own: own[1] if low == own[0] else None,
        )


def final_kernel(groups, tile, early, *refs):
    pays = refs[:groups]
    apart = dict(zip(early, refs[groups:]))
    refs = refs[len(early) :]
    second, ease, lead, trail, visc, ice, grad = refs[groups : groups + 7]
    misfit, u, v, sxx, syy, sxy, table, total, rows_x, rows_y, turned = refs[groups + 7 :]
    rows, wide = visc.shape
    cells_y = wide - LANE
    cells = rows - 2 * PAD
    blocks = tile // PACK
    tiles_y = cells_y // tile
    slots = cells // tile * tiles_y
    lift = (u, v)
    for group in range(groups):
        rows_x[pl.ds(group, PACK, stride=groups), :] = pays[group][CAP * 2 * blocks].astype(F32)
        side = apart[group][0] if group in early else pays[group][CAP * 2 * blocks + 1]
        rows_y[pl.ds(group, PACK, stride=groups), :] = side.astype(F32)

    def raw(source, number):
        return source[number * groups : (number + 1) * groups, :]

    def spread(source, number, row=8):
        return jnp.broadcast_to(raw(source, row)[:, number : number + 1], (groups, LANE))

    def gathered(value):
        return jnp.sum(value, axis=0, keepdims=True)

    for position in range(slots):
        weights = [spread(rows_x, rank * slots + position) for rank in range(CAP)]
        for rank in range(CAP):
            at = (rank * slots + position) * groups
            table[at : at + groups, :] = weights[rank]
        total[position : position + 1, :] = gathered(sum(weights))
    for field in lift:
        field[0:PAD, :] = jnp.zeros((PAD, wide), F32)
        field[PAD + cells :, :] = jnp.zeros((PAD, wide), F32)
    turned[...] = jnp.zeros_like(turned)
    for side in range(2):
        at = PAD + cells if side == 0 else PAD - 1
        for column in range(2):
            lanes = slice(column * tile, (column + 1) * tile)
            weights = [spread(rows_x, 8 + (side * CAP + rank) * 2 + column) for rank in range(CAP)]
            weight = gathered(sum(weights))
            for part in range(2):
                seen = gathered(sum(weights[rank] * raw(rows_x, (side * CAP + rank) * 2 + part) for rank in range(CAP)))
                gap = weight * second[part, at : at + 1, lanes] - ice[at : at + 1, lanes] * seen
                lift[part][at : at + 1, lanes] = ease[part, at : at + 1, lanes] * gap
        lines = [[None] * 2 for _ in range(3)]
        for column in range(2):
            weights = [spread(rows_y, rank * 2 + column, side * 8 + 4) for rank in range(CAP)]
            lines[2][column] = gathered(sum(weights))
            for part in range(2):
                lines[part][column] = gathered(
                    sum(weights[rank] * raw(rows_y, side * 8 + rank * 2 + part) for rank in range(CAP))
                )
        weights = [spread(rows_y, 8 + rank * 3 + 2, side * 8 + 4) for rank in range(CAP)]
        corners = [
            gathered(sum(weights[rank] * spread(rows_y, 8 + rank * 3 + part, side * 8 + 4) for rank in range(CAP)))
            for part in range(2)
        ] + [gathered(sum(weights))]
        lane = lax.broadcasted_iota(jnp.int32, (1, turned.shape[1]), 1)
        for number in range(3):
            line = jnp.concatenate(
                lines[number] + [jnp.zeros((1, turned.shape[1] - 2 * tile), F32)], axis=1
            )
            line = pltpu.roll(jnp.broadcast_to(line, (8, turned.shape[1])), PAD, 1)[0:1]
            corner = jnp.concatenate([corners[number]] * (turned.shape[1] // LANE), axis=1)
            line = jnp.where(lane == (PAD - 1 if side == 0 else PAD + cells), corner, line)
            at = number if side == 0 else LANE - 1 - number
            turned[at : at + 1, :] = line
    upright = jnp.transpose(turned[...])[0:rows]
    lane = lax.broadcasted_iota(jnp.int32, (rows, LANE), 1)

    def sides(number):
        after = pltpu.roll(upright, (LANE - number) % LANE, 1)
        before = pltpu.roll(upright, number, 1)
        return jnp.where(lane == 0, after, jnp.where(lane == LANE - 1, before, 0.0))

    weight = sides(2)
    for part in range(2):
        gap = weight * second[part, :, cells_y:wide] - ice[:, cells_y:wide] * sides(part)
        lift[part][:, cells_y:wide] = ease[part, :, cells_y:wide] * gap

    def step(index, carry):
        part, chunk = index // blocks, index % blocks
        sums = [jnp.zeros((PACK, LANE), F32) for _ in range(slots)]
        for group in range(groups):
            for rank in range(CAP):
                got = pays[group][rank * 2 * blocks + index].astype(F32)
                for position in range(slots):
                    sums[position] += table[pl.ds((rank * slots + position) * groups + group, 1), :] * got
        for position in range(slots):
            lanes = slice((position % tiles_y) * tile, (position % tiles_y + 1) * tile)
            at = pl.multiple_of((position // tiles_y) * tile + chunk * PACK, PACK)
            here = pl.ds(pl.multiple_of(at + PAD, PACK), PACK)
            gap = total[position : position + 1, :] * second[part, here, lanes] - ice[here, lanes] * sums[position]
            misfit[part, pl.ds(at, PACK), lanes] = gap
            sums[position] = ease[part, here, lanes] * gap

        for number, field in enumerate(lift):

            @pl.when(part == number)
            def _():
                for position in range(slots):
                    lanes = slice((position % tiles_y) * tile, (position % tiles_y + 1) * tile)
                    at = pl.multiple_of((position // tiles_y) * tile + chunk * PACK + PAD, PACK)
                    field[pl.ds(at, PACK), lanes] = sums[position]

        return carry

    lax.fori_loop(0, 2 * blocks, step, 0)
    for low in (8, *range(PAD, rows - PAD, 32)):
        size = 32 if low >= PAD else 8
        here = pl.ds(low, size)
        sxx[here, :], syy[here, :], sxy[here, :] = stress_block(u, v, visc, low, size, wide)
    for low in range(PAD, rows - PAD, 32):
        mine = pl.ds(low - PAD, 32)
        here = pl.ds(low, 32)
        sums = jnp.zeros((32, cells_y), F32)
        for part, push in enumerate(image_block(sxx, syy, sxy, low, 32)):
            sums += (misfit[part, mine, :] - push[:, 0:cells_y]) * lead[part, mine, :]
            sums += lift[part][here, 0:cells_y] * trail[part, mine, :]
        grad[mine, :] = sums


def body(vel0, visc, fric, drive, scene_obs, scene_weight, scene_owner, scene_slot, ice_mask):
    cells_x, cells_y = visc.shape
    tile = scene_obs.shape[-1]
    count = scene_obs.shape[1]
    groups = lax.axis_size("gx")
    blocks = tile // PACK
    rows, wide = cells_x + 2 * PAD, cells_y + LANE
    long = -(-rows // LANE) * LANE
    obs = scene_obs.reshape(count, 2 * blocks, PACK, LANE)
    owner, slot, weight = scene_owner.reshape(1, count), scene_slot, scene_weight
    limit = pltpu.CompilerParams(vmem_limit_bytes=40 << 20)
    dma = pltpu.SemaphoreType.DMA
    def shape(*dims, dtype=F32):
        return jax.ShapeDtypeStruct(dims, dtype)

    def short(*dims):
        return pltpu.VMEM(dims, jnp.bfloat16)

    def full(*dims):
        return pltpu.VMEM(dims, F32)

    bf16, i32 = jnp.bfloat16, jnp.int32
    deep = CAP * 2 * blocks
    tall = PACK + groups // 2 * 8
    half = groups // 2
    early = (half + 1, half)
    late = tuple(step for step in range(groups) if step not in early)
    halo = 2 * (wide // LANE)

    def pay(step):
        more = 0 if step in early else 1 + (halo if step in halo_steps(groups) else 0)
        return pltpu.VMEM((deep + 1 + more, PACK, LANE), bf16)

    def move(step, value, *others):
        pairs = [(me, partner(me, step)) for me in range(groups)]
        return lax.ppermute(after(value, *others) if others else value, "gx", pairs)

    scalars = [
        pltpu.SMEM((1, count), i32), pltpu.SMEM((1, count), i32), short(1, count), full(1, count),
        pltpu.SMEM((1, count), F32),
    ]
    places = [pltpu.SMEM(((groups + 2) * CAP,), i32), pltpu.SMEM((groups,), i32)]
    pays = pl.pallas_call(
        functools.partial(gather_kernel, groups, count, tile),
        out_shape=[pay(step) for step in range(groups)],
        in_specs=[HBM] * 4,
        out_specs=[VMEM] * groups,
        scratch_shapes=[
            *scalars, short(4, count, PACK, LANE), *places, dma((3,)), dma((4,)),
            dma((groups * CAP,)),
        ],
        compiler_params=limit,
        name="gather",
    )(*in_place(owner, slot, weight, obs))
    got = [pays[0]] * groups
    for step in early:
        got[step] = move(step, pays[step])
    *north, edge = pl.pallas_call(
        functools.partial(pack_kernel, groups, count, tile),
        out_shape=[pltpu.VMEM((tall, cells_x), F32)] * 2 + [pltpu.VMEM((2, PACK, cells_y), F32)],
        in_specs=[HBM] * 9,
        out_specs=[VMEM] * 3,
        scratch_shapes=scalars + [
            pltpu.SMEM(ice_mask.shape, i32), short(*obs.shape), short(*vel0.shape), full(*visc.shape),
            full(*fric.shape), short(*drive.shape), full(tall, cells_x), full(tall, cells_x), full(2, count, cells_x),
            *places, dma((3,)), dma((1,)), dma((5,)),
        ],
        compiler_params=limit,
        name="pack",
    )(*in_place(after(owner, pays[half]), slot, weight, ice_mask, obs, vel0, visc, fric, drive))
    first, second = swap(*north)
    outs = pl.pallas_call(
        functools.partial(widen_kernel, groups, tile, early, late),
        out_shape=[pay(step) for step in late] + [pltpu.VMEM((1, PACK, LANE), bf16)] * len(early),
        in_specs=[VMEM] * (3 + len(late)),
        out_specs=[VMEM] * groups,
        input_output_aliases={3 + number: number for number in range(len(late))},
        scratch_shapes=[full(LANE, cells_x), full(PACK, wide), full(PACK, wide)],
        compiler_params=limit,
        name="widen",
    )(first, second, edge, *(pays[step] for step in late))
    ready = dict(zip(late, outs))
    got[0] = ready[0]
    order = [groups - 1, 1, *range(half + 2, groups - 1), half - 1, *range(2, half - 1)]
    ties = {half + 2: [got[half + 1]], 2: [got[half]], 1: [], half - 1: [], groups - 1: []}
    for step in order:
        got[step] = move(step, ready[step], *ties.get(step, []))
    apart = [move(step, value, *more) for step, value, more in zip(early, outs[len(late) :], ([got[half]], [got[half]]))]
    strip = shape(len(FIELDS), 2, STRIP, wide)
    base_shapes = [shape(2, rows, wide)] * 2 + [shape(2, cells_x, cells_y)] * 2 + [shape(rows, wide)] * 2
    *base, strips = pl.pallas_call(
        functools.partial(sweep_kernel, tile),
        out_shape=base_shapes + [strip],
        in_specs=[HBM] + [VMEM] * 6,
        out_specs=[VMEM] * 7,
        scratch_shapes=[full(rows, wide)] * 12 + [full(LANE, cells_x), pltpu.SMEM(ice_mask.shape, i32), dma((1,))],
        compiler_params=limit,
        name="sweep",
    )(ice_mask, vel0, visc, fric, drive, after(first, *[got[half]]), second)
    near = [got[step] for step in halo_steps(groups)]
    base = pl.pallas_call(
        functools.partial(trim_kernel, groups, tile),
        out_shape=base_shapes,
        in_specs=[VMEM] * (len(near) + 7),
        out_specs=[VMEM] * 6,
        input_output_aliases={len(near) + 1 + number: number for number in range(6)},
        scratch_shapes=[full(STRIP + 16, wide)] * 14 + [full(PACK, wide)],
        compiler_params=limit,
        name="trim",
    )(*near, strips, *base)
    return pl.pallas_call(
        functools.partial(final_kernel, groups, tile, early),
        out_shape=shape(cells_x, cells_y),
        in_specs=[VMEM] * (groups + len(early) + 6),
        out_specs=VMEM,
        scratch_shapes=[full(2, cells_x, cells_y)] + [full(rows, wide)] * 5
        + [
            full(groups * CAP * 4, LANE), full(8, LANE), full(PACK * groups, LANE), full(PACK * groups, LANE),
            full(LANE, long),
        ],
        compiler_params=limit,
        name="final",
    )(*got, *apart, *base)


def solution(mesh):
    placed = (
        P(None, "gx", "gy"),
        P("gx", "gy"),
        P("gx", "gy"),
        P(None, "gx", "gy"),
        P("gy", "gx", None, None, None),
        P("gy", "gx"),
        P("gy", "gx", None),
        P("gy", "gx"),
        P("gx", "gy"),
    )
    return jax.shard_map(body, mesh=mesh, in_specs=placed, out_specs=P("gx", "gy"), check_vma=False)
```

```python
import functools

import jax
import jax.numpy as jnp
from jax import lax
from jax.experimental import pallas as pl
from jax.experimental.pallas import tpu as pltpu
from jax.sharding import PartitionSpec as P

CAP = 2
OMEGA = 0.6
LANE = 128
PAD = 16
PACK = 16
FIELDS = ((0, 3), (3, 3), (6, 3), (9, 2), (11, 2), (13, 2), (15, 1))
U, V, VISC, FRIC, DRIVE_U, DRIVE_V, ICE = range(7)

VMEM = pl.BlockSpec(memory_space=pltpu.VMEM)
HBM = pl.BlockSpec(memory_space=pltpu.HBM)
F32 = jnp.float32


def partner(me, step):
    return me ^ step


def halo_steps(groups):
    return [step for step in range(1, groups) if step & (step + 1) == 0]


def after(value, *others):
    return lax.optimization_barrier((value, *others))[0]


def in_place(*values):
    return [pltpu.with_memory_space_constraint(value, pltpu.HBM) for value in values]


def swap(even, odd):
    count = lax.axis_size("gy")
    near = [(me, me ^ 1) for me in range(count)]
    far = [(me, me + 1 if me % 2 else me - 1) for me in range(1, count - 1)]
    return lax.ppermute(even, "gy", near), lax.ppermute(odd, "gy", far)


def both_sides(first, second):
    even = lax.rem(lax.axis_index("gy"), 2) == 0
    return jnp.where(even, first, second), jnp.where(even, second, first)


def copy_all(pairs, sems, first=0):
    copies = [
        pltpu.make_async_copy(source, target, sems.at[first + number])
        for number, (source, target) in enumerate(pairs)
    ]
    for copy in copies:
        copy.start()
    return copies


def wait_all(copies):
    for copy in copies:
        copy.wait()


def ice_line(values, shape, tile):
    lane = lax.broadcasted_iota(jnp.int32, shape, 1)
    line = jnp.zeros(shape, F32)
    for number, value in enumerate(values):
        line = jnp.where(lane // tile == number, value.astype(F32), line)
    return line


def fill_places(place, filled, groups, count, owner_of):
    for index in range((groups + 2) * CAP):
        place[index] = -1
    for index in range(groups):
        filled[index] = 0
    for scene in range(count):
        who = owner_of(scene)
        rank = filled[who]
        place[(who + 1) * CAP + rank] = scene
        filled[who] = rank + 1


def split(value):
    high = value.astype(jnp.bfloat16)
    rest = value - high.astype(F32)
    middle = rest.astype(jnp.bfloat16)
    return high, middle, (rest - middle.astype(F32)).astype(jnp.bfloat16)


def columns_of(pick, block):
    return lax.dot_general(pick, block, (((1,), (1,)), ((), ())), preferred_element_type=F32)


def load_scalars(owner, slot, weight, owner_s, slot_s, weight_b, weight_v, weight_s, sems):
    loads = copy_all([(owner, owner_s), (slot, slot_s), (weight, weight_b)], sems)
    loads[2].wait()
    weight_v[...] = weight_b[...].astype(F32)
    loads[2] = pltpu.make_async_copy(weight_v, weight_s, sems.at[2])
    loads[2].start()
    return loads


def easting_block(to, place, slot_s, weight_s, edge):
    row = lax.broadcasted_iota(jnp.int32, (PACK, LANE), 0)
    lane = lax.broadcasted_iota(jnp.int32, (PACK, LANE), 1)
    block = jnp.zeros((PACK, LANE), F32)
    for side in range(2):
        for rank in range(CAP):
            spot = place[(to + (2 if side == 0 else 0)) * CAP + rank]
            scene = jnp.maximum(spot, 0)
            amount = jnp.where(spot >= 0, weight_s[0, scene], 0.0)
            where = slot_s[0, scene]
            for part in range(2):
                line = edge(scene, part, side).astype(F32)
                line = line[0:1] if side == 0 else line[PACK - 1 : PACK]
                block = jnp.where(row == (side * CAP + rank) * 2 + part, line, block)
                value = jnp.where(where == side * 2 + part, amount, 0.0)
                block = jnp.where((row == 8) & (lane == 8 + (side * CAP + rank) * 2 + part), value, block)
    for rank in range(CAP):
        spot = place[(to + 1) * CAP + rank]
        scene = jnp.maximum(spot, 0)
        amount = jnp.where(spot >= 0, weight_s[0, scene], 0.0)
        for position in range(4):
            value = jnp.where(slot_s[0, scene] == position, amount, 0.0)
            block = jnp.where((row == 8) & (lane == rank * 4 + position), value, block)
    return block.astype(jnp.bfloat16)


def gather_scenes(obs, pays, steps, place, groups, blocks, me, sems):
    copies = []
    for number, step in enumerate(steps):
        to = partner(me, step)
        for rank in range(CAP):
            scene = jnp.maximum(place[(to + 1) * CAP + rank], 0)
            target = pays[number].at[pl.ds(rank * 2 * blocks, 2 * blocks)]
            copies += copy_all([(obs.at[scene], target)], sems, number * CAP + rank)
    return copies


def gather_kernel(groups, count, tile, *refs):
    owner, slot, weight, obs = refs[:4]
    pays = refs[4 : 4 + groups]
    owner_s, slot_s, weight_b, weight_v, weight_s, edges, place, filled, scalar_sem, edge_sem, scene_sem = refs[
        4 + groups :
    ]
    blocks = tile // PACK
    me = lax.axis_index("gx")
    loads = copy_all(
        [(obs.at[:, at], edges.at[number]) for number, at in enumerate((0, blocks, blocks - 1, 2 * blocks - 1))], edge_sem
    )
    scalars = load_scalars(owner, slot, weight, owner_s, slot_s, weight_b, weight_v, weight_s, scalar_sem)
    scalars[0].wait()
    fill_places(place, filled, groups, count, lambda scene: owner_s[0, scene])
    copies = gather_scenes(obs, pays, range(groups), place, groups, blocks, me, scene_sem)
    wait_all(scalars[1:] + loads)
    for step in range(groups):
        to = partner(me, step)
        pays[step][CAP * 2 * blocks] = easting_block(
            to, place, slot_s, weight_s, lambda scene, part, side: edges[side * 2 + part, scene]
        )
    wait_all(copies)


def northing_block(side, to, place, slot_s, weight_s, lines, tile):
    row = lax.broadcasted_iota(jnp.int32, (8, LANE), 0)
    lane = lax.broadcasted_iota(jnp.int32, (8, LANE), 1)
    block = jnp.zeros((8, LANE), F32)
    for rank in range(CAP):
        spot = place[(to + 1) * CAP + rank]
        scene = jnp.maximum(spot, 0)
        amount = jnp.where(spot >= 0, weight_s[0, scene], 0.0)
        where = slot_s[0, scene]
        line = lines[pl.ds(scene, 1), :]
        for part in range(2):
            block = jnp.where(row == rank * 2 + part, line[:, part * LANE : (part + 1) * LANE], block)
            value = jnp.where(where == part * 2 + side, amount, 0.0)
            block = jnp.where((row == 4) & (lane == rank * 2 + part), value, block)
        spot = place[(to + (0 if side == 0 else 2)) * CAP + rank]
        scene = jnp.maximum(spot, 0)
        amount = jnp.where(spot >= 0, weight_s[0, scene], 0.0)
        line = lines[pl.ds(scene, 1), :]
        at = tile - 1 if side == 0 else 0
        base = 8 + rank * 3
        for part in range(2):
            value = jnp.broadcast_to(line[:, part * LANE + at : part * LANE + at + 1], (1, LANE))
            block = jnp.where((row == 4) & (lane == base + part), value, block)
        value = jnp.where(slot_s[0, scene] == (2 if side == 0 else 1), amount, 0.0)
        block = jnp.where((row == 4) & (lane == base + 2), value, block)
    return block


def pack_kernel(groups, count, tile, *refs):
    owner, slot, weight, ice, obs_h, vel_h, visc_h, fric_h, drive_h, first, second, edge = refs[:12]
    (
        owner_s, slot_s, weight_b, weight_v, weight_s, ice_s, obs, vel, visc, fric, drive, to_low, to_high, lines,
        place, filled, scalar_sem, more_sem, load_sem,
    ) = refs[12:]
    loads = copy_all([(vel_h, vel), (drive_h, drive), (visc_h, visc), (fric_h, fric), (obs_h, obs)], load_sem)
    more = copy_all([(ice, ice_s)], more_sem)
    scalars = load_scalars(owner, slot, weight, owner_s, slot_s, weight_b, weight_v, weight_s, scalar_sem)
    picked = lax.broadcasted_iota(jnp.int32, (8, LANE), 0)
    across = lax.broadcasted_iota(jnp.int32, (8, LANE), 1)
    cells, cells_y = visc.shape
    scalars[0].wait()
    fill_places(place, filled, groups, count, lambda scene: owner_s[0, scene])

    def pick(depth):
        picked = lax.broadcasted_iota(jnp.int32, (8, cells_y), 0)
        across = lax.broadcasted_iota(jnp.int32, (8, cells_y), 1)
        wanted = jnp.where(picked < depth, picked, picked + cells_y - 2 * depth)
        return (across == wanted).astype(jnp.bfloat16)

    wait_all(loads[:4] + more)
    for index, (at, depth) in enumerate(FIELDS):
        if index == ICE:
            for target, column in ((to_low, 0), (to_high, ice_s.shape[1] - 1)):
                target[at : at + 1, :] = ice_line([ice_s[row, column] for row in range(ice_s.shape[0])], (1, cells), tile)
            for number, row in enumerate((0, ice_s.shape[0] - 1)):
                edge[number, at : at + 1, :] = ice_line(
                    [ice_s[row, column] for column in range(ice_s.shape[1])], (1, cells_y), tile
                )
            continue
        field = {VISC: visc, FRIC: fric}.get(index)
        if field is None:
            field = vel.at[index] if index in (U, V) else drive.at[index - DRIVE_U]
        parts = [field[...]] if index not in (VISC, FRIC) else split(field[...])
        rows = sum(columns_of(pick(depth), part) for part in parts)
        to_low[at : at + depth, :] = rows[0:depth]
        to_high[at : at + depth, :] = rows[depth : 2 * depth]
        edge[0, at : at + depth, :] = field[0:16, :].astype(F32)[0:depth]
        edge[1, at : at + depth, :] = field[cells - 16 : cells, :].astype(F32)[16 - depth : 16]
    loads[4].wait()
    both = (across == jnp.where(picked == 0, 0, LANE - 1)).astype(jnp.bfloat16)
    for scene in range(count):
        rows = columns_of(both, obs[scene].reshape(2 * tile, LANE))
        lines[0, scene : scene + 1, :] = rows[0:1]
        lines[1, scene : scene + 1, :] = rows[1:2]
    wait_all(scalars[1:])
    half = groups // 2
    for side, target in enumerate((to_low, to_high)):
        for to in range(groups):
            at = PACK + to % half * 8
            lanes = slice(to // half * LANE, (to // half + 1) * LANE)
            target[at : at + 8, lanes] = northing_block(side, to, place, slot_s, weight_s, lines.at[side], tile)
    even = lax.rem(lax.axis_index("gy"), 2) == 0
    first[...] = jnp.where(even, to_high[...], to_low[...])
    second[...] = jnp.where(even, to_low[...], to_high[...])


def side_tiles(right, left, turned):
    turned[...] = jnp.zeros_like(turned)
    turned[0:PACK, :] = right
    turned[PACK : 2 * PACK, :] = left
    return jnp.transpose(turned[...])


def side_tile(upright, index):
    at, depth = FIELDS[index]
    lane = lax.broadcasted_iota(jnp.int32, upright.shape, 1)
    after = pltpu.roll(upright, (LANE - at) % LANE, 1)
    before = pltpu.roll(upright, LANE - depth - PACK - at, 1)
    return jnp.where(lane < depth, after, jnp.where(lane >= LANE - depth, before, 0.0))


def write_halo(pay, base, pack):
    first = FIELDS[VISC][0]
    last = FIELDS[FRIC][0] + FIELDS[FRIC][1]
    for number in range(pack.shape[1] // LANE):
        whole = pack[:, number * LANE : (number + 1) * LANE]
        high = whole.astype(jnp.bfloat16)
        rest = whole - high.astype(F32)
        middle = rest.astype(jnp.bfloat16).astype(F32)
        pay[base + 2 * number] = high
        both = jnp.concatenate([middle[first:last], (rest - middle)[first:last]], axis=0)
        fill = jnp.zeros((PACK - both.shape[0], LANE), F32)
        pay[base + 2 * number + 1] = jnp.concatenate([both, fill], axis=0).astype(jnp.bfloat16)


def read_halo(pays, base, pack, me, beside):
    first = FIELDS[VISC][0]
    count = FIELDS[FRIC][0] + FIELDS[FRIC][1] - first
    for number in range(pack.shape[1] // LANE):
        lanes = slice(number * LANE, (number + 1) * LANE)
        high, more = jnp.zeros((PACK, LANE), F32), jnp.zeros((PACK, LANE), F32)
        for step, pay in pays.items():
            here = partner(me, step) == beside
            high = jnp.where(here, pay[base + 2 * number].astype(F32), high)
            more = jnp.where(here, pay[base + 2 * number + 1].astype(F32), more)
        pack[:, lanes] = high
        pack[first : first + count, lanes] += more[0:count]
        pack[first : first + count, lanes] += more[count : 2 * count]


def widen_kernel(groups, tile, early, late, *refs):
    first, second, edge = refs[:3]
    pays = dict(zip(late, refs[3 + len(late) :]))
    refs = refs[3 + 2 * len(late) :]
    apart = dict(zip(early, refs))
    turned, to_low, to_high = refs[len(early) :]
    cells_y = edge.shape[2]
    blocks = tile // PACK
    me = lax.axis_index("gx")
    half = groups // 2
    for step in late + early:
        to = partner(me, step)
        here = pl.ds(pl.multiple_of(PACK + lax.rem(to, half) * 8, 8), 8)
        sides = both_sides(first[here, :], second[here, :])
        block = jnp.concatenate([jnp.where(to < half, side[:, 0:LANE], side[:, LANE:]) for side in sides], axis=0)
        if step in early:
            apart[step][0] = block.astype(jnp.bfloat16)
        else:
            pays[step][CAP * 2 * blocks + 1] = block.astype(jnp.bfloat16)
    upright = side_tiles(*both_sides(first[0:PACK, :], second[0:PACK, :]), turned)
    cells = upright.shape[0]
    to_low[:, 0:cells_y] = edge[0]
    to_high[:, 0:cells_y] = edge[1]
    for index, (at, depth) in enumerate(FIELDS):
        to_low[at : at + depth, cells_y:] = side_tile(upright[0:8], index)[0:depth]
        to_high[at : at + depth, cells_y:] = side_tile(upright[cells - 8 :], index)[8 - depth : 8]
    base = CAP * 2 * blocks + 2
    for step in halo_steps(groups):
        write_halo(pays[step], base, jnp.where(partner(me, step) > me, to_high[...], to_low[...]))


def stress_block(u, v, visc, low, rows, wide):
    here, after = pl.ds(low, rows), pl.ds(low + 1, rows)
    vel_u, vel_v = u[here, :], v[here, :]
    a_x = u[after, :] - vel_u
    b_x = v[after, :] - vel_v
    a_y = pltpu.roll(vel_u, wide - 1, 1) - vel_u
    b_y = pltpu.roll(vel_v, wide - 1, 1) - vel_v
    nu = visc[here, :]
    return nu * (4.0 * a_x + 2.0 * b_y), nu * (4.0 * b_y + 2.0 * a_x), nu * (a_y + b_x)


def image_block(sxx, syy, sxy, low, rows):
    here, before = pl.ds(low, rows), pl.ds(low - 1, rows)
    mid = sxy[here, :]
    push_u = sxx[before, :] - sxx[here, :] + pltpu.roll(mid, 1, 1) - mid
    side = syy[here, :]
    push_v = sxy[before, :] - mid + pltpu.roll(side, 1, 1) - side
    return push_u, push_v


def relaxation(fields, work, wide, cells_y, spans, outs, shift, own_of, size=8):
    u, v, visc, fric, drive_u, drive_v, ice = fields
    next_u, next_v, relax_u, relax_v, sxx, syy, sxy = work
    second, ease, lead, trail = outs
    for low in spans[0]:
        here = pl.ds(low, size)
        nu, drag = visc[here, :], fric[here, :]
        nu_x = visc[pl.ds(low - 1, size), :]
        nu_y = pltpu.roll(nu, 1, 1)
        inside = drag > 0.0
        for out, diag in ((relax_u, 5.0 * nu + 4.0 * nu_x + nu_y), (relax_v, 5.0 * nu + nu_x + 4.0 * nu_y)):
            out[here, :] = jnp.where(inside, 1.0 / jnp.where(inside, diag + drag, 1.0), 0.0)
    for low in spans[1]:
        here = pl.ds(low, size)
        sxx[here, :], syy[here, :], sxy[here, :] = stress_block(u, v, visc, low, size, wide)
    for low in spans[2]:
        here, there = pl.ds(low, size), pl.ds(low + shift, size)
        pushes = image_block(sxx, syy, sxy, low, size)
        for part, (push, speed, force, relax, then) in enumerate(
            zip(pushes, (u, v), (drive_u, drive_v), (relax_u, relax_v), (next_u, next_v))
        ):
            now, soft = speed[here, :], relax[here, :]
            move = soft * (force[here, :] - push - fric[here, :] * now)
            then[here, :] = now + OMEGA * move
            if low in spans[4]:
                slack = OMEGA * soft
                ease[part, there, :] = slack
                if own_of(low) is not None:
                    factor = -ice[here, 0:cells_y] * (slack * (move + now))[:, 0:cells_y]
                    lead[part, pl.ds(own_of(low), size), :] = factor
    for low in spans[3]:
        here = pl.ds(low, size)
        sxx[here, :], syy[here, :], sxy[here, :] = stress_block(next_u, next_v, visc, low, size, wide)
    for low in spans[4]:
        here, there = pl.ds(low, size), pl.ds(low + shift, size)
        pushes = image_block(sxx, syy, sxy, low, size)
        for part, (push, speed, force, relax) in enumerate(
            zip(pushes, (next_u, next_v), (drive_u, drive_v), (relax_u, relax_v))
        ):
            now = speed[here, :]
            move = relax[here, :] * (force[here, :] - push - fric[here, :] * now)
            second[part, there, :] = ice[here, :] * (now + OMEGA * move)
            if own_of(low) is not None:
                mine = pl.ds(own_of(low), size)
                trail[part, mine, :] = (
                    -ice[here, 0:cells_y] * (move + now)[:, 0:cells_y] - fric[here, 0:cells_y] * lead[part, mine, :]
                )


STRIP = 32


def sweep_kernel(tile, ice, vel, visc, fric, drive, first, then, *refs):
    second, ease, lead, trail, wide_visc, wide_ice, strips = refs[:7]
    u, v, wide_fric, drive_u, drive_v = refs[7:12]
    work = refs[12:19]
    turned, ice_s, sems = refs[19:]
    cells, cells_y = visc.shape
    rows, wide = wide_visc.shape
    loads = copy_all([(ice, ice_s)], sems)
    upright = side_tiles(*both_sides(first[0:PACK, :], then[0:PACK, :]), turned)
    wait_all(loads)
    own_rows = slice(PAD, PAD + cells)
    fields = (u, v, wide_visc, wide_fric, drive_u, drive_v, wide_ice)
    for index, field in enumerate(fields):
        field[0:PAD, :] = jnp.zeros((PAD, wide), F32)
        field[PAD + cells :, :] = jnp.zeros((PAD, wide), F32)
        if index == ICE:
            for number in range(cells // tile):
                field[PAD + number * tile : PAD + (number + 1) * tile, 0:cells_y] = ice_line(
                    [ice_s[number, column] for column in range(ice_s.shape[1])], (tile, cells_y), tile
                )
        elif index in (VISC, FRIC):
            field[own_rows, 0:cells_y] = (visc if index == VISC else fric)[...]
        else:
            source = vel if index in (U, V) else drive
            field[own_rows, 0:cells_y] = source[index % DRIVE_U].astype(F32)
        field[own_rows, cells_y:wide] = side_tile(upright, index)
        strips[index, 0] = field[8 : 8 + STRIP, :]
        strips[index, 1] = field[rows - 8 - STRIP : rows - 8, :]
    last = PAD + cells
    spans = [range(PAD, last, 32)] * 5
    relaxation(fields, work, wide, cells_y, spans, (second, ease, lead, trail), 0, lambda low: low - PAD, 32)


def trim_kernel(groups, tile, *refs):
    steps = halo_steps(groups)
    pays = dict(zip(steps, refs))
    strips = refs[len(steps)]
    second, ease, lead, trail, visc, ice = refs[len(steps) + 7 : len(steps) + 13]
    refs = refs[len(steps) + 13 :]
    fields, work, pack = refs[:7], refs[7:14], refs[14]
    rows, wide = visc.shape
    cells_y = wide - LANE
    cells = rows - 2 * PAD
    base = CAP * 2 * (tile // PACK) + 2
    me = lax.axis_index("gx")
    spans = (
        [(8, 16, 24), (8, 16, 24), (8, 16, 24), (8, 16), (8, 16)],
        [(16, 24, 32), (8, 16, 24, 32), (16, 24, 32), (16, 24, 32), (24, 32)],
    )
    for strip in range(2):
        read_halo(pays, base, pack, me, me - 1 if strip == 0 else me + 1)
        shift = 0 if strip == 0 else rows - 16 - STRIP
        edge = PAD if strip == 0 else PAD + cells - shift
        for index, field in enumerate(fields):
            at, depth = FIELDS[index]
            field[8 : 8 + STRIP, :] = strips[index, strip]
            target = slice(edge - depth, edge) if strip == 0 else slice(edge, edge + depth)
            field[target, :] = pack[at : at + depth, :]
            if index in (VISC, ICE):
                (visc if index == VISC else ice)[target.start + shift : target.stop + shift, :] = pack[at : at + depth, :]
        own = {0: (16, 0), 1: (24, cells - 8)}[strip]
        relaxation(
            fields, work, wide, cells_y, spans[strip], (second, ease, lead, trail), shift,
            lambda low, own=own: own[1] if low == own[0] else None,
        )


def part_kernel(slots, tile, *refs):
    pays, (sums, table) = refs[:-2], refs[-2:]
    blocks = tile // PACK
    for number, pay in enumerate(pays):
        meta = pay[CAP * 2 * blocks].astype(F32)[8:9]
        for index in range(CAP * slots):
            at = number * CAP * slots + index
            table[at : at + 1, :] = jnp.broadcast_to(meta[:, index : index + 1], (1, LANE))

    def step(index, carry):
        total = [jnp.zeros((PACK, LANE), F32) for _ in range(slots)]
        for number, pay in enumerate(pays):
            for rank in range(CAP):
                got = pay[rank * 2 * blocks + index].astype(F32)
                for position in range(slots):
                    at = (number * CAP + rank) * slots + position
                    total[position] += table[at : at + 1, :] * got
        for position in range(slots):
            sums[index, position] = total[position]
        return carry

    lax.fori_loop(0, 2 * blocks, step, 0)


def final_kernel(groups, tile, early, summed, *refs):
    sums_before, refs = refs[0], refs[1:]
    pays = refs[:groups]
    apart = dict(zip(early, refs[groups:]))
    refs = refs[len(early) :]
    second, ease, lead, trail, visc, ice, grad = refs[groups : groups + 7]
    misfit, u, v, sxx, syy, sxy, table, total, rows_x, rows_y, turned, result, result_sem = refs[groups + 7 :]
    rows, wide = visc.shape
    cells_y = wide - LANE
    cells = rows - 2 * PAD
    blocks = tile // PACK
    tiles_y = cells_y // tile
    slots = cells // tile * tiles_y
    lift = (u, v)
    for group in range(groups):
        rows_x[pl.ds(group, PACK, stride=groups), :] = pays[group][CAP * 2 * blocks].astype(F32)
        side = apart[group][0] if group in early else pays[group][CAP * 2 * blocks + 1]
        rows_y[pl.ds(group, PACK, stride=groups), :] = side.astype(F32)

    def raw(source, number):
        return source[number * groups : (number + 1) * groups, :]

    def spread(source, number, row=8):
        return jnp.broadcast_to(raw(source, row)[:, number : number + 1], (groups, LANE))

    def gathered(value):
        return jnp.sum(value, axis=0, keepdims=True)

    for position in range(slots):
        weights = [spread(rows_x, rank * slots + position) for rank in range(CAP)]
        for rank in range(CAP):
            at = (rank * slots + position) * groups
            table[at : at + groups, :] = weights[rank]
        total[position : position + 1, :] = gathered(sum(weights))
    for field in lift:
        field[0:PAD, :] = jnp.zeros((PAD, wide), F32)
        field[PAD + cells :, :] = jnp.zeros((PAD, wide), F32)
    turned[...] = jnp.zeros_like(turned)
    for side in range(2):
        at = PAD + cells if side == 0 else PAD - 1
        for column in range(2):
            lanes = slice(column * tile, (column + 1) * tile)
            weights = [spread(rows_x, 8 + (side * CAP + rank) * 2 + column) for rank in range(CAP)]
            weight = gathered(sum(weights))
            for part in range(2):
                seen = gathered(sum(weights[rank] * raw(rows_x, (side * CAP + rank) * 2 + part) for rank in range(CAP)))
                gap = weight * second[part, at : at + 1, lanes] - ice[at : at + 1, lanes] * seen
                lift[part][at : at + 1, lanes] = ease[part, at : at + 1, lanes] * gap
        lines = [[None] * 2 for _ in range(3)]
        for column in range(2):
            weights = [spread(rows_y, rank * 2 + column, side * 8 + 4) for rank in range(CAP)]
            lines[2][column] = gathered(sum(weights))
            for part in range(2):
                lines[part][column] = gathered(
                    sum(weights[rank] * raw(rows_y, side * 8 + rank * 2 + part) for rank in range(CAP))
                )
        weights = [spread(rows_y, 8 + rank * 3 + 2, side * 8 + 4) for rank in range(CAP)]
        corners = [
            gathered(sum(weights[rank] * spread(rows_y, 8 + rank * 3 + part, side * 8 + 4) for rank in range(CAP)))
            for part in range(2)
        ] + [gathered(sum(weights))]
        lane = lax.broadcasted_iota(jnp.int32, (1, turned.shape[1]), 1)
        for number in range(3):
            line = jnp.concatenate(
                lines[number] + [jnp.zeros((1, turned.shape[1] - 2 * tile), F32)], axis=1
            )
            line = pltpu.roll(jnp.broadcast_to(line, (8, turned.shape[1])), PAD, 1)[0:1]
            corner = jnp.concatenate([corners[number]] * (turned.shape[1] // LANE), axis=1)
            line = jnp.where(lane == (PAD - 1 if side == 0 else PAD + cells), corner, line)
            at = number if side == 0 else LANE - 1 - number
            turned[at : at + 1, :] = line
    upright = jnp.transpose(turned[...])[0:rows]
    lane = lax.broadcasted_iota(jnp.int32, (rows, LANE), 1)

    def sides(number):
        after = pltpu.roll(upright, (LANE - number) % LANE, 1)
        before = pltpu.roll(upright, number, 1)
        return jnp.where(lane == 0, after, jnp.where(lane == LANE - 1, before, 0.0))

    weight = sides(2)
    for part in range(2):
        gap = weight * second[part, :, cells_y:wide] - ice[:, cells_y:wide] * sides(part)
        lift[part][:, cells_y:wide] = ease[part, :, cells_y:wide] * gap

    def step(index, carry):
        part, chunk = index // blocks, index % blocks
        sums = [sums_before[index, position] for position in range(slots)]
        for group in range(groups):
            if group in summed:
                continue
            for rank in range(CAP):
                got = pays[group][rank * 2 * blocks + index].astype(F32)
                for position in range(slots):
                    sums[position] += table[pl.ds((rank * slots + position) * groups + group, 1), :] * got
        for position in range(slots):
            lanes = slice((position % tiles_y) * tile, (position % tiles_y + 1) * tile)
            at = pl.multiple_of((position // tiles_y) * tile + chunk * PACK, PACK)
            here = pl.ds(pl.multiple_of(at + PAD, PACK), PACK)
            gap = total[position : position + 1, :] * second[part, here, lanes] - ice[here, lanes] * sums[position]
            misfit[part, pl.ds(at, PACK), lanes] = gap
            sums[position] = ease[part, here, lanes] * gap

        for number, field in enumerate(lift):

            @pl.when(part == number)
            def _():
                for position in range(slots):
                    lanes = slice((position % tiles_y) * tile, (position % tiles_y + 1) * tile)
                    at = pl.multiple_of((position // tiles_y) * tile + chunk * PACK + PAD, PACK)
                    field[pl.ds(at, PACK), lanes] = sums[position]

        return carry

    lax.fori_loop(0, 2 * blocks, step, 0)
    for low in (8, *range(PAD, rows - PAD, 32)):
        size = 32 if low >= PAD else 8
        here = pl.ds(low, size)
        sxx[here, :], syy[here, :], sxy[here, :] = stress_block(u, v, visc, low, size, wide)
    copies, quarter = [], cells // 4
    for low in range(PAD, rows - PAD, 32):
        mine = pl.ds(low - PAD, 32)
        here = pl.ds(low, 32)
        sums = jnp.zeros((32, cells_y), F32)
        for part, push in enumerate(image_block(sxx, syy, sxy, low, 32)):
            sums += (misfit[part, mine, :] - push[:, 0:cells_y]) * lead[part, mine, :]
            sums += lift[part][here, 0:cells_y] * trail[part, mine, :]
        result[mine, :] = sums
        done = low - PAD + 32
        if done % quarter == 0:
            part_rows = pl.ds(done - quarter, quarter)
            copies += copy_all([(result.at[part_rows], grad.at[part_rows])], result_sem, done // quarter - 1)
    wait_all(copies)


def body(vel0, visc, fric, drive, scene_obs, scene_weight, scene_owner, scene_slot, ice_mask):
    cells_x, cells_y = visc.shape
    tile = scene_obs.shape[-1]
    count = scene_obs.shape[1]
    groups = lax.axis_size("gx")
    blocks = tile // PACK
    rows, wide = cells_x + 2 * PAD, cells_y + LANE
    long = -(-rows // LANE) * LANE
    obs = scene_obs.reshape(count, 2 * blocks, PACK, LANE)
    owner, slot, weight = scene_owner.reshape(1, count), scene_slot, scene_weight
    limit = pltpu.CompilerParams(vmem_limit_bytes=40 << 20)
    dma = pltpu.SemaphoreType.DMA
    def shape(*dims, dtype=F32):
        return jax.ShapeDtypeStruct(dims, dtype)

    def short(*dims):
        return pltpu.VMEM(dims, jnp.bfloat16)

    def full(*dims):
        return pltpu.VMEM(dims, F32)

    bf16, i32 = jnp.bfloat16, jnp.int32
    deep = CAP * 2 * blocks
    tall = PACK + groups // 2 * 8
    half = groups // 2
    early = (half + 1, half)
    late = tuple(step for step in range(groups) if step not in early)
    halo = 2 * (wide // LANE)

    def pay(step):
        more = 0 if step in early else 1 + (halo if step in halo_steps(groups) else 0)
        return pltpu.VMEM((deep + 1 + more, PACK, LANE), bf16)

    def move(step, value, *others):
        pairs = [(me, partner(me, step)) for me in range(groups)]
        return lax.ppermute(after(value, *others) if others else value, "gx", pairs)

    scalars = [
        pltpu.SMEM((1, count), i32), pltpu.SMEM((1, count), i32), short(1, count), full(1, count),
        pltpu.SMEM((1, count), F32),
    ]
    places = [pltpu.SMEM(((groups + 2) * CAP,), i32), pltpu.SMEM((groups,), i32)]
    pays = pl.pallas_call(
        functools.partial(gather_kernel, groups, count, tile),
        out_shape=[pay(step) for step in range(groups)],
        in_specs=[HBM] * 4,
        out_specs=[VMEM] * groups,
        scratch_shapes=[
            *scalars, short(4, count, PACK, LANE), *places, dma((3,)), dma((4,)),
            dma((groups * CAP,)),
        ],
        compiler_params=limit,
        name="gather",
    )(*in_place(owner, slot, weight, obs))
    got = [pays[0]] * groups
    for step in early:
        got[step] = move(step, pays[step])
    *north, edge = pl.pallas_call(
        functools.partial(pack_kernel, groups, count, tile),
        out_shape=[pltpu.VMEM((tall, cells_x), F32)] * 2 + [pltpu.VMEM((2, PACK, cells_y), F32)],
        in_specs=[HBM] * 9,
        out_specs=[VMEM] * 3,
        scratch_shapes=scalars + [
            pltpu.SMEM(ice_mask.shape, i32), short(*obs.shape), short(*vel0.shape), full(*visc.shape),
            full(*fric.shape), short(*drive.shape), full(tall, cells_x), full(tall, cells_x), full(2, count, cells_x),
            *places, dma((3,)), dma((1,)), dma((5,)),
        ],
        compiler_params=limit,
        name="pack",
    )(*in_place(after(owner, pays[half]), slot, weight, ice_mask, obs, vel0, visc, fric, drive))
    first, second = swap(*north)
    outs = pl.pallas_call(
        functools.partial(widen_kernel, groups, tile, early, late),
        out_shape=[pay(step) for step in late] + [pltpu.VMEM((1, PACK, LANE), bf16)] * len(early),
        in_specs=[VMEM] * (3 + len(late)),
        out_specs=[VMEM] * groups,
        input_output_aliases={3 + number: number for number in range(len(late))},
        scratch_shapes=[full(LANE, cells_x), full(PACK, wide), full(PACK, wide)],
        compiler_params=limit,
        name="widen",
    )(first, second, edge, *(pays[step] for step in late))
    ready = dict(zip(late, outs))
    got[0] = ready[0]
    ties = {half + 2: [got[half + 1]], 1: [], half - 1: [], groups - 1: []}
    for step in (groups - 1, 1, *range(half + 2, groups - 1), half - 1):
        got[step] = move(step, ready[step], *ties.get(step, []))
    strip = shape(len(FIELDS), 2, STRIP, wide)
    base_shapes = [shape(2, rows, wide)] * 2 + [shape(2, cells_x, cells_y)] * 2 + [shape(rows, wide)] * 2
    *base, strips = pl.pallas_call(
        functools.partial(sweep_kernel, tile),
        out_shape=base_shapes + [strip],
        in_specs=[HBM] + [VMEM] * 6,
        out_specs=[VMEM] * 7,
        scratch_shapes=[full(rows, wide)] * 12 + [full(LANE, cells_x), pltpu.SMEM(ice_mask.shape, i32), dma((1,))],
        compiler_params=limit,
        name="sweep",
    )(ice_mask, vel0, visc, fric, drive, after(first, *[got[half + 1]]), second)
    for step in range(2, half - 1):
        got[step] = move(step, ready[step], strips)
    apart = [move(step, value, *more) for step, value, more in zip(early, outs[len(late) :], ([strips], [strips]))]
    near = [got[step] for step in halo_steps(groups)]
    base = pl.pallas_call(
        functools.partial(trim_kernel, groups, tile),
        out_shape=base_shapes,
        in_specs=[VMEM] * (len(near) + 7),
        out_specs=[VMEM] * 6,
        input_output_aliases={len(near) + 1 + number: number for number in range(6)},
        scratch_shapes=[full(STRIP + 16, wide)] * 14 + [full(PACK, wide)],
        compiler_params=limit,
        name="trim",
    )(*near, strips, *base)
    summed = (0, *early, *halo_steps(groups))
    slots = cells_x // tile * (cells_y // tile)
    partial = pl.pallas_call(
        functools.partial(part_kernel, slots, tile),
        out_shape=shape(2 * blocks, slots, PACK, LANE),
        in_specs=[VMEM] * len(summed),
        out_specs=VMEM,
        scratch_shapes=[full(len(summed) * CAP * slots, LANE)],
        compiler_params=limit,
        name="part",
    )(after(got[0], strips), *(got[step] for step in summed[1:]))
    return pl.pallas_call(
        functools.partial(final_kernel, groups, tile, early, summed),
        out_shape=shape(cells_x, cells_y),
        in_specs=[VMEM] * (groups + len(early) + 7),
        out_specs=HBM,
        scratch_shapes=[full(2, cells_x, cells_y)] + [full(rows, wide)] * 5
        + [
            full(groups * CAP * 4, LANE), full(8, LANE), full(PACK * groups, LANE), full(PACK * groups, LANE),
            full(LANE, long), full(cells_x, cells_y), dma((4,)),
        ],
        compiler_params=limit,
        name="final",
    )(partial, *got, *apart, *base)


def solution(mesh):
    placed = (
        P(None, "gx", "gy"),
        P("gx", "gy"),
        P("gx", "gy"),
        P(None, "gx", "gy"),
        P("gy", "gx", None, None, None),
        P("gy", "gx"),
        P("gy", "gx", None),
        P("gy", "gx"),
        P("gx", "gy"),
    )
    return jax.shard_map(body, mesh=mesh, in_specs=placed, out_specs=P("gx", "gy"), check_vma=False)
```

```python
import functools

import jax
import jax.numpy as jnp
from jax import lax
from jax.experimental import pallas as pl
from jax.experimental.pallas import tpu as pltpu
from jax.sharding import PartitionSpec as P

CAP = 2
OMEGA = 0.6
LANE = 128
PAD = 16
PACK = 16
FIELDS = ((0, 3), (3, 3), (6, 3), (9, 2), (11, 2), (13, 2), (15, 1))
U, V, VISC, FRIC, DRIVE_U, DRIVE_V, ICE = range(7)

VMEM = pl.BlockSpec(memory_space=pltpu.VMEM)
HBM = pl.BlockSpec(memory_space=pltpu.HBM)
F32 = jnp.float32


def partner(me, step):
    return me ^ step


def halo_steps(groups):
    return [step for step in range(1, groups) if step & (step + 1) == 0]


def after(value, *others):
    return lax.optimization_barrier((value, *others))[0]


def in_place(*values):
    return [pltpu.with_memory_space_constraint(value, pltpu.HBM) for value in values]


def swap(even, odd):
    count = lax.axis_size("gy")
    near = [(me, me ^ 1) for me in range(count)]
    far = [(me, me + 1 if me % 2 else me - 1) for me in range(1, count - 1)]
    return lax.ppermute(even, "gy", near), lax.ppermute(odd, "gy", far)


def both_sides(first, second):
    even = lax.rem(lax.axis_index("gy"), 2) == 0
    return jnp.where(even, first, second), jnp.where(even, second, first)


def copy_all(pairs, sems, first=0):
    copies = [
        pltpu.make_async_copy(source, target, sems.at[first + number])
        for number, (source, target) in enumerate(pairs)
    ]
    for copy in copies:
        copy.start()
    return copies


def wait_all(copies):
    for copy in copies:
        copy.wait()


def ice_line(values, shape, tile):
    lane = lax.broadcasted_iota(jnp.int32, shape, 1)
    line = jnp.zeros(shape, F32)
    for number, value in enumerate(values):
        line = jnp.where(lane // tile == number, value.astype(F32), line)
    return line


def fill_places(place, filled, groups, count, owner_of):
    for index in range((groups + 2) * CAP):
        place[index] = -1
    for index in range(groups):
        filled[index] = 0
    for scene in range(count):
        who = owner_of(scene)
        rank = filled[who]
        place[(who + 1) * CAP + rank] = scene
        filled[who] = rank + 1


def split(value):
    high = value.astype(jnp.bfloat16)
    rest = value - high.astype(F32)
    middle = rest.astype(jnp.bfloat16)
    return high, middle, (rest - middle.astype(F32)).astype(jnp.bfloat16)


def columns_of(pick, block):
    return lax.dot_general(pick, block, (((1,), (1,)), ((), ())), preferred_element_type=F32)


def load_scalars(owner, slot, weight, owner_s, slot_s, weight_b, weight_v, weight_s, sems):
    loads = copy_all([(owner, owner_s), (slot, slot_s), (weight, weight_b)], sems)
    loads[2].wait()
    weight_v[...] = weight_b[...].astype(F32)
    loads[2] = pltpu.make_async_copy(weight_v, weight_s, sems.at[2])
    loads[2].start()
    return loads


def easting_block(to, place, slot_s, weight_s, edge):
    row = lax.broadcasted_iota(jnp.int32, (PACK, LANE), 0)
    lane = lax.broadcasted_iota(jnp.int32, (PACK, LANE), 1)
    block = jnp.zeros((PACK, LANE), F32)
    for side in range(2):
        for rank in range(CAP):
            spot = place[(to + (2 if side == 0 else 0)) * CAP + rank]
            scene = jnp.maximum(spot, 0)
            amount = jnp.where(spot >= 0, weight_s[0, scene], 0.0)
            where = slot_s[0, scene]
            for part in range(2):
                line = edge(scene, part, side).astype(F32)
                line = line[0:1] if side == 0 else line[PACK - 1 : PACK]
                block = jnp.where(row == (side * CAP + rank) * 2 + part, line, block)
                value = jnp.where(where == side * 2 + part, amount, 0.0)
                block = jnp.where((row == 8) & (lane == 8 + (side * CAP + rank) * 2 + part), value, block)
    for rank in range(CAP):
        spot = place[(to + 1) * CAP + rank]
        scene = jnp.maximum(spot, 0)
        amount = jnp.where(spot >= 0, weight_s[0, scene], 0.0)
        for position in range(4):
            value = jnp.where(slot_s[0, scene] == position, amount, 0.0)
            block = jnp.where((row == 8) & (lane == rank * 4 + position), value, block)
    return block.astype(jnp.bfloat16)


def gather_scenes(obs, pays, steps, place, groups, blocks, me, sems):
    copies = []
    for number, step in enumerate(steps):
        to = partner(me, step)
        for rank in range(CAP):
            scene = jnp.maximum(place[(to + 1) * CAP + rank], 0)
            target = pays[number].at[pl.ds(rank * 2 * blocks, 2 * blocks)]
            copies += copy_all([(obs.at[scene], target)], sems, number * CAP + rank)
    return copies


def gather_kernel(groups, count, tile, *refs):
    owner, slot, weight, obs = refs[:4]
    pays = refs[4 : 4 + groups]
    owner_s, slot_s, weight_b, weight_v, weight_s, edges, place, filled, scalar_sem, edge_sem, scene_sem = refs[
        4 + groups :
    ]
    blocks = tile // PACK
    me = lax.axis_index("gx")
    loads = copy_all(
        [(obs.at[:, at], edges.at[number]) for number, at in enumerate((0, blocks, blocks - 1, 2 * blocks - 1))], edge_sem
    )
    scalars = load_scalars(owner, slot, weight, owner_s, slot_s, weight_b, weight_v, weight_s, scalar_sem)
    scalars[0].wait()
    fill_places(place, filled, groups, count, lambda scene: owner_s[0, scene])
    copies = gather_scenes(obs, pays, range(groups), place, groups, blocks, me, scene_sem)
    wait_all(scalars[1:] + loads)
    for step in range(groups):
        to = partner(me, step)
        pays[step][CAP * 2 * blocks] = easting_block(
            to, place, slot_s, weight_s, lambda scene, part, side: edges[side * 2 + part, scene]
        )
    wait_all(copies)


def northing_block(side, to, place, slot_s, weight_s, lines, tile):
    row = lax.broadcasted_iota(jnp.int32, (8, LANE), 0)
    lane = lax.broadcasted_iota(jnp.int32, (8, LANE), 1)
    block = jnp.zeros((8, LANE), F32)
    for rank in range(CAP):
        spot = place[(to + 1) * CAP + rank]
        scene = jnp.maximum(spot, 0)
        amount = jnp.where(spot >= 0, weight_s[0, scene], 0.0)
        where = slot_s[0, scene]
        line = lines[pl.ds(scene, 1), :]
        for part in range(2):
            block = jnp.where(row == rank * 2 + part, line[:, part * LANE : (part + 1) * LANE], block)
            value = jnp.where(where == part * 2 + side, amount, 0.0)
            block = jnp.where((row == 4) & (lane == rank * 2 + part), value, block)
        spot = place[(to + (0 if side == 0 else 2)) * CAP + rank]
        scene = jnp.maximum(spot, 0)
        amount = jnp.where(spot >= 0, weight_s[0, scene], 0.0)
        line = lines[pl.ds(scene, 1), :]
        at = tile - 1 if side == 0 else 0
        base = 8 + rank * 3
        for part in range(2):
            value = jnp.broadcast_to(line[:, part * LANE + at : part * LANE + at + 1], (1, LANE))
            block = jnp.where((row == 4) & (lane == base + part), value, block)
        value = jnp.where(slot_s[0, scene] == (2 if side == 0 else 1), amount, 0.0)
        block = jnp.where((row == 4) & (lane == base + 2), value, block)
    return block


def pack_kernel(groups, count, tile, *refs):
    owner, slot, weight, ice, obs_h, vel_h, visc_h, fric_h, drive_h, first, second, edge = refs[:12]
    (
        owner_s, slot_s, weight_b, weight_v, weight_s, ice_s, obs, vel, visc, fric, drive, to_low, to_high, lines,
        place, filled, scalar_sem, more_sem, load_sem,
    ) = refs[12:]
    loads = copy_all([(vel_h, vel), (drive_h, drive), (visc_h, visc), (fric_h, fric), (obs_h, obs)], load_sem)
    more = copy_all([(ice, ice_s)], more_sem)
    scalars = load_scalars(owner, slot, weight, owner_s, slot_s, weight_b, weight_v, weight_s, scalar_sem)
    picked = lax.broadcasted_iota(jnp.int32, (8, LANE), 0)
    across = lax.broadcasted_iota(jnp.int32, (8, LANE), 1)
    cells, cells_y = visc.shape
    scalars[0].wait()
    fill_places(place, filled, groups, count, lambda scene: owner_s[0, scene])

    def pick(depth):
        picked = lax.broadcasted_iota(jnp.int32, (8, cells_y), 0)
        across = lax.broadcasted_iota(jnp.int32, (8, cells_y), 1)
        wanted = jnp.where(picked < depth, picked, picked + cells_y - 2 * depth)
        return (across == wanted).astype(jnp.bfloat16)

    wait_all(loads[:4] + more)
    for index, (at, depth) in enumerate(FIELDS):
        if index == ICE:
            for target, column in ((to_low, 0), (to_high, ice_s.shape[1] - 1)):
                target[at : at + 1, :] = ice_line([ice_s[row, column] for row in range(ice_s.shape[0])], (1, cells), tile)
            for number, row in enumerate((0, ice_s.shape[0] - 1)):
                edge[number, at : at + 1, :] = ice_line(
                    [ice_s[row, column] for column in range(ice_s.shape[1])], (1, cells_y), tile
                )
            continue
        field = {VISC: visc, FRIC: fric}.get(index)
        if field is None:
            field = vel.at[index] if index in (U, V) else drive.at[index - DRIVE_U]
        parts = [field[...]] if index not in (VISC, FRIC) else split(field[...])
        rows = sum(columns_of(pick(depth), part) for part in parts)
        to_low[at : at + depth, :] = rows[0:depth]
        to_high[at : at + depth, :] = rows[depth : 2 * depth]
        edge[0, at : at + depth, :] = field[0:16, :].astype(F32)[0:depth]
        edge[1, at : at + depth, :] = field[cells - 16 : cells, :].astype(F32)[16 - depth : 16]
    loads[4].wait()
    both = (across == jnp.where(picked == 0, 0, LANE - 1)).astype(jnp.bfloat16)
    for scene in range(count):
        rows = columns_of(both, obs[scene].reshape(2 * tile, LANE))
        lines[0, scene : scene + 1, :] = rows[0:1]
        lines[1, scene : scene + 1, :] = rows[1:2]
    wait_all(scalars[1:])
    half = groups // 2
    for side, target in enumerate((to_low, to_high)):
        for to in range(groups):
            at = PACK + to % half * 8
            lanes = slice(to // half * LANE, (to // half + 1) * LANE)
            target[at : at + 8, lanes] = northing_block(side, to, place, slot_s, weight_s, lines.at[side], tile)
    even = lax.rem(lax.axis_index("gy"), 2) == 0
    first[...] = jnp.where(even, to_high[...], to_low[...])
    second[...] = jnp.where(even, to_low[...], to_high[...])


def side_tiles(right, left, turned):
    turned[...] = jnp.zeros_like(turned)
    turned[0:PACK, :] = right
    turned[PACK : 2 * PACK, :] = left
    return jnp.transpose(turned[...])


def side_tile(upright, index):
    at, depth = FIELDS[index]
    lane = lax.broadcasted_iota(jnp.int32, upright.shape, 1)
    after = pltpu.roll(upright, (LANE - at) % LANE, 1)
    before = pltpu.roll(upright, LANE - depth - PACK - at, 1)
    return jnp.where(lane < depth, after, jnp.where(lane >= LANE - depth, before, 0.0))


def write_halo(pay, base, pack):
    first = FIELDS[VISC][0]
    last = FIELDS[FRIC][0] + FIELDS[FRIC][1]
    for number in range(pack.shape[1] // LANE):
        whole = pack[:, number * LANE : (number + 1) * LANE]
        high = whole.astype(jnp.bfloat16)
        rest = whole - high.astype(F32)
        middle = rest.astype(jnp.bfloat16).astype(F32)
        pay[base + 2 * number] = high
        both = jnp.concatenate([middle[first:last], (rest - middle)[first:last]], axis=0)
        fill = jnp.zeros((PACK - both.shape[0], LANE), F32)
        pay[base + 2 * number + 1] = jnp.concatenate([both, fill], axis=0).astype(jnp.bfloat16)


def read_halo(pays, base, pack, me, beside):
    first = FIELDS[VISC][0]
    count = FIELDS[FRIC][0] + FIELDS[FRIC][1] - first
    for number in range(pack.shape[1] // LANE):
        lanes = slice(number * LANE, (number + 1) * LANE)
        high, more = jnp.zeros((PACK, LANE), F32), jnp.zeros((PACK, LANE), F32)
        for step, pay in pays.items():
            here = partner(me, step) == beside
            high = jnp.where(here, pay[base + 2 * number].astype(F32), high)
            more = jnp.where(here, pay[base + 2 * number + 1].astype(F32), more)
        pack[:, lanes] = high
        pack[first : first + count, lanes] += more[0:count]
        pack[first : first + count, lanes] += more[count : 2 * count]


def widen_kernel(groups, tile, early, late, *refs):
    first, second, edge = refs[:3]
    pays = dict(zip(late, refs[3 + len(late) :]))
    refs = refs[3 + 2 * len(late) :]
    apart = dict(zip(early, refs))
    turned, to_low, to_high = refs[len(early) :]
    cells_y = edge.shape[2]
    blocks = tile // PACK
    me = lax.axis_index("gx")
    half = groups // 2
    for step in late + early:
        to = partner(me, step)
        here = pl.ds(pl.multiple_of(PACK + lax.rem(to, half) * 8, 8), 8)
        sides = both_sides(first[here, :], second[here, :])
        block = jnp.concatenate([jnp.where(to < half, side[:, 0:LANE], side[:, LANE:]) for side in sides], axis=0)
        if step in early:
            apart[step][0] = block.astype(jnp.bfloat16)
        else:
            pays[step][CAP * 2 * blocks + 1] = block.astype(jnp.bfloat16)
    upright = side_tiles(*both_sides(first[0:PACK, :], second[0:PACK, :]), turned)
    cells = upright.shape[0]
    to_low[:, 0:cells_y] = edge[0]
    to_high[:, 0:cells_y] = edge[1]
    for index, (at, depth) in enumerate(FIELDS):
        to_low[at : at + depth, cells_y:] = side_tile(upright[0:8], index)[0:depth]
        to_high[at : at + depth, cells_y:] = side_tile(upright[cells - 8 :], index)[8 - depth : 8]
    base = CAP * 2 * blocks + 2
    for step in halo_steps(groups):
        write_halo(pays[step], base, jnp.where(partner(me, step) > me, to_high[...], to_low[...]))


def stress_block(u, v, visc, low, rows, wide):
    here, after = pl.ds(low, rows), pl.ds(low + 1, rows)
    vel_u, vel_v = u[here, :], v[here, :]
    a_x = u[after, :] - vel_u
    b_x = v[after, :] - vel_v
    a_y = pltpu.roll(vel_u, wide - 1, 1) - vel_u
    b_y = pltpu.roll(vel_v, wide - 1, 1) - vel_v
    nu = visc[here, :]
    return nu * (4.0 * a_x + 2.0 * b_y), nu * (4.0 * b_y + 2.0 * a_x), nu * (a_y + b_x)


def image_block(sxx, syy, sxy, low, rows):
    here, before = pl.ds(low, rows), pl.ds(low - 1, rows)
    mid = sxy[here, :]
    push_u = sxx[before, :] - sxx[here, :] + pltpu.roll(mid, 1, 1) - mid
    side = syy[here, :]
    push_v = sxy[before, :] - mid + pltpu.roll(side, 1, 1) - side
    return push_u, push_v


def relaxation(fields, work, wide, cells_y, spans, outs, shift, own_of, size=8):
    u, v, visc, fric, drive_u, drive_v, ice = fields
    next_u, next_v, relax_u, relax_v, sxx, syy, sxy = work
    second, ease, lead, trail = outs
    for low in spans[0]:
        here = pl.ds(low, size)
        nu, drag = visc[here, :], fric[here, :]
        nu_x = visc[pl.ds(low - 1, size), :]
        nu_y = pltpu.roll(nu, 1, 1)
        inside = drag > 0.0
        for out, diag in ((relax_u, 5.0 * nu + 4.0 * nu_x + nu_y), (relax_v, 5.0 * nu + nu_x + 4.0 * nu_y)):
            out[here, :] = jnp.where(inside, 1.0 / jnp.where(inside, diag + drag, 1.0), 0.0)
    for low in spans[1]:
        here = pl.ds(low, size)
        sxx[here, :], syy[here, :], sxy[here, :] = stress_block(u, v, visc, low, size, wide)
    for low in spans[2]:
        here, there = pl.ds(low, size), pl.ds(low + shift, size)
        pushes = image_block(sxx, syy, sxy, low, size)
        for part, (push, speed, force, relax, then) in enumerate(
            zip(pushes, (u, v), (drive_u, drive_v), (relax_u, relax_v), (next_u, next_v))
        ):
            now, soft = speed[here, :], relax[here, :]
            move = soft * (force[here, :] - push - fric[here, :] * now)
            then[here, :] = now + OMEGA * move
            if low in spans[4]:
                slack = OMEGA * soft
                ease[part, there, :] = slack
                if own_of(low) is not None:
                    factor = -ice[here, 0:cells_y] * (slack * (move + now))[:, 0:cells_y]
                    lead[part, pl.ds(own_of(low), size), :] = factor
    for low in spans[3]:
        here = pl.ds(low, size)
        sxx[here, :], syy[here, :], sxy[here, :] = stress_block(next_u, next_v, visc, low, size, wide)
    for low in spans[4]:
        here, there = pl.ds(low, size), pl.ds(low + shift, size)
        pushes = image_block(sxx, syy, sxy, low, size)
        for part, (push, speed, force, relax) in enumerate(
            zip(pushes, (next_u, next_v), (drive_u, drive_v), (relax_u, relax_v))
        ):
            now = speed[here, :]
            move = relax[here, :] * (force[here, :] - push - fric[here, :] * now)
            second[part, there, :] = ice[here, :] * (now + OMEGA * move)
            if own_of(low) is not None:
                mine = pl.ds(own_of(low), size)
                trail[part, mine, :] = (
                    -ice[here, 0:cells_y] * (move + now)[:, 0:cells_y] - fric[here, 0:cells_y] * lead[part, mine, :]
                )


STRIP = 32


def sweep_kernel(tile, ice, vel, visc, fric, drive, first, then, *refs):
    second, ease, lead, trail, wide_visc, wide_ice, strips = refs[:7]
    u, v, wide_fric, drive_u, drive_v = refs[7:12]
    work = refs[12:19]
    turned, ice_s, sems = refs[19:]
    cells, cells_y = visc.shape
    rows, wide = wide_visc.shape
    loads = copy_all([(ice, ice_s)], sems)
    upright = side_tiles(*both_sides(first[0:PACK, :], then[0:PACK, :]), turned)
    wait_all(loads)
    own_rows = slice(PAD, PAD + cells)
    fields = (u, v, wide_visc, wide_fric, drive_u, drive_v, wide_ice)
    for index, field in enumerate(fields):
        field[0:PAD, :] = jnp.zeros((PAD, wide), F32)
        field[PAD + cells :, :] = jnp.zeros((PAD, wide), F32)
        if index == ICE:
            for number in range(cells // tile):
                field[PAD + number * tile : PAD + (number + 1) * tile, 0:cells_y] = ice_line(
                    [ice_s[number, column] for column in range(ice_s.shape[1])], (tile, cells_y), tile
                )
        elif index in (VISC, FRIC):
            field[own_rows, 0:cells_y] = (visc if index == VISC else fric)[...]
        else:
            source = vel if index in (U, V) else drive
            field[own_rows, 0:cells_y] = source[index % DRIVE_U].astype(F32)
        field[own_rows, cells_y:wide] = side_tile(upright, index)
        strips[index, 0] = field[8 : 8 + STRIP, :]
        strips[index, 1] = field[rows - 8 - STRIP : rows - 8, :]
    last = PAD + cells
    spans = [range(PAD, last, 32)] * 5
    relaxation(fields, work, wide, cells_y, spans, (second, ease, lead, trail), 0, lambda low: low - PAD, 32)


def trim_kernel(groups, tile, *refs):
    steps = halo_steps(groups)
    pays = dict(zip(steps, refs))
    strips = refs[len(steps)]
    second, ease, lead, trail, visc, ice = refs[len(steps) + 7 : len(steps) + 13]
    refs = refs[len(steps) + 13 :]
    fields, work, pack = refs[:7], refs[7:14], refs[14]
    rows, wide = visc.shape
    cells_y = wide - LANE
    cells = rows - 2 * PAD
    base = CAP * 2 * (tile // PACK) + 2
    me = lax.axis_index("gx")
    spans = (
        [(8, 16, 24), (8, 16, 24), (8, 16, 24), (8, 16), (8, 16)],
        [(16, 24, 32), (8, 16, 24, 32), (16, 24, 32), (16, 24, 32), (24, 32)],
    )
    for strip in range(2):
        read_halo(pays, base, pack, me, me - 1 if strip == 0 else me + 1)
        shift = 0 if strip == 0 else rows - 16 - STRIP
        edge = PAD if strip == 0 else PAD + cells - shift
        for index, field in enumerate(fields):
            at, depth = FIELDS[index]
            field[8 : 8 + STRIP, :] = strips[index, strip]
            target = slice(edge - depth, edge) if strip == 0 else slice(edge, edge + depth)
            field[target, :] = pack[at : at + depth, :]
            if index in (VISC, ICE):
                (visc if index == VISC else ice)[target.start + shift : target.stop + shift, :] = pack[at : at + depth, :]
        own = {0: (16, 0), 1: (24, cells - 8)}[strip]
        relaxation(
            fields, work, wide, cells_y, spans[strip], (second, ease, lead, trail), shift,
            lambda low, own=own: own[1] if low == own[0] else None,
        )


def part_kernel(slots, tile, *refs):
    pays, (sums, table) = refs[:-2], refs[-2:]
    blocks = tile // PACK
    for number, pay in enumerate(pays):
        meta = pay[CAP * 2 * blocks].astype(F32)[8:9]
        for index in range(CAP * slots):
            at = number * CAP * slots + index
            table[at : at + 1, :] = jnp.broadcast_to(meta[:, index : index + 1], (1, LANE))

    def step(index, carry):
        total = [jnp.zeros((PACK, LANE), F32) for _ in range(slots)]
        for number, pay in enumerate(pays):
            for rank in range(CAP):
                got = pay[rank * 2 * blocks + index].astype(F32)
                for position in range(slots):
                    at = (number * CAP + rank) * slots + position
                    total[position] += table[at : at + 1, :] * got
        for position in range(slots):
            sums[index, position] = total[position]
        return carry

    lax.fori_loop(0, 2 * blocks, step, 0)


def final_kernel(groups, tile, early, summed, *refs):
    sums_before, refs = refs[0], refs[1:]
    pays = refs[:groups]
    apart = dict(zip(early, refs[groups:]))
    refs = refs[len(early) :]
    second, ease, lead, trail, visc, ice, grad = refs[groups : groups + 7]
    misfit, u, v, sxx, syy, sxy, table, total, rows_x, rows_y, turned, result, result_sem = refs[groups + 7 :]
    rows, wide = visc.shape
    cells_y = wide - LANE
    cells = rows - 2 * PAD
    blocks = tile // PACK
    tiles_y = cells_y // tile
    slots = cells // tile * tiles_y
    lift = (u, v)
    for group in range(groups):
        rows_x[pl.ds(group, PACK, stride=groups), :] = pays[group][CAP * 2 * blocks].astype(F32)
        side = apart[group][0] if group in early else pays[group][CAP * 2 * blocks + 1]
        rows_y[pl.ds(group, PACK, stride=groups), :] = side.astype(F32)

    def raw(source, number):
        return source[number * groups : (number + 1) * groups, :]

    def spread(source, number, row=8):
        return jnp.broadcast_to(raw(source, row)[:, number : number + 1], (groups, LANE))

    def gathered(value):
        return jnp.sum(value, axis=0, keepdims=True)

    for position in range(slots):
        weights = [spread(rows_x, rank * slots + position) for rank in range(CAP)]
        for rank in range(CAP):
            at = (rank * slots + position) * groups
            table[at : at + groups, :] = weights[rank]
        total[position : position + 1, :] = gathered(sum(weights))
    for field in lift:
        field[0:PAD, :] = jnp.zeros((PAD, wide), F32)
        field[PAD + cells :, :] = jnp.zeros((PAD, wide), F32)
    turned[...] = jnp.zeros_like(turned)
    for side in range(2):
        at = PAD + cells if side == 0 else PAD - 1
        for column in range(2):
            lanes = slice(column * tile, (column + 1) * tile)
            weights = [spread(rows_x, 8 + (side * CAP + rank) * 2 + column) for rank in range(CAP)]
            weight = gathered(sum(weights))
            for part in range(2):
                seen = gathered(sum(weights[rank] * raw(rows_x, (side * CAP + rank) * 2 + part) for rank in range(CAP)))
                gap = weight * second[part, at : at + 1, lanes] - ice[at : at + 1, lanes] * seen
                lift[part][at : at + 1, lanes] = ease[part, at : at + 1, lanes] * gap
        lines = [[None] * 2 for _ in range(3)]
        for column in range(2):
            weights = [spread(rows_y, rank * 2 + column, side * 8 + 4) for rank in range(CAP)]
            lines[2][column] = gathered(sum(weights))
            for part in range(2):
                lines[part][column] = gathered(
                    sum(weights[rank] * raw(rows_y, side * 8 + rank * 2 + part) for rank in range(CAP))
                )
        weights = [spread(rows_y, 8 + rank * 3 + 2, side * 8 + 4) for rank in range(CAP)]
        corners = [
            gathered(sum(weights[rank] * spread(rows_y, 8 + rank * 3 + part, side * 8 + 4) for rank in range(CAP)))
            for part in range(2)
        ] + [gathered(sum(weights))]
        lane = lax.broadcasted_iota(jnp.int32, (1, turned.shape[1]), 1)
        for number in range(3):
            line = jnp.concatenate(
                lines[number] + [jnp.zeros((1, turned.shape[1] - 2 * tile), F32)], axis=1
            )
            line = pltpu.roll(jnp.broadcast_to(line, (8, turned.shape[1])), PAD, 1)[0:1]
            corner = jnp.concatenate([corners[number]] * (turned.shape[1] // LANE), axis=1)
            line = jnp.where(lane == (PAD - 1 if side == 0 else PAD + cells), corner, line)
            at = number if side == 0 else LANE - 1 - number
            turned[at : at + 1, :] = line
    upright = jnp.transpose(turned[...])[0:rows]
    lane = lax.broadcasted_iota(jnp.int32, (rows, LANE), 1)

    def sides(number):
        after = pltpu.roll(upright, (LANE - number) % LANE, 1)
        before = pltpu.roll(upright, number, 1)
        return jnp.where(lane == 0, after, jnp.where(lane == LANE - 1, before, 0.0))

    weight = sides(2)
    for part in range(2):
        gap = weight * second[part, :, cells_y:wide] - ice[:, cells_y:wide] * sides(part)
        lift[part][:, cells_y:wide] = ease[part, :, cells_y:wide] * gap

    def step(index, carry):
        part, chunk = index // blocks, index % blocks
        sums = [sums_before[index, position] for position in range(slots)]
        for group in range(groups):
            if group in summed:
                continue
            for rank in range(CAP):
                got = pays[group][rank * 2 * blocks + index].astype(F32)
                for position in range(slots):
                    sums[position] += table[pl.ds((rank * slots + position) * groups + group, 1), :] * got
        for position in range(slots):
            lanes = slice((position % tiles_y) * tile, (position % tiles_y + 1) * tile)
            at = pl.multiple_of((position // tiles_y) * tile + chunk * PACK, PACK)
            here = pl.ds(pl.multiple_of(at + PAD, PACK), PACK)
            gap = total[position : position + 1, :] * second[part, here, lanes] - ice[here, lanes] * sums[position]
            misfit[part, pl.ds(at, PACK), lanes] = gap
            sums[position] = ease[part, here, lanes] * gap

        for number, field in enumerate(lift):

            @pl.when(part == number)
            def _():
                for position in range(slots):
                    lanes = slice((position % tiles_y) * tile, (position % tiles_y + 1) * tile)
                    at = pl.multiple_of((position // tiles_y) * tile + chunk * PACK + PAD, PACK)
                    field[pl.ds(at, PACK), lanes] = sums[position]

        return carry

    lax.fori_loop(0, 2 * blocks, step, 0)
    for low in (8, *range(PAD, rows - PAD, 32)):
        size = 32 if low >= PAD else 8
        here = pl.ds(low, size)
        sxx[here, :], syy[here, :], sxy[here, :] = stress_block(u, v, visc, low, size, wide)
    copies, quarter = [], cells // 4
    for low in range(PAD, rows - PAD, 32):
        mine = pl.ds(low - PAD, 32)
        here = pl.ds(low, 32)
        sums = jnp.zeros((32, cells_y), F32)
        for part, push in enumerate(image_block(sxx, syy, sxy, low, 32)):
            sums += (misfit[part, mine, :] - push[:, 0:cells_y]) * lead[part, mine, :]
            sums += lift[part][here, 0:cells_y] * trail[part, mine, :]
        result[mine, :] = sums
        done = low - PAD + 32
        if done % quarter == 0:
            part_rows = pl.ds(done - quarter, quarter)
            copies += copy_all([(result.at[part_rows], grad.at[part_rows])], result_sem, done // quarter - 1)
    wait_all(copies)


def body(vel0, visc, fric, drive, scene_obs, scene_weight, scene_owner, scene_slot, ice_mask):
    cells_x, cells_y = visc.shape
    tile = scene_obs.shape[-1]
    count = scene_obs.shape[1]
    groups = lax.axis_size("gx")
    blocks = tile // PACK
    rows, wide = cells_x + 2 * PAD, cells_y + LANE
    long = -(-rows // LANE) * LANE
    obs = scene_obs.reshape(count, 2 * blocks, PACK, LANE)
    owner, slot, weight = scene_owner.reshape(1, count), scene_slot, scene_weight
    limit = pltpu.CompilerParams(vmem_limit_bytes=40 << 20)
    dma = pltpu.SemaphoreType.DMA
    def shape(*dims, dtype=F32):
        return jax.ShapeDtypeStruct(dims, dtype)

    def short(*dims):
        return pltpu.VMEM(dims, jnp.bfloat16)

    def full(*dims):
        return pltpu.VMEM(dims, F32)

    bf16, i32 = jnp.bfloat16, jnp.int32
    deep = CAP * 2 * blocks
    tall = PACK + groups // 2 * 8
    half = groups // 2
    early = (half + 1, half)
    late = tuple(step for step in range(groups) if step not in early)
    halo = 2 * (wide // LANE)

    def pay(step):
        more = 0 if step in early else 1 + (halo if step in halo_steps(groups) else 0)
        return pltpu.VMEM((deep + 1 + more, PACK, LANE), bf16)

    def move(step, value, *others):
        pairs = [(me, partner(me, step)) for me in range(groups)]
        return lax.ppermute(after(value, *others) if others else value, "gx", pairs)

    scalars = [
        pltpu.SMEM((1, count), i32), pltpu.SMEM((1, count), i32), short(1, count), full(1, count),
        pltpu.SMEM((1, count), F32),
    ]
    places = [pltpu.SMEM(((groups + 2) * CAP,), i32), pltpu.SMEM((groups,), i32)]
    pays = pl.pallas_call(
        functools.partial(gather_kernel, groups, count, tile),
        out_shape=[pay(step) for step in range(groups)],
        in_specs=[HBM] * 4,
        out_specs=[VMEM] * groups,
        scratch_shapes=[
            *scalars, short(4, count, PACK, LANE), *places, dma((3,)), dma((4,)),
            dma((groups * CAP,)),
        ],
        compiler_params=limit,
        name="gather",
    )(*in_place(owner, slot, weight, obs))
    got = [pays[0]] * groups
    for step in early:
        got[step] = move(step, pays[step])
    *north, edge = pl.pallas_call(
        functools.partial(pack_kernel, groups, count, tile),
        out_shape=[pltpu.VMEM((tall, cells_x), F32)] * 2 + [pltpu.VMEM((2, PACK, cells_y), F32)],
        in_specs=[HBM] * 9,
        out_specs=[VMEM] * 3,
        scratch_shapes=scalars + [
            pltpu.SMEM(ice_mask.shape, i32), short(*obs.shape), short(*vel0.shape), full(*visc.shape),
            full(*fric.shape), short(*drive.shape), full(tall, cells_x), full(tall, cells_x), full(2, count, cells_x),
            *places, dma((3,)), dma((1,)), dma((5,)),
        ],
        compiler_params=limit,
        name="pack",
    )(*in_place(after(owner, pays[half]), slot, weight, ice_mask, obs, vel0, visc, fric, drive))
    first, second = swap(*north)
    outs = pl.pallas_call(
        functools.partial(widen_kernel, groups, tile, early, late),
        out_shape=[pay(step) for step in late] + [pltpu.VMEM((1, PACK, LANE), bf16)] * len(early),
        in_specs=[VMEM] * (3 + len(late)),
        out_specs=[VMEM] * groups,
        input_output_aliases={3 + number: number for number in range(len(late))},
        scratch_shapes=[full(LANE, cells_x), full(PACK, wide), full(PACK, wide)],
        compiler_params=limit,
        name="widen",
    )(first, second, edge, *(pays[step] for step in late))
    ready = dict(zip(late, outs))
    got[0] = ready[0]
    ties = {half + 2: [got[half + 1]], 1: [], half - 1: [], groups - 1: []}
    for step in (groups - 1, 1, *range(half + 2, groups - 1), half - 1):
        got[step] = move(step, ready[step], *ties.get(step, []))
    strip = shape(len(FIELDS), 2, STRIP, wide)
    base_shapes = [shape(2, rows, wide)] * 2 + [shape(2, cells_x, cells_y)] * 2 + [shape(rows, wide)] * 2
    *base, strips = pl.pallas_call(
        functools.partial(sweep_kernel, tile),
        out_shape=base_shapes + [strip],
        in_specs=[HBM] + [VMEM] * 6,
        out_specs=[VMEM] * 7,
        scratch_shapes=[full(rows, wide)] * 12 + [full(LANE, cells_x), pltpu.SMEM(ice_mask.shape, i32), dma((1,))],
        compiler_params=limit,
        name="sweep",
    )(ice_mask, vel0, visc, fric, drive, after(first, *[got[half + 1]]), second)
    for step in range(2, half - 1):
        got[step] = move(step, ready[step], strips)
    apart = [move(step, value, *more) for step, value, more in zip(early, outs[len(late) :], ([strips], [strips]))]
    near = [got[step] for step in halo_steps(groups)]
    base = pl.pallas_call(
        functools.partial(trim_kernel, groups, tile),
        out_shape=base_shapes,
        in_specs=[VMEM] * (len(near) + 7),
        out_specs=[VMEM] * 6,
        input_output_aliases={len(near) + 1 + number: number for number in range(6)},
        scratch_shapes=[full(STRIP + 16, wide)] * 14 + [full(PACK, wide)],
        compiler_params=limit,
        name="trim",
    )(*near, strips, *base)
    summed = (0, *early, *halo_steps(groups), 2)
    slots = cells_x // tile * (cells_y // tile)
    partial = pl.pallas_call(
        functools.partial(part_kernel, slots, tile),
        out_shape=shape(2 * blocks, slots, PACK, LANE),
        in_specs=[VMEM] * len(summed),
        out_specs=VMEM,
        scratch_shapes=[full(len(summed) * CAP * slots, LANE)],
        compiler_params=limit,
        name="part",
    )(after(got[0], strips), *(got[step] for step in summed[1:]))
    return pl.pallas_call(
        functools.partial(final_kernel, groups, tile, early, summed),
        out_shape=shape(cells_x, cells_y),
        in_specs=[VMEM] * (groups + len(early) + 7),
        out_specs=HBM,
        scratch_shapes=[full(2, cells_x, cells_y)] + [full(rows, wide)] * 5
        + [
            full(groups * CAP * 4, LANE), full(8, LANE), full(PACK * groups, LANE), full(PACK * groups, LANE),
            full(LANE, long), full(cells_x, cells_y), dma((4,)),
        ],
        compiler_params=limit,
        name="final",
    )(partial, *got, *apart, *base)


def solution(mesh):
    placed = (
        P(None, "gx", "gy"),
        P("gx", "gy"),
        P("gx", "gy"),
        P(None, "gx", "gy"),
        P("gy", "gx", None, None, None),
        P("gy", "gx"),
        P("gy", "gx", None),
        P("gy", "gx"),
        P("gx", "gy"),
    )
    return jax.shard_map(body, mesh=mesh, in_specs=placed, out_specs=P("gx", "gy"), check_vma=False)
```
